32 devices in a mesh: dp: 16 (over z, y, core), blk: 2 (over x).
Axes of the slice: x: 2, y: 2, z: 4, core: 2. Of those that a mesh axis runs over, the one named last changes fastest.
Arguments:
- tokens: bfloat16 [256, 64, 768], P('blk', 'dp'), may hold values from -6 to 6
- timesteps: int32 [64], P('dp'), may hold values from 0 to 1999
- boundary: int32 [64], P('dp'), may hold values from 64 to 192
- importance: float32 [64], P('dp'), may hold values from 0.5 to 2
- cotangent: bfloat16 [256, 64, 768], P('blk', 'dp'), may hold values from -6 to 6
- time_weight: bfloat16 [128, 768], replicated, may hold values from -0.5 to 0.5
- time_bias: bfloat16 [768], replicated, may hold values from -3 to 3
- mixing_weight: bfloat16 [768, 2304], replicated, may hold values from -0.21875 to 0.21875
- query_bias: bfloat16 [768], replicated, may hold values from -2 to 2
- value_bias: bfloat16 [768], replicated, may hold values from -2 to 2
- output_weight: bfloat16 [768, 768], replicated, may hold values from -1.25 to 1.25
- output_bias: bfloat16 [768], replicated, may hold values from -2 to 2
- first_gain: bfloat16 [768], replicated, may hold values from 0.5 to 1.5
- first_shift: bfloat16 [768], replicated, may hold values from -2 to 2
- widen_weight: bfloat16 [768, 3072], replicated, may hold values from -0.21875 to 0.21875
- widen_bias: bfloat16 [3072], replicated, may hold values from -2 to 2
- narrow_weight: bfloat16 [3072, 768], replicated, may hold values from -0.15625 to 0.15625
- narrow_bias: bfloat16 [768], replicated, may hold values from -2 to 2
- second_gain: bfloat16 [768], replicated, may hold values from 0.5 to 1.5
- second_shift: bfloat16 [768], replicated, may hold values from -2 to 2
Outputs:
- output: bfloat16 [256, 64, 768], P('blk', 'dp')
- input_grad: bfloat16 [256, 64, 768], P('blk', 'dp')
- time_weight_grad: float32 [128, 768], replicated
- time_bias_grad: float32 [768], replicated
- mixing_weight_grad: float32 [768, 2304], replicated
- query_bias_grad: float32 [768], replicated
- value_bias_grad: float32 [768], replicated
- output_weight_grad: float32 [768, 768], replicated
- output_bias_grad: float32 [768], replicated
- first_gain_grad: float32 [768], replicated
- first_shift_grad: float32 [768], replicated
- expand_weight_grad: float32 [768, 3072], replicated
- expand_bias_grad: float32 [3072], replicated
- shrink_weight_grad: float32 [3072, 768], replicated
- shrink_bias_grad: float32 [768], replicated
- second_gain_grad: float32 [768], replicated
- second_shift_grad: float32 [768], replicated
The draws below stay inside these ranges and needn't reach their ends.
All inputs are finite; a program needn't handle non-finite values.
Results may differ from the reference program's by a relative error of at most 0.023.
Values may be sent and summed in bfloat16 or wider, within the bound.
No kernel may reach another device: no remote copies, remote signals or barrier semaphores. Data moves between devices by JAX's collectives and lax.ppermute only.
A program may use at most 256 MiB of HBM per device.

```python
import math
import jax
import jax.numpy as jnp
from jax import lax

D = 768
HEADS = 12
HEAD = 64
FF = 3072
TDIM = 128
SEQ_DEV = 4
SEQ_LEN = 256
NSEQ = 64


def with_ends(drawn, stream_key, smallest, high):
    shape = drawn.shape
    place = [jax.random.randint(jax.random.fold_in(stream_key, axis), (), 0, shape[axis]) for axis in range(len(shape))]
    drawn = drawn.at[tuple(place)].set(smallest)
    longest = shape.index(max(shape))
    place[longest] = (place[longest] + 1) % shape[longest]
    return drawn.at[tuple(place)].set(high)


def block_levels(rng, shape, split, smallest, high):
    loudness = 1.0
    for dim, shards_of in split:
        steps = jax.random.uniform(jax.random.fold_in(jax.random.fold_in(rng, 6), dim), (shards_of,), jnp.float32, smallest / len(split), high / len(split))
        loudness = loudness * jnp.repeat(jnp.exp(steps), shape[dim] // shards_of).reshape((-1,) + (1,) * (len(shape) - 1 - dim))
    return loudness


def noise(key, extent, scale, reach, cuts=(), kind=jnp.bfloat16):
    result = jax.random.normal(key, extent, jnp.float32) * scale
    if len(cuts) > 0:
        result = block_levels(key, extent, cuts, -0.22, 0.18) * result
    return jnp.clip(result, min=-reach, max=reach).astype(kind)


def setup_inputs(seed: int = 0) -> dict:
    splits = jax.random.split(jax.random.key(seed), 21)
    return {
        "tokens": noise(splits[0], (SEQ_LEN, NSEQ, D), 1.0, 6.0, ((0, 2), (1, 16))),
        "timesteps": with_ends(jax.random.randint(splits[1], (NSEQ,), 0, 2000), jax.random.fold_in(splits[1], 1), 0, 1999).astype(jnp.int32),
        "boundary": with_ends(jax.random.randint(splits[2], (NSEQ,), SEQ_LEN // 4, 3 * SEQ_LEN // 4 + 1), jax.random.fold_in(splits[2], 1), SEQ_LEN // 4, (3 * SEQ_LEN // 4 + 1) - 1).astype(jnp.int32),
        "importance": jnp.clip(jnp.exp(math.log(2.0) - 1.3862944 * jax.random.uniform(splits[3], (NSEQ,), jnp.float32) ** block_levels(splits[3], (NSEQ,), ((0, 16),), -0.2, 0.2)), 0.5, 2.0),
        "cotangent": noise(splits[4], (SEQ_LEN, NSEQ, D), 1.0, 6.0, ((0, 2), (1, 16))),
        "time_weight": noise(splits[5], (TDIM, D), TDIM ** -0.5, 0.5),
        "time_bias": noise(splits[6], (D,), 0.5, 3.0),
        "mixing_weight": noise(splits[7], (D, 3 * D), D ** -0.5, 0.21875),
        "query_bias": noise(splits[8], (D,), 0.3, 2.0),
        "value_bias": noise(splits[9], (D,), 0.3, 2.0),
        "output_weight": noise(splits[10], (D, D), (D // 32) ** -0.5, 1.25),
        "output_bias": noise(splits[11], (D,), 0.3, 2.0),
        "first_gain": jnp.clip(1.0 + 0.1 * jax.random.normal(splits[12], (D,), jnp.float32), 0.5, 1.5).astype(jnp.bfloat16),
        "first_shift": noise(splits[13], (D,), 0.3, 2.0),
        "widen_weight": noise(splits[14], (D, FF), D ** -0.5, 0.21875),
        "widen_bias": noise(splits[15], (FF,), 0.3, 2.0),
        "narrow_weight": noise(splits[16], (FF, D), (FF // 2) ** -0.5, 0.15625),
        "narrow_bias": noise(splits[17], (D,), 0.3, 2.0),
        "second_gain": jnp.clip(1.0 + 0.1 * jax.random.normal(splits[18], (D,), jnp.float32), 0.5, 1.5).astype(jnp.bfloat16),
        "second_shift": noise(splits[19], (D,), 0.3, 2.0),
    }


epsilon = 1e-05

@jax.custom_vjp
def reduced_copy(v):
    return lax.optimization_barrier(v.astype(jnp.bfloat16)).astype(jnp.float32)

@jax.custom_vjp
def reduced_backward(v):
    return v

def low_keep(v):
    return (reduced_copy(v), None)

def low_pass(kept, grad):
    return (grad,)

def back_keep(v):
    return (v, None)

def back_low(kept, grad):
    return (reduced_copy(grad),)
reduced_copy.defvjp(low_keep, low_pass)
reduced_backward.defvjp(back_keep, back_low)

def sinusoid(step_ids, code_width):
    half_width = code_width // 2
    frequency = jnp.exp(-math.log(10000.0) * jnp.arange(half_width, dtype=jnp.float32) / half_width)
    angles = step_ids.astype(jnp.float32)[:, None] * frequency[None, :]
    return jnp.concatenate([jnp.cos(angles), jnp.sin(angles)], axis=-1)

def layer_norm(inputs, norm_gain, norm_shift):
    centred = inputs - lax.optimization_barrier(jnp.mean(inputs, axis=-1, keepdims=True))
    variance = lax.optimization_barrier(jnp.mean(centred * centred, axis=-1, keepdims=True))
    return centred * lax.rsqrt(variance + epsilon) * norm_gain + norm_shift

def matrix_product(left, right, form):
    return jnp.einsum(form, left, right, precision=lax.Precision.HIGHEST)

def layer_loss(params, inputs, upstream, step_ids, bounds, weights):
    time_weight, time_bias, mixing_weight, query_bias, value_bias, output_weight, output_bias, first_gain, first_shift, widen_weight, widen_bias, narrow_weight, narrow_bias, second_gain, second_shift = params
    row_count = inputs.shape[0]
    group_count = inputs.shape[1]
    model_width = inputs.shape[2]
    time_code = reduced_copy(sinusoid(step_ids, time_weight.shape[0]))
    time_embed = matrix_product(time_code, time_weight, 'sc,cd->sd') + time_bias
    hidden = inputs + time_embed[None]
    hidden_low = reduced_copy(hidden)
    bias_pack = jnp.concatenate([query_bias, jnp.zeros_like(query_bias), value_bias])
    packed = reduced_copy(reduced_backward(matrix_product(hidden_low, mixing_weight, 'lsd,de->lse')) + bias_pack)
    queries = packed[..., :model_width].reshape(row_count, group_count, HEADS, HEAD)
    keys_all = packed[..., model_width:2 * model_width].reshape(row_count, group_count, HEADS, HEAD)
    values_all = packed[..., 2 * model_width:].reshape(row_count, group_count, HEADS, HEAD)
    scores = reduced_backward(matrix_product(queries, keys_all, 'qshe,kshe->shqk') * (1.0 / math.sqrt(HEAD)))
    probs_low = reduced_copy(jax.nn.softmax(scores, axis=-1))
    context = reduced_backward(reduced_copy(matrix_product(probs_low, values_all, 'shqk,kshe->qshe').reshape(row_count, group_count, model_width)))
    first_sum = hidden + reduced_backward(matrix_product(context, output_weight, 'lsd,de->lse')) + output_bias
    leading_norm = layer_norm(first_sum, first_gain, first_shift)
    before_activation = reduced_backward(matrix_product(reduced_copy(leading_norm), widen_weight, 'ikg,gv->ikv')) + widen_bias
    activation_reduced = reduced_copy(jax.nn.gelu(before_activation, approximate=False))
    residual_sum = leading_norm + reduced_backward(matrix_product(activation_reduced, narrow_weight, 'ema,aw->emw')) + narrow_bias
    out_full = layer_norm(residual_sum, second_gain, second_shift)
    positions = jnp.arange(row_count, dtype=jnp.int32)
    row_weight = jnp.where(positions[:, None] >= bounds[None, :], weights[None, :], 0.0)
    total_loss = jnp.sum(out_full * upstream * row_weight[:, :, None])
    return (total_loss, out_full)

def reference(tokens, timesteps, boundary, importance, cotangent, time_weight, time_bias, mixing_weight, query_bias, value_bias, output_weight, output_bias, first_gain, first_shift, widen_weight, widen_bias, narrow_weight, narrow_bias, second_gain, second_shift):
    params = (time_weight.astype(jnp.float32), time_bias.astype(jnp.float32), mixing_weight.astype(jnp.float32), query_bias.astype(jnp.float32), value_bias.astype(jnp.float32), output_weight.astype(jnp.float32), output_bias.astype(jnp.float32), first_gain.astype(jnp.float32), first_shift.astype(jnp.float32), widen_weight.astype(jnp.float32), widen_bias.astype(jnp.float32), narrow_weight.astype(jnp.float32), narrow_bias.astype(jnp.float32), second_gain.astype(jnp.float32), second_shift.astype(jnp.float32))
    row_count = tokens.shape[0]
    seq_total = tokens.shape[1]
    model_width = tokens.shape[2]
    group_total = seq_total // SEQ_DEV

    def regroup(array):
        return array.astype(jnp.float32).reshape(row_count, group_total, SEQ_DEV, model_width).transpose(1, 0, 2, 3)

    def ungroup(array):
        return array.transpose(1, 0, 2, 3).reshape(row_count, seq_total, model_width)
    inputs_all = regroup(tokens)
    upstream_all = regroup(cotangent)
    steps_all = timesteps.reshape(group_total, SEQ_DEV)
    bounds_all = boundary.reshape(group_total, SEQ_DEV)
    weights_all = importance.reshape(group_total, SEQ_DEV)

    def advance(totals, group_item):
        inputs, upstream, step_ids, bounds, weights = group_item

        def local_loss(param_set, input_set):
            return layer_loss(param_set, input_set, upstream, step_ids, bounds, weights)
        total_loss, pullback, out_full = jax.vjp(local_loss, params, inputs, has_aux=True)
        param_grads, input_grad = pullback(jnp.ones_like(total_loss))
        totals = jax.tree.map(jnp.add, totals, param_grads)
        return (totals, (out_full.astype(jnp.bfloat16), input_grad.astype(jnp.bfloat16)))
    totals, outcome = lax.scan(advance, jax.tree.map(jnp.zeros_like, params), (inputs_all, upstream_all, steps_all, bounds_all, weights_all))
    out_groups, grad_groups = outcome
    return (ungroup(out_groups), ungroup(grad_groups), totals[0], totals[1], totals[2], totals[3], totals[4], totals[5], totals[6], totals[7], totals[8], totals[9], totals[10], totals[11], totals[12], totals[13], totals[14])
```

```python
from functools import partial
import math

import jax
import jax.numpy as jnp
from jax import lax
from jax.experimental import pallas as pl
from jax.experimental.pallas import tpu as pltpu
from jax.sharding import PartitionSpec as P

HEADS = 12
HEAD = 64


epsilon = 1e-05


def sinusoid(step_ids, code_width):
    half_width = code_width // 2
    frequency = jnp.exp(-math.log(10000.0) * jnp.arange(half_width, dtype=jnp.float32) / half_width)
    angles = step_ids.astype(jnp.float32)[:, None] * frequency[None, :]
    return jnp.concatenate([jnp.cos(angles), jnp.sin(angles)], axis=-1)


def layer_norm(inputs, norm_gain, norm_shift):
    centred = inputs - jnp.mean(inputs, axis=-1, keepdims=True)
    variance = jnp.mean(centred * centred, axis=-1, keepdims=True)
    return centred * lax.rsqrt(variance + epsilon) * norm_gain + norm_shift


def reduce_dp(parts):
    shares = (
        lax.psum_scatter(
            parts[0].astype(jnp.bfloat16), "dp", scatter_dimension=1, tiled=True
        ).astype(jnp.float32),
        lax.psum_scatter(
            parts[1].astype(jnp.bfloat16), "dp", scatter_dimension=0, tiled=True
        ).astype(jnp.float32),
        lax.psum_scatter(
            parts[2].astype(jnp.bfloat16), "dp", scatter_dimension=0, tiled=True
        ).astype(jnp.float32),
        lax.psum_scatter(
            parts[3].astype(jnp.bfloat16), "dp", scatter_dimension=0, tiled=True
        ).astype(jnp.float32),
        lax.psum_scatter(
            parts[4].astype(jnp.bfloat16), "dp", scatter_dimension=0, tiled=True
        ).astype(jnp.float32),
        lax.psum_scatter(
            parts[5].astype(jnp.bfloat16), "dp", scatter_dimension=0, tiled=True
        ).astype(jnp.float32),
        lax.psum_scatter(
            parts[6].astype(jnp.bfloat16), "dp", scatter_dimension=0, tiled=True
        ).astype(jnp.float32),
        lax.psum_scatter(
            parts[7].astype(jnp.bfloat16), "dp", scatter_dimension=0, tiled=True
        ).astype(jnp.float32),
        lax.psum_scatter(
            parts[8].astype(jnp.bfloat16), "dp", scatter_dimension=0, tiled=True
        ).astype(jnp.float32),
        lax.psum_scatter(
            parts[9].astype(jnp.bfloat16), "dp", scatter_dimension=0, tiled=True
        ).astype(jnp.float32),
        lax.psum_scatter(
            parts[10].astype(jnp.bfloat16), "dp", scatter_dimension=0, tiled=True
        ).astype(jnp.float32),
        lax.psum_scatter(
            parts[11].astype(jnp.bfloat16), "dp", scatter_dimension=0, tiled=True
        ).astype(jnp.float32),
        lax.psum_scatter(
            parts[12].astype(jnp.bfloat16), "dp", scatter_dimension=0, tiled=True
        ).astype(jnp.float32),
        lax.psum_scatter(
            parts[13].astype(jnp.bfloat16), "dp", scatter_dimension=0, tiled=True
        ).astype(jnp.float32),
        lax.psum_scatter(
            parts[14].astype(jnp.bfloat16), "dp", scatter_dimension=0, tiled=True
        ).astype(jnp.float32),
    )
    summed = (
        lax.psum(shares[0].astype(jnp.bfloat16), "blk").astype(jnp.float32),
        lax.psum(shares[1].astype(jnp.bfloat16), "blk").astype(jnp.float32),
        lax.psum(shares[2].astype(jnp.bfloat16), "blk").astype(jnp.float32),
        lax.psum(shares[3].astype(jnp.bfloat16), "blk").astype(jnp.float32),
        lax.psum(shares[4].astype(jnp.bfloat16), "blk").astype(jnp.float32),
        lax.psum(shares[5].astype(jnp.bfloat16), "blk").astype(jnp.float32),
        lax.psum(shares[6].astype(jnp.bfloat16), "blk").astype(jnp.float32),
        lax.psum(shares[7].astype(jnp.bfloat16), "blk").astype(jnp.float32),
        lax.psum(shares[8].astype(jnp.bfloat16), "blk").astype(jnp.float32),
        lax.psum(shares[9].astype(jnp.bfloat16), "blk").astype(jnp.float32),
        lax.psum(shares[10].astype(jnp.bfloat16), "blk").astype(jnp.float32),
        lax.psum(shares[11].astype(jnp.bfloat16), "blk").astype(jnp.float32),
        lax.psum(shares[12].astype(jnp.bfloat16), "blk").astype(jnp.float32),
        lax.psum(shares[13].astype(jnp.bfloat16), "blk").astype(jnp.float32),
        lax.psum(shares[14].astype(jnp.bfloat16), "blk").astype(jnp.float32),
    )
    return (
        lax.all_gather(summed[0].astype(jnp.bfloat16), "dp", axis=1, tiled=True).astype(
            jnp.float32
        ),
        lax.all_gather(summed[1].astype(jnp.bfloat16), "dp", axis=0, tiled=True).astype(
            jnp.float32
        ),
        lax.all_gather(summed[2].astype(jnp.bfloat16), "dp", axis=0, tiled=True).astype(
            jnp.float32
        ),
        lax.all_gather(summed[3].astype(jnp.bfloat16), "dp", axis=0, tiled=True).astype(
            jnp.float32
        ),
        lax.all_gather(summed[4].astype(jnp.bfloat16), "dp", axis=0, tiled=True).astype(
            jnp.float32
        ),
        lax.all_gather(summed[5].astype(jnp.bfloat16), "dp", axis=0, tiled=True).astype(
            jnp.float32
        ),
        lax.all_gather(summed[6].astype(jnp.bfloat16), "dp", axis=0, tiled=True).astype(
            jnp.float32
        ),
        lax.all_gather(summed[7].astype(jnp.bfloat16), "dp", axis=0, tiled=True).astype(
            jnp.float32
        ),
        lax.all_gather(summed[8].astype(jnp.bfloat16), "dp", axis=0, tiled=True).astype(
            jnp.float32
        ),
        lax.all_gather(summed[9].astype(jnp.bfloat16), "dp", axis=0, tiled=True).astype(
            jnp.float32
        ),
        lax.all_gather(summed[10].astype(jnp.bfloat16), "dp", axis=0, tiled=True).astype(
            jnp.float32
        ),
        lax.all_gather(summed[11].astype(jnp.bfloat16), "dp", axis=0, tiled=True).astype(
            jnp.float32
        ),
        lax.all_gather(summed[12].astype(jnp.bfloat16), "dp", axis=0, tiled=True).astype(
            jnp.float32
        ),
        lax.all_gather(summed[13].astype(jnp.bfloat16), "dp", axis=0, tiled=True).astype(
            jnp.float32
        ),
        lax.all_gather(summed[14].astype(jnp.bfloat16), "dp", axis=0, tiled=True).astype(
            jnp.float32
        ),
    )


def general_shards(
    tokens,
    timesteps,
    boundary,
    importance,
    cotangent,
    time_weight,
    time_bias,
    mixing_weight,
    query_bias,
    value_bias,
    output_weight,
    output_bias,
    first_gain,
    first_shift,
    widen_weight,
    widen_bias,
    narrow_weight,
    narrow_bias,
    second_gain,
    second_shift,
):
    model_width = tokens.shape[2]
    score_scale = 1.0 / math.sqrt(HEAD)
    inputs, upstream = (tokens, cotangent)
    step_ids, bounds, weights = (timesteps, boundary, importance)
    offset = lax.axis_index("blk") * tokens.shape[0]
    row_count = inputs.shape[0]
    group_count = inputs.shape[1]
    time_code = sinusoid(step_ids, time_weight.shape[0]).astype(jnp.bfloat16)
    time_embed = jnp.dot(
        time_code, time_weight, preferred_element_type=jnp.float32
    ) + time_bias.astype(jnp.float32)
    hidden = inputs.astype(jnp.float32) + time_embed[None]
    hidden_low = hidden.astype(jnp.bfloat16)
    bias_pack = jnp.concatenate(
        [
            query_bias.astype(jnp.float32),
            jnp.zeros((model_width,), jnp.float32),
            value_bias.astype(jnp.float32),
        ]
    )
    packed = (
        jnp.einsum("lsd,de->lse", hidden_low, mixing_weight, preferred_element_type=jnp.float32)
        + bias_pack
    ).astype(jnp.bfloat16)
    queries = packed[..., :model_width].reshape(row_count, group_count, HEADS, HEAD)
    keys_values = packed[..., model_width:]
    both_all = lax.all_gather(keys_values, "blk", axis=0, tiled=True)
    total_rows = both_all.shape[0]
    keys_all = both_all[..., :model_width].reshape(total_rows, group_count, HEADS, HEAD)
    values_all = both_all[..., model_width:].reshape(total_rows, group_count, HEADS, HEAD)
    scores = (
        jnp.einsum("qshe,kshe->shqk", queries, keys_all, preferred_element_type=jnp.float32)
        * score_scale
    )
    row_peak = jnp.max(scores, axis=-1, keepdims=True)
    powered = jnp.exp(scores - row_peak)
    totals_soft = jnp.sum(powered, axis=-1, keepdims=True)
    probs_low = (powered / totals_soft).astype(jnp.bfloat16)
    log_total = row_peak + jnp.log(totals_soft)
    context = jnp.einsum(
        "shqk,kshe->qshe", probs_low, values_all, preferred_element_type=jnp.float32
    )
    context_low = context.reshape(row_count, group_count, model_width).astype(jnp.bfloat16)
    gain_one = first_gain.astype(jnp.float32)
    shift_one = first_shift.astype(jnp.float32)
    gain_two = second_gain.astype(jnp.float32)
    shift_two = second_shift.astype(jnp.float32)
    first_sum = (
        hidden
        + jnp.einsum("lsd,de->lse", context_low, output_weight, preferred_element_type=jnp.float32)
        + output_bias.astype(jnp.float32)
    )
    leading_norm, first_back = jax.vjp(layer_norm, first_sum, gain_one, shift_one)
    norm_reduced = leading_norm.astype(jnp.bfloat16)
    before_activation = jnp.einsum(
        "ikg,gv->ikv", norm_reduced, widen_weight, preferred_element_type=jnp.float32
    ) + widen_bias.astype(jnp.float32)
    activated, gelu_back = jax.vjp(partial(jax.nn.gelu, approximate=False), before_activation)
    activation_reduced = activated.astype(jnp.bfloat16)
    residual_sum = (
        leading_norm
        + jnp.einsum(
            "ema,aw->emw", activation_reduced, narrow_weight, preferred_element_type=jnp.float32
        )
        + narrow_bias.astype(jnp.float32)
    )
    out_full, second_back = jax.vjp(layer_norm, residual_sum, gain_two, shift_two)
    output = out_full.astype(jnp.bfloat16)
    positions = jnp.arange(row_count, dtype=jnp.int32) + offset
    row_weight = jnp.where(positions[:, None] >= bounds[None, :], weights[None, :], 0.0)
    out_grad = upstream.astype(jnp.float32) * row_weight[:, :, None]
    second_grad, second_gain_grad, second_shift_grad = second_back(out_grad)
    shrink_bias_grad = jnp.sum(second_grad, axis=(0, 1))
    narrow_reduced = second_grad.astype(jnp.bfloat16)
    shrink_weight_grad = jnp.einsum(
        "egk,egy->ky", activation_reduced, narrow_reduced, preferred_element_type=jnp.float32
    )
    act_grad = jnp.einsum(
        "ztv,ov->zto", narrow_reduced, narrow_weight, preferred_element_type=jnp.float32
    )
    pre_grad = gelu_back(act_grad)[0]
    expand_bias_grad = jnp.sum(pre_grad, axis=(0, 1))
    before_reduced = pre_grad.astype(jnp.bfloat16)
    expand_weight_grad = jnp.einsum(
        "thk,thr->kr", norm_reduced, before_reduced, preferred_element_type=jnp.float32
    )
    norm_grad = second_grad + jnp.einsum(
        "xcu,pu->xcp", before_reduced, widen_weight, preferred_element_type=jnp.float32
    )
    first_grad, first_gain_grad, first_shift_grad = first_back(norm_grad)
    output_bias_grad = jnp.sum(first_grad, axis=(0, 1))
    attn_low = first_grad.astype(jnp.bfloat16)
    output_weight_grad = jnp.einsum(
        "lsd,lse->de", context_low, attn_low, preferred_element_type=jnp.float32
    )
    context_grad = jnp.einsum(
        "lse,de->lsd", attn_low, output_weight, preferred_element_type=jnp.float32
    )
    context_grad = context_grad.astype(jnp.bfloat16).reshape(row_count, group_count, HEADS, HEAD)
    again = (
        jnp.einsum("qshe,kshe->shqk", queries, keys_all, preferred_element_type=jnp.float32)
        * score_scale
    )
    soft_probs = jnp.exp(again - log_total)
    prob_grad = jnp.einsum(
        "qshe,kshe->shqk", context_grad, values_all, preferred_element_type=jnp.float32
    )
    row_dot = jnp.sum(soft_probs * prob_grad, axis=-1, keepdims=True)
    score_low = (soft_probs * (prob_grad - row_dot)).astype(jnp.bfloat16)
    query_grad = (
        jnp.einsum("shqk,kshe->qshe", score_low, keys_all, preferred_element_type=jnp.float32)
        * score_scale
    )
    query_every, cgrad_every = (
        lax.all_gather(queries, "blk", axis=0, tiled=True),
        lax.all_gather(context_grad, "blk", axis=0, tiled=True),
    )
    total_every, dot_every = (
        lax.all_gather(log_total, "blk", axis=2, tiled=True),
        lax.all_gather(row_dot, "blk", axis=2, tiled=True),
    )
    own_keys = packed[..., model_width : 2 * model_width].reshape(
        row_count, group_count, HEADS, HEAD
    )
    own_values = packed[..., 2 * model_width :].reshape(row_count, group_count, HEADS, HEAD)
    local_scores = (
        jnp.einsum("qshe,kshe->shqk", query_every, own_keys, preferred_element_type=jnp.float32)
        * score_scale
    )
    local_probs = jnp.exp(local_scores - total_every)
    local_low = local_probs.astype(jnp.bfloat16)
    local_grad = jnp.einsum(
        "qshe,kshe->shqk", cgrad_every, own_values, preferred_element_type=jnp.float32
    )
    local_score_low = (local_probs * (local_grad - dot_every)).astype(jnp.bfloat16)
    value_own = jnp.einsum(
        "shqk,qshe->kshe", local_low, cgrad_every, preferred_element_type=jnp.float32
    )
    key_own = (
        jnp.einsum(
            "shqk,qshe->kshe", local_score_low, query_every, preferred_element_type=jnp.float32
        )
        * score_scale
    )
    key_here = jnp.concatenate(
        [
            key_own.reshape(row_count, group_count, model_width),
            value_own.reshape(row_count, group_count, model_width),
        ],
        axis=-1,
    )
    packed_grad = jnp.concatenate(
        [query_grad.reshape(row_count, group_count, model_width), key_here], axis=-1
    )
    query_bias_grad = jnp.sum(packed_grad[..., :model_width], axis=(0, 1))
    value_bias_grad = jnp.sum(packed_grad[..., 2 * model_width :], axis=(0, 1))
    packed_low = packed_grad.astype(jnp.bfloat16)
    mixing_weight_grad = jnp.einsum(
        "lsd,lse->de", hidden_low, packed_low, preferred_element_type=jnp.float32
    )
    hidden_grad = first_grad + jnp.einsum(
        "lse,de->lsd", packed_low, mixing_weight, preferred_element_type=jnp.float32
    )
    input_grad = hidden_grad.astype(jnp.bfloat16)
    time_total = jnp.sum(hidden_grad, axis=0)
    time_bias_grad = jnp.sum(time_total, axis=0)
    time_weight_grad = jnp.dot(
        time_code.astype(jnp.float32).T, time_total, precision=lax.Precision.HIGHEST
    )
    parts = (
        time_weight_grad,
        time_bias_grad,
        mixing_weight_grad,
        query_bias_grad,
        value_bias_grad,
        output_weight_grad,
        output_bias_grad,
        first_gain_grad,
        first_shift_grad,
        expand_weight_grad,
        expand_bias_grad,
        shrink_weight_grad,
        shrink_bias_grad,
        second_gain_grad,
        second_shift_grad,
    )
    summed = reduce_dp(parts)
    return (
        output,
        input_grad,
        summed[0],
        summed[1],
        summed[2],
        summed[3],
        summed[4],
        summed[5],
        summed[6],
        summed[7],
        summed[8],
        summed[9],
        summed[10],
        summed[11],
        summed[12],
        summed[13],
        summed[14],
    )


LOW = jnp.bfloat16
FULL = jnp.float32
PLACES = {"c": ("dp", 1), "y": ("dp", 2), "z": ("dp", 4), "w": ("dp", 8), "x": ("blk", 1)}
SHRINK_ORDERS = ("xyz", "yxz")
EXPAND_ORDERS = ("xyz", "yzx", "zxy")
MIXING_ORDERS = ("xyz", "yzx", "zxy")
ALL_ORDERS = ("xyz", "yxz", "yzx", "zxy")
CORE, SIDE, NUMBERS = 0, 1, 2
WIDTH = 768
GRAD_ROWS = 3072


def swap(value, place):
    axis, bit = PLACES[place]
    count = lax.axis_size(axis)
    return lax.ppermute(value, axis, [(i, i ^ bit) for i in range(count)])


def place_bit(place):
    axis, bit = PLACES[place]
    return (lax.axis_index(axis) // bit) % 2


def device_info():
    core = place_bit("c")
    numbers = []
    for order in ALL_ORDERS:
        number = core
        for place in order:
            number = number * 2 + place_bit(place)
        numbers.append(number)
    return jnp.stack([core, lax.axis_index("blk")] + numbers).astype(jnp.int32)


def order_number(info_ref, orders, unit):
    number = info_ref[NUMBERS + ALL_ORDERS.index(orders[0])]
    for k in range(1, len(orders)):
        number = jnp.where(unit == k, info_ref[NUMBERS + ALL_ORDERS.index(orders[k])], number)
    return number


def weight_half(left, right, info, orders, left_of, right_of, got=None):
    units = len(orders)
    block = GRAD_ROWS // units // 16
    tile_rows = 4 * block
    quarter = 4 * block
    half = 8 * block
    mine = got is not None

    def tile_of(step, info_ref):
        core = info_ref[CORE]
        side = core if mine else 1 - core
        return 4 * (step // 2) + 2 * side + step % 2

    def body(info_ref, left_ref, right_ref, *refs):
        step = pl.program_id(0)
        unit = step // 2
        number = order_number(info_ref, orders, unit)
        product = turned_times(left_ref[...], right_ref[...])
        spots = [((4 * (step % 2) + i) ^ number) & 7 for i in range(4)]
        if not mine:
            (out_ref,) = refs
            low = product.astype(LOW)
            for i, spot in enumerate(spots):
                row = pl.multiple_of(unit * half + spot * block, block)
                out_ref[pl.ds(row, block), :] = low[i * block : (i + 1) * block, :]
            return
        got_ref, upper_refs, lower_ref = refs[0], refs[1:-1], refs[-1]
        upper = (step % 2) ^ ((number // 4) % 2)
        low = []
        for i, spot in enumerate(spots):
            row = pl.multiple_of(unit * half + spot * block, block)
            total = product[i * block : (i + 1) * block, :] + got_ref[pl.ds(row, block), :].astype(FULL)
            low.append(total.astype(LOW))

        @pl.when(upper == 0)
        def _():
            for i, spot in enumerate(spots):
                row = pl.multiple_of(unit * quarter + (spot & 3) * block, block)
                lower_ref[pl.ds(row, block), :] = low[i]

        for k in range(units):

            @pl.when((upper == 1) & (unit == k))
            def _(k=k):
                for i, spot in enumerate(spots):
                    row = pl.multiple_of((spot & 3) * block, block)
                    upper_refs[k][pl.ds(row, block), :] = low[i]

    rows = left.shape[0]
    operands = [left, right]
    in_specs = [
        pl.BlockSpec((rows, tile_rows), lambda s, p: (0, left_of(tile_of(s, p)))),
        pl.BlockSpec((rows, WIDTH), lambda s, p: (0, right_of(tile_of(s, p)))),
    ]

    def whole(count):
        return pl.BlockSpec((count, WIDTH), lambda s, p: (0, 0))

    if mine:
        operands.append(got)
        in_specs.append(
            pl.BlockSpec((units * half, WIDTH), lambda s, p: (0, 0), pipeline_mode=ONE)
        )
        counts = [quarter] * units + [units * quarter]
    else:
        counts = [units * half]
    found = pl.pallas_call(
        body,
        grid_spec=pltpu.PrefetchScalarGridSpec(
            num_scalar_prefetch=1,
            grid=(2 * units,),
            in_specs=in_specs,
            out_specs=[whole(c) for c in counts],
        ),
        out_shape=[jax.ShapeDtypeStruct((c, WIDTH), LOW) for c in counts],
        compiler_params=kernel_params(),
        cost_estimate=pl.CostEstimate(
            flops=rows * GRAD_ROWS * WIDTH, bytes_accessed=6000000, transcendentals=0
        ),
        name="weight_keep" if mine else "weight_send",
    )(info, *operands)
    return found if mine else found[0]


def widen_out(near, far, info, orders, first_tile, tile_count, columns):
    units = len(orders)
    block = GRAD_ROWS // units // 16
    tall = 4 * block * tile_count // columns
    pieces = 4 if columns == 1 else 1
    stride = tall // block
    first_block = 4 * first_tile

    def body(info_ref, near_ref, far_ref, out_ref):
        step = pl.program_id(0)
        for column in range(columns):
            for piece in range(pieces):
                index = first_block + column * stride + step * pieces + piece
                unit = index // 16
                number = order_number(info_ref, orders, unit)
                own = (index % 16) // 8 == info_ref[CORE]
                row = pl.multiple_of((unit * 8 + ((index ^ number) & 7)) * block, block)
                target = (
                    slice(piece * block, (piece + 1) * block),
                    slice(column * WIDTH, (column + 1) * WIDTH),
                )

                @pl.when(own)
                def _(row=row, target=target):
                    out_ref[target] = near_ref[pl.ds(row, block), :].astype(FULL)

                @pl.when(jnp.logical_not(own))
                def _(row=row, target=target):
                    out_ref[target] = far_ref[pl.ds(row, block), :].astype(FULL)

    whole = pl.BlockSpec(near.shape, lambda t, p: (0, 0), pipeline_mode=ONE)
    return pl.pallas_call(
        body,
        grid_spec=pltpu.PrefetchScalarGridSpec(
            num_scalar_prefetch=1,
            grid=(tall // (pieces * block),),
            in_specs=[whole, whole],
            out_specs=pl.BlockSpec((pieces * block, columns * WIDTH), lambda t, p: (t, 0)),
        ),
        out_shape=jax.ShapeDtypeStruct((tall, columns * WIDTH), FULL),
        compiler_params=kernel_params(),
        cost_estimate=pl.CostEstimate(
            flops=0, bytes_accessed=tall * columns * WIDTH * 6, transcendentals=0
        ),
        name="widen_out",
    )(info, near, far)


def combine(outputs):
    arrays = []

    def number(array):
        for k, known in enumerate(arrays):
            if known is array:
                return k
        arrays.append(array)
        return len(arrays) - 1

    plan = [
        [[(number(array), row, rows) for array, row, rows in piece] for piece in pieces]
        for pieces in outputs
    ]
    heights = [sum(piece[0][2] for piece in pieces) for pieces in outputs]
    width = arrays[0].shape[1]

    def body(*refs):
        sources, targets = refs[: len(arrays)], refs[len(arrays) :]
        for pieces, target in zip(plan, targets):
            place = 0
            for piece in pieces:
                rows = piece[0][2]
                for first in range(0, rows, 128):
                    count = min(128, rows - first)
                    values = [sources[k][row + first : row + first + count, :] for k, row, _ in piece]
                    total = values[0] if len(values) == 1 else values[0] + values[1]
                    target[place + first : place + first + count, :] = total
                place += rows

    vmem = pl.BlockSpec(memory_space=pltpu.VMEM)
    return pl.pallas_call(
        body,
        in_specs=[vmem] * len(arrays),
        out_specs=[vmem] * len(outputs),
        out_shape=[jax.ShapeDtypeStruct((h, width), LOW) for h in heights],
        compiler_params=kernel_params(),
        cost_estimate=pl.CostEstimate(
            flops=0, bytes_accessed=4 * sum(heights) * width, transcendentals=0
        ),
        name="combine",
    )(*arrays)


def flow(orders, uppers, lower):
    units = len(orders)
    size = lower.shape[0] // units
    mine = [(lower, k * size, size) for k in range(units)]

    def cut(view, part):
        array, row, rows = view
        return array, row + part * rows // 2, rows // 2

    got = yield [(order[0], value) for order, value in zip(orders, uppers)]
    for level in (1, 2):
        views = [(g, 0, size) for g in got]
        away = [[(cut(m, 1), cut(v, 1))] for m, v in zip(mine, views)]
        kept = [(cut(m, 0), cut(v, 0)) for m, v in zip(mine, views)]
        size = size // 2
        *sends, rest = combine(away + [kept])
        mine = [(rest, k * size, size) for k in range(units)]
        places = [order[level] for order in orders]
        got = yield list(zip(places, sends))
    (joined,) = combine([[(m, (g, 0, size)) for m, g in zip(mine, got)]])
    (other,) = yield [("w", joined)]
    values = combine([[((joined, k * size, size), (other, k * size, size))] for k in range(units)])
    for level in (2, 1, 0):
        got = yield [(order[level], value) for order, value in zip(orders, values)]
        pieces = [[((v, 0, size),), ((g, 0, size),)] for v, g in zip(values, got)]
        size = 2 * size
        if level > 0:
            values = combine(pieces)
    (near,) = combine([sum(pieces, [])])
    (far,) = yield [("c", near)]
    return near, far


SMALL_SUMS = 96
SMALL_ROWS = 16


def small_flow(packed):
    for place in "wzyxc":
        (other,) = yield [(place, packed)]
        count = packed.shape[0]
        (packed,) = combine(
            [
                [
                    ((packed, 0, SMALL_SUMS), (other, 0, SMALL_SUMS)),
                    ((packed, SMALL_SUMS, count - SMALL_SUMS),),
                    ((other, SMALL_SUMS, count - SMALL_SUMS),),
                ]
            ]
        )
    return packed


def pack_small(sums_zero, sums_one, sums_two, expand_bias, time_total, time_code):
    pair, code_width = time_code.shape
    width = sums_one.shape[1]
    blocks = width // 128

    def body(zero_ref, one_ref, two_ref, bias_ref, total_ref, code_ref, out_ref):
        bias = [bias_ref[:, k * width : (k + 1) * width] for k in range(4)]
        rows = jnp.concatenate(
            [zero_ref[0] + zero_ref[1], one_ref[:3, :], two_ref[:3, :]]
            + bias
            + [jnp.zeros((4, width), FULL)],
            axis=0,
        ).astype(LOW)
        for j in range(blocks):
            out_ref[16 * j : 16 * j + 16, :] = rows[:, 128 * j : 128 * j + 128]
        totals = [
            total_ref[s, :, 128 * j : 128 * j + 128] for s in range(pair) for j in range(blocks)
        ]
        codes = code_ref[...].astype(FULL)
        out_ref[SMALL_SUMS:, :] = jnp.concatenate(
            totals + [codes, jnp.zeros((16 - pair * (blocks + 1), 128), FULL)], axis=0
        ).astype(LOW)

    return pl.pallas_call(
        body,
        out_shape=jax.ShapeDtypeStruct((SMALL_SUMS + SMALL_ROWS, 128), LOW),
        compiler_params=kernel_params(),
        name="pack_small",
    )(sums_zero, sums_one, sums_two, expand_bias, time_total, time_code)


def unpack_small(packed, pair, width, code_width):
    blocks = width // 128
    count = packed.shape[0]
    devices = (count - SMALL_SUMS) // SMALL_ROWS

    def body(packed_ref, sums_ref, weight_ref, bias_ref, wide_ref):
        wide_ref[...] = packed_ref[...].astype(FULL)

        def every(row):
            return wide_ref[pl.ds(SMALL_SUMS + row, devices, stride=SMALL_ROWS), :]

        codes = [every(pair * blocks + s).astype(LOW) for s in range(pair)]
        for j in range(blocks):
            columns = slice(128 * j, 128 * j + 128)
            sums_ref[:, columns] = wide_ref[16 * j : 16 * j + 16, :]
            totals = [every(s * blocks + j) for s in range(pair)]
            weight_ref[:, columns] = sum(
                turned_times(c, t.astype(LOW)) for c, t in zip(codes, totals)
            )
            bias_ref[:, columns] = jnp.sum(sum(totals), axis=0, keepdims=True)

    return pl.pallas_call(
        body,
        out_shape=[
            jax.ShapeDtypeStruct((16, width), FULL),
            jax.ShapeDtypeStruct((code_width, width), FULL),
            jax.ShapeDtypeStruct((1, width), FULL),
        ],
        scratch_shapes=[pltpu.VMEM((count, 128), FULL)],
        compiler_params=kernel_params(),
        name="unpack_small",
    )(packed)


class Order:
    def __init__(self):
        self.token = None
        self.flows = {}

    def after(self, *values):
        if self.token is None:
            return values
        return lax.optimization_barrier((self.token,) + tuple(values))[1:]

    def run(self, function, *values, token=0):
        found = function(*self.after(*values))
        self.token = found[token] if isinstance(found, (tuple, list)) else found
        return found

    def begin(self, name, steps):
        pairs = next(steps)
        self.flows[name] = steps, [swap(value, place) for place, value in pairs]

    def advance(self, name):
        steps, got = self.flows[name]
        try:
            pairs = steps.send(list(self.after(*got)))
        except StopIteration as stop:
            return stop.value
        self.token = pairs[0][1]
        self.flows[name] = steps, [swap(value, place) for place, value in pairs]
        return None


VMEM_LIMIT = 21 * 1024 * 1024
ONE = pl.Buffered(1)


def kernel_params():
    return pltpu.CompilerParams(vmem_limit_bytes=VMEM_LIMIT)


def times(left, right):
    return jnp.dot(left, right, preferred_element_type=FULL)


def times_turned(left, right):
    return lax.dot_general(left, right, (((1,), (1,)), ((), ())), preferred_element_type=FULL)


def turned_times(left, right):
    return lax.dot_general(left, right, (((0,), (0,)), ((), ())), preferred_element_type=FULL)


def split_rows(values, info):
    near, group, width = values.shape
    pair = group // 2
    count = near * group

    def body(info_ref, values_ref, away_ref, own_ref):
        side = info_ref[SIDE]
        rows = values_ref[...].reshape(count, width)
        row = lax.broadcasted_iota(jnp.int32, (count, count), 0)
        column = lax.broadcasted_iota(jnp.int32, (count, count), 1)
        half = pair * near
        first = jnp.where(row < half, pair * (1 - side), pair * side)
        place = jnp.where(row < half, row, row - half)
        source = (place % near) * group + first + place // near
        pick = (source == column).astype(FULL).astype(LOW)
        moved = times(pick, rows).astype(LOW)
        away_ref[...] = moved[:half].reshape(pair, near, width)
        own_ref[...] = moved[half:].reshape(pair, near, width)

    shape = jax.ShapeDtypeStruct((pair, near, width), values.dtype)
    return pl.pallas_call(
        body,
        in_specs=[
            pl.BlockSpec(memory_space=pltpu.SMEM),
            pl.BlockSpec(memory_space=pltpu.VMEM),
        ],
        out_shape=[shape, shape],
        compiler_params=kernel_params(),
        name="split_rows",
    )(info, values)


def join_rows(own, got, info):
    pair, near, width = own.shape
    group = 2 * pair
    count = near * group

    def body(info_ref, own_ref, got_ref, out_ref):
        side = info_ref[SIDE]
        row = lax.broadcasted_iota(jnp.int32, (count, count), 0)
        column = lax.broadcasted_iota(jnp.int32, (count, count), 1)
        half = pair * near
        sequence = row % group
        position = row // group
        from_own = sequence // pair == side
        source = jnp.where(from_own, 0, half) + (sequence % pair) * near + position
        pick = (source == column).astype(FULL).astype(LOW)
        rows = jnp.concatenate(
            [own_ref[...].reshape(half, width), got_ref[...].reshape(half, width)], axis=0
        )
        out_ref[...] = times(pick, rows).astype(LOW).reshape(near, group, width)

    return pl.pallas_call(
        body,
        in_specs=[
            pl.BlockSpec(memory_space=pltpu.SMEM),
            pl.BlockSpec(memory_space=pltpu.VMEM),
            pl.BlockSpec(memory_space=pltpu.VMEM),
        ],
        out_shape=jax.ShapeDtypeStruct((near, group, width), own.dtype),
        compiler_params=kernel_params(),
        name="join_rows",
    )(info, own, got)


QUERY_BIAS, VALUE_BIAS, OUTPUT_BIAS, FIRST_GAIN, FIRST_SHIFT = range(5)
NARROW_BIAS, SECOND_GAIN, SECOND_SHIFT = range(5, 8)


def head_masks(scale):
    lane = lax.broadcasted_iota(jnp.int32, (1, 2 * HEAD), 1)
    first = jnp.where(lane < HEAD, scale, 0.0).astype(LOW)
    second = jnp.where(lane < HEAD, 0.0, scale).astype(LOW)
    return first, second


def attend(own, got, embed, mixing_weight, output_weight, vectors):
    pair, near, width = own.shape
    length = 2 * near
    scale = 1.0 / math.sqrt(HEAD)
    duo = 2 * HEAD

    def body(own_ref, got_ref, embed_ref, mix_ref, wout_ref, vec_ref, left_ref, packed_ref,
             probs_ref, centred_ref, scale_ref, norm_ref):
        hidden = jnp.concatenate([own_ref[0], got_ref[0]], axis=0).astype(FULL) + embed_ref[0]
        hidden_low = hidden.astype(LOW)
        left_ref[:, :width] = hidden_low
        for part, bias in ((0, QUERY_BIAS), (1, None), (2, VALUE_BIAS)):
            columns = slice(part * width, (part + 1) * width)
            product = times(hidden_low, mix_ref[:, columns])
            if bias is not None:
                product = product + vec_ref[bias : bias + 1, :]
            packed_ref[:, columns] = product.astype(LOW)
        masks = head_masks(scale)
        lane = lax.broadcasted_iota(jnp.int32, (length, duo), 1)
        for j in range(width // duo):
            query = packed_ref[:, j * duo : (j + 1) * duo]
            key = packed_ref[:, width + j * duo : width + (j + 1) * duo]
            value = packed_ref[:, 2 * width + j * duo : 2 * width + (j + 1) * duo]
            found = []
            for head in range(2):
                scores = times_turned(query * masks[head], key)
                peak = jnp.max(scores, axis=-1, keepdims=True)
                powered = jnp.exp(scores - peak)
                total = jnp.sum(powered, axis=-1, keepdims=True)
                low = (powered * (1.0 / total)).astype(LOW)
                probs_ref[0, 2 * j + head] = low
                found.append(times(low, value))
            left_ref[:, width + j * duo : width + (j + 1) * duo] = jnp.where(
                lane < HEAD, found[0], found[1]
            ).astype(LOW)
        first_sum = (
            hidden
            + times(left_ref[:, width:], wout_ref[...])
            + vec_ref[OUTPUT_BIAS : OUTPUT_BIAS + 1, :]
        )
        centred = first_sum - jnp.mean(first_sum, axis=-1, keepdims=True)
        variance = jnp.mean(centred * centred, axis=-1, keepdims=True)
        inverse = lax.rsqrt(variance + epsilon)
        centred = centred * inverse
        centred_ref[...] = centred
        scale_ref[...] = jnp.broadcast_to(inverse, (length, 128))
        norm_ref[...] = (
            centred * vec_ref[FIRST_GAIN : FIRST_GAIN + 1, :]
            + vec_ref[FIRST_SHIFT : FIRST_SHIFT + 1, :]
        ).astype(LOW)

    rows = pair * length
    half = pl.BlockSpec((1, near, width), lambda s: (s, 0, 0))

    def by_rows(columns):
        return pl.BlockSpec((length, columns), lambda s: (s, 0))

    def whole(array):
        return pl.BlockSpec(array.shape, lambda s: (0,) * array.ndim, pipeline_mode=ONE)

    return pl.pallas_call(
        body,
        grid=(pair,),
        in_specs=[
            half,
            half,
            pl.BlockSpec((1, 1, width), lambda s: (s, 0, 0)),
            whole(mixing_weight),
            whole(output_weight),
            whole(vectors),
        ],
        out_specs=[
            by_rows(2 * width),
            by_rows(3 * width),
            pl.BlockSpec((1, HEADS, length, length), lambda s: (s, 0, 0, 0)),
            by_rows(width),
            by_rows(128),
            by_rows(width),
        ],
        out_shape=[
            jax.ShapeDtypeStruct((rows, 2 * width), LOW),
            jax.ShapeDtypeStruct((rows, 3 * width), LOW),
            jax.ShapeDtypeStruct((pair, HEADS, length, length), LOW),
            jax.ShapeDtypeStruct((rows, width), FULL),
            jax.ShapeDtypeStruct((rows, 128), FULL),
            jax.ShapeDtypeStruct((rows, width), LOW),
        ],
        compiler_params=kernel_params(),
        cost_estimate=pl.CostEstimate(
            flops=2 * rows * width * 4 * width, bytes_accessed=20000000, transcendentals=0
        ),
        name="attend",
    )(own, got, embed, mixing_weight, output_weight, vectors)


def gelu_parts(value):
    size = jnp.abs(value) * math.sqrt(0.5)
    t = 1.0 / (1.0 + 0.3275911 * size)
    tail = t * (
        0.254829592 + t * (-0.284496736 + t * (1.421413741 + t * (-1.453152027 + t * 1.061405429)))
    )
    power = jnp.exp(-size * size)
    tail = 0.5 * tail * power
    return jnp.where(value < 0, tail, 1.0 - tail), power * (1.0 / math.sqrt(2.0 * math.pi))


STRIP = 512
LONG = 128
PART = 768
UNROLL = 1


def sum_eights(value):
    return jnp.sum(value.reshape(-1, 8, value.shape[-1]), axis=0)


def feed(norm_low, centred, widen_weight, widen_bias, narrow_weight, vectors, own_cot, got_cot,
         info, bounds, weights):
    rows, width = norm_low.shape
    pair, near, _ = own_cot.shape
    length = 2 * near
    inner = widen_weight.shape[1]
    chunk = width
    steps = inner // chunk

    def body(info_ref, bound_ref, weight_ref, norm_ref, centred_ref, wide_ref, wbias_ref, narrow_ref, vec_ref,
             own_ref, got_ref, act_ref, slope_ref, out_own_ref, out_away_ref, grad_ref, low_ref,
             sums_ref, pre_ref, total_ref):
        step = pl.program_id(0)
        pre_ref[...] = times(norm_ref[...], wide_ref[...])

        def strip(i, carry):
            row = pl.multiple_of(i * STRIP, STRIP)
            for c in range(0, chunk, PART):
                value = pre_ref[pl.ds(row, STRIP), c : c + PART] + wbias_ref[:, c : c + PART]
                below, density = gelu_parts(value)
                act_ref[pl.ds(row, STRIP), c : c + PART] = (value * below).astype(LOW)
                slope_ref[pl.ds(row, STRIP), c : c + PART] = (below + value * density).astype(LOW)
            return carry

        lax.fori_loop(0, rows // STRIP, strip, 0, unroll=UNROLL)
        product = times(act_ref[...], narrow_ref[...])

        @pl.when(step == 0)
        def _():
            total_ref[...] = product

        @pl.when(step > 0)
        def _():
            total_ref[...] += product

        @pl.when(step == steps - 1)
        def _():
            side = info_ref[SIDE]

            def vector(k):
                return vec_ref[k : k + 1, :]

            zero = jnp.zeros((8, width), FULL)
            sums = (zero, zero, zero)
            for quarter in range(2 * pair):
                sequence, far = quarter // 2, quarter % 2
                cot_ref = got_ref if far else own_ref
                back_ref = out_away_ref if far else out_own_ref
                bound = bound_ref[pair * side + sequence]
                weight = weight_ref[pair * side + sequence]
                start = jnp.where(side == far, 0, near)

                def finish(i, sums, quarter=quarter, sequence=sequence, cot_ref=cot_ref,
                           back_ref=back_ref, bound=bound, weight=weight, start=start):
                    inside = pl.multiple_of(i * LONG, LONG)
                    row = pl.multiple_of(quarter * near + i * LONG, LONG)
                    first_norm = (
                        centred_ref[pl.ds(row, LONG), :] * vector(FIRST_GAIN) + vector(FIRST_SHIFT)
                    )
                    total = first_norm + total_ref[pl.ds(row, LONG), :] + vector(NARROW_BIAS)
                    level = total - jnp.mean(total, axis=-1, keepdims=True)
                    inverse = lax.rsqrt(jnp.mean(level * level, axis=-1, keepdims=True) + epsilon)
                    level = level * inverse
                    back_ref[sequence, pl.ds(inside, LONG), :] = (
                        level * vector(SECOND_GAIN) + vector(SECOND_SHIFT)
                    ).astype(LOW)
                    place = start + inside + lax.broadcasted_iota(jnp.int32, (LONG, 1), 0)
                    factor = jnp.where(place >= bound, weight, 0.0)
                    upstream = cot_ref[sequence, pl.ds(inside, LONG), :].astype(FULL) * factor
                    gained = upstream * vector(SECOND_GAIN)
                    mean = jnp.mean(gained, axis=-1, keepdims=True)
                    along = jnp.mean(gained * level, axis=-1, keepdims=True)
                    grad = inverse * (gained - mean - level * along)
                    grad_ref[pl.ds(row, LONG), :] = grad
                    low_ref[pl.ds(row, LONG), :] = grad.astype(LOW)
                    return (
                        sums[0] + sum_eights(grad),
                        sums[1] + sum_eights(upstream * level),
                        sums[2] + sum_eights(upstream),
                    )

                sums = lax.fori_loop(0, near // LONG, finish, sums)
            sums_ref[...] = jnp.concatenate(
                [jnp.sum(v, axis=0, keepdims=True) for v in sums] + [jnp.zeros((5, width), FULL)],
                axis=0,
            )

    def whole(array):
        return pl.BlockSpec(array.shape, lambda s, *_: (0,) * array.ndim, pipeline_mode=ONE)

    def fixed(shape):
        return pl.BlockSpec(shape, lambda s, *_: (0,) * len(shape))

    by_columns = pl.BlockSpec((rows, chunk), lambda s, *_: (0, s))
    half = (pair, near, width)
    return pl.pallas_call(
        body,
        grid_spec=pltpu.PrefetchScalarGridSpec(
            num_scalar_prefetch=3,
            grid=(steps,),
            in_specs=[
                whole(norm_low),
                whole(centred),
                pl.BlockSpec((width, chunk), lambda s, *_: (0, s)),
                pl.BlockSpec((1, chunk), lambda s, *_: (0, s)),
                pl.BlockSpec((chunk, width), lambda s, *_: (s, 0)),
                whole(vectors),
                whole(own_cot),
                whole(got_cot),
            ],
            out_specs=[
                by_columns,
                by_columns,
                fixed(half),
                fixed(half),
                fixed((rows, width)),
                fixed((rows, width)),
                fixed((8, width)),
            ],
            scratch_shapes=[pltpu.VMEM((rows, chunk), FULL), pltpu.VMEM((rows, width), FULL)],
        ),
        out_shape=[
            jax.ShapeDtypeStruct((rows, inner), LOW),
            jax.ShapeDtypeStruct((rows, inner), LOW),
            jax.ShapeDtypeStruct(half, LOW),
            jax.ShapeDtypeStruct(half, LOW),
            jax.ShapeDtypeStruct((rows, width), FULL),
            jax.ShapeDtypeStruct((rows, width), LOW),
            jax.ShapeDtypeStruct((8, width), FULL),
        ],
        compiler_params=kernel_params(),
        cost_estimate=pl.CostEstimate(
            flops=4 * rows * width * inner, bytes_accessed=20000000, transcendentals=0
        ),
        name="feed",
    )(info, bounds, weights, norm_low, centred, widen_weight, widen_bias, narrow_weight, vectors,
      own_cot, got_cot)


def feed_back(shrink_low, second_grad, slope, centred, inverse, widen_weight, narrow_weight, vectors):
    rows, width = shrink_low.shape
    inner = slope.shape[1]
    chunk = width
    steps = inner // chunk

    def body(low_ref, grad_ref, slope_ref, centred_ref, inverse_ref, wide_ref, narrow_ref, vec_ref,
             pre_ref, bias_ref, first_ref, attn_ref, sums_ref, act_ref, total_ref):
        step = pl.program_id(0)
        act_ref[...] = times_turned(low_ref[...], narrow_ref[...])

        def strip(i, sums):
            row = pl.multiple_of(i * STRIP, STRIP)
            value = act_ref[pl.ds(row, STRIP), :] * slope_ref[pl.ds(row, STRIP), :].astype(FULL)
            pre_ref[pl.ds(row, STRIP), :] = value.astype(LOW)
            return sums + sum_eights(value)

        sums = lax.fori_loop(0, rows // STRIP, strip, jnp.zeros((8, chunk), FULL), unroll=UNROLL)
        bias_ref[...] = jnp.sum(sums, axis=0, keepdims=True)
        product = times_turned(pre_ref[...], wide_ref[...])

        @pl.when(step == 0)
        def _():
            total_ref[...] = product

        @pl.when(step > 0)
        def _():
            total_ref[...] += product

        @pl.when(step == steps - 1)
        def _():
            gain = vec_ref[FIRST_GAIN : FIRST_GAIN + 1, :]

            def finish(i, sums):
                row = pl.multiple_of(i * LONG, LONG)
                upstream = grad_ref[pl.ds(row, LONG), :] + total_ref[pl.ds(row, LONG), :]
                level = centred_ref[pl.ds(row, LONG), :]
                gained = upstream * gain
                mean = jnp.mean(gained, axis=-1, keepdims=True)
                along = jnp.mean(gained * level, axis=-1, keepdims=True)
                grad = inverse_ref[pl.ds(row, LONG), :1] * (gained - mean - level * along)
                first_ref[pl.ds(row, LONG), :] = grad
                attn_ref[pl.ds(row, LONG), :] = grad.astype(LOW)
                return (
                    sums[0] + sum_eights(grad),
                    sums[1] + sum_eights(upstream * level),
                    sums[2] + sum_eights(upstream),
                )

            zero = jnp.zeros((8, width), FULL)
            sums = lax.fori_loop(0, rows // LONG, finish, (zero, zero, zero))
            sums_ref[...] = jnp.concatenate(
                [jnp.sum(v, axis=0, keepdims=True) for v in sums] + [jnp.zeros((5, width), FULL)],
                axis=0,
            )

    def whole(array):
        return pl.BlockSpec(array.shape, lambda s: (0,) * array.ndim, pipeline_mode=ONE)

    def fixed(shape):
        return pl.BlockSpec(shape, lambda s: (0,) * len(shape))

    by_columns = pl.BlockSpec((rows, chunk), lambda s: (0, s))
    return pl.pallas_call(
        body,
        grid=(steps,),
        in_specs=[
            whole(shrink_low),
            whole(second_grad),
            by_columns,
            whole(centred),
            whole(inverse),
            pl.BlockSpec((width, chunk), lambda s: (0, s)),
            pl.BlockSpec((chunk, width), lambda s: (s, 0)),
            whole(vectors),
        ],
        out_specs=[
            by_columns,
            pl.BlockSpec((1, chunk), lambda s: (0, s)),
            fixed((rows, width)),
            fixed((rows, width)),
            fixed((8, width)),
        ],
        out_shape=[
            jax.ShapeDtypeStruct((rows, inner), LOW),
            jax.ShapeDtypeStruct((1, inner), FULL),
            jax.ShapeDtypeStruct((rows, width), FULL),
            jax.ShapeDtypeStruct((rows, width), LOW),
            jax.ShapeDtypeStruct((8, width), FULL),
        ],
        scratch_shapes=[pltpu.VMEM((rows, chunk), FULL), pltpu.VMEM((rows, width), FULL)],
        compiler_params=kernel_params(),
        cost_estimate=pl.CostEstimate(
            flops=4 * rows * width * inner, bytes_accessed=20000000, transcendentals=0
        ),
        name="feed_back",
    )(shrink_low, second_grad, slope, centred, inverse, widen_weight, narrow_weight, vectors)


def attend_back(attn_low, packed, probs, output_weight):
    pair, _, length, _ = probs.shape
    width = attn_low.shape[1]
    rows = attn_low.shape[0]
    scale = 1.0 / math.sqrt(HEAD)
    duo = 2 * HEAD

    def body(attn_ref, packed_ref, probs_ref, wout_ref, right_ref, sums_ref, context_ref):
        context_ref[...] = times_turned(attn_ref[...], wout_ref[...]).astype(LOW)
        masks = head_masks(1.0)
        lane = lax.broadcasted_iota(jnp.int32, (length, duo), 1)
        for j in range(width // duo):
            query = packed_ref[:, j * duo : (j + 1) * duo]
            key = packed_ref[:, width + j * duo : width + (j + 1) * duo]
            value = packed_ref[:, 2 * width + j * duo : 2 * width + (j + 1) * duo]
            upstream = context_ref[:, j * duo : (j + 1) * duo]
            parts = []
            for head in range(2):
                low = probs_ref[0, 2 * j + head]
                probs_full = low.astype(FULL)
                slope = times_turned(upstream * masks[head], value)
                dot = jnp.sum(probs_full * slope, axis=-1, keepdims=True)
                score = (probs_full * (slope - dot)).astype(LOW)
                parts.append(
                    (times(score, key), turned_times(score, query), turned_times(low, upstream))
                )
            first, second = parts
            query_grad = jnp.where(lane < HEAD, first[0], second[0]) * scale
            key_grad = jnp.where(lane < HEAD, first[1], second[1]) * scale
            value_grad = jnp.where(lane < HEAD, first[2], second[2])
            right_ref[:, j * duo : (j + 1) * duo] = query_grad.astype(LOW)
            right_ref[:, width + j * duo : width + (j + 1) * duo] = key_grad.astype(LOW)
            right_ref[:, 2 * width + j * duo : 2 * width + (j + 1) * duo] = value_grad.astype(LOW)
            sums_ref[0, 0:1, j * duo : (j + 1) * duo] = jnp.sum(query_grad, axis=0, keepdims=True)
            sums_ref[0, 1:2, j * duo : (j + 1) * duo] = jnp.sum(value_grad, axis=0, keepdims=True)
        right_ref[:, 3 * width :] = attn_ref[...]

    def by_rows(columns):
        return pl.BlockSpec((length, columns), lambda s: (s, 0))

    return pl.pallas_call(
        body,
        grid=(pair,),
        in_specs=[
            by_rows(width),
            by_rows(3 * width),
            pl.BlockSpec((1, HEADS, length, length), lambda s: (s, 0, 0, 0)),
            pl.BlockSpec(output_weight.shape, lambda s: (0, 0), pipeline_mode=ONE),
        ],
        out_specs=[by_rows(4 * width), pl.BlockSpec((1, 2, width), lambda s: (s, 0, 0))],
        out_shape=[
            jax.ShapeDtypeStruct((rows, 4 * width), LOW),
            jax.ShapeDtypeStruct((pair, 2, width), FULL),
        ],
        scratch_shapes=[pltpu.VMEM((length, width), LOW)],
        compiler_params=kernel_params(),
        cost_estimate=pl.CostEstimate(
            flops=2 * rows * width * 4 * width, bytes_accessed=10000000, transcendentals=0
        ),
        name="attend_back",
    )(attn_low, packed, probs, output_weight)


def hidden_back(right, first_grad, mixing_weight, pair):
    rows, width = first_grad.shape
    length = rows // pair
    near = length // 2

    def body(right_ref, grad_ref, mix_ref, own_ref, away_ref, total_ref):
        hidden = grad_ref[...] + times_turned(right_ref[...], mix_ref[...])
        low = hidden.astype(LOW)
        own_ref[0] = low[:near]
        away_ref[0] = low[near:]
        total_ref[0] = jnp.sum(hidden, axis=0, keepdims=True)

    half = pl.BlockSpec((1, near, width), lambda s: (s, 0, 0))
    return pl.pallas_call(
        body,
        grid=(pair,),
        in_specs=[
            pl.BlockSpec((length, 3 * width), lambda s: (s, 0)),
            pl.BlockSpec((length, width), lambda s: (s, 0)),
            pl.BlockSpec(mixing_weight.shape, lambda s: (0, 0), pipeline_mode=ONE),
        ],
        out_specs=[half, half, pl.BlockSpec((1, 1, width), lambda s: (s, 0, 0))],
        out_shape=[
            jax.ShapeDtypeStruct((pair, near, width), LOW),
            jax.ShapeDtypeStruct((pair, near, width), LOW),
            jax.ShapeDtypeStruct((pair, 1, width), FULL),
        ],
        compiler_params=kernel_params(),
        cost_estimate=pl.CostEstimate(
            flops=6 * rows * width * width, bytes_accessed=8000000, transcendentals=0
        ),
        name="hidden_back",
    )(right, first_grad, mixing_weight)


def pair_shards(
    tokens,
    timesteps,
    boundary,
    importance,
    cotangent,
    time_weight,
    time_bias,
    mixing_weight,
    query_bias,
    value_bias,
    output_weight,
    output_bias,
    first_gain,
    first_shift,
    widen_weight,
    widen_bias,
    narrow_weight,
    narrow_bias,
    second_gain,
    second_shift,
):
    near, group, width = tokens.shape
    pair = group // 2
    side = lax.axis_index("blk")
    info = device_info()

    away, own = split_rows(tokens, info)
    got = swap(away, "x")
    away_cot, own_cot = split_rows(cotangent, info)
    got_cot = swap(away_cot, "x")
    vectors = jnp.stack(
        [
            query_bias,
            value_bias,
            output_bias,
            first_gain,
            first_shift,
            narrow_bias,
            second_gain,
            second_shift,
        ]
    ).astype(FULL)
    time_code = sinusoid(
        lax.dynamic_slice_in_dim(timesteps, side * pair, pair, 0), time_weight.shape[0]
    ).astype(LOW)
    embed = jnp.dot(time_code, time_weight, preferred_element_type=FULL) + time_bias.astype(FULL)

    left, packed, probs, centred, inverse, norm_low = attend(
        own, got, embed[:, None], mixing_weight, output_weight, vectors
    )
    (act_low, slope, out_own, out_away, second_grad, shrink_low, sums_two) = feed(
        norm_low,
        centred,
        widen_weight,
        widen_bias.astype(FULL)[None],
        narrow_weight,
        vectors,
        own_cot,
        got_cot,
        info,
        boundary,
        importance,
    )
    shrink_of = (SHRINK_ORDERS, lambda t: t, lambda t: 0)
    expand_of = (EXPAND_ORDERS, lambda t: t % 3, lambda t: t // 3)
    mixing_of = (MIXING_ORDERS, lambda t: t % 3 + 3 * (t // 9), lambda t: t // 3)

    def send_half(left, right, of):
        return weight_half(left, right, info, *of)

    def keep_half(left, right, got, of):
        found = weight_half(left, right, info, *of, got=got)
        return found[:-1], found[-1]

    line = Order()
    shrink_send = line.run(partial(send_half, of=shrink_of), act_low, shrink_low)
    shrink_got = swap(shrink_send, "c")
    out_got = swap(out_away, "x")
    pre_low, expand_bias, first_grad, attn_low, sums_one = line.run(
        feed_back, shrink_low, second_grad, slope, centred, inverse, widen_weight, narrow_weight,
        vectors, token=4
    )
    uppers, lower = line.run(
        partial(keep_half, of=shrink_of), act_low, shrink_low, shrink_got, token=1
    )
    line.begin("S", flow(SHRINK_ORDERS, uppers, lower))
    expand_send = line.run(partial(send_half, of=expand_of), norm_low, pre_low)
    expand_got = swap(expand_send, "c")
    right, sums_zero = line.run(attend_back, attn_low, packed, probs, output_weight, token=1)
    line.advance("S")
    uppers, lower = line.run(
        partial(keep_half, of=expand_of), norm_low, pre_low, expand_got, token=1
    )
    line.begin("E", flow(EXPAND_ORDERS, uppers, lower))
    mixing_send = line.run(partial(send_half, of=mixing_of), left, right)
    mixing_got = swap(mixing_send, "c")
    line.advance("S")
    grad_own, grad_away, time_total = line.run(
        partial(hidden_back, pair=pair), right, first_grad, mixing_weight, token=2
    )
    grad_got = swap(grad_away, "x")
    uppers, lower = line.run(partial(keep_half, of=mixing_of), left, right, mixing_got, token=1)
    line.begin("M", flow(MIXING_ORDERS, uppers, lower))
    small = line.run(pack_small, sums_zero, sums_one, sums_two, expand_bias, time_total, time_code)
    line.begin("R", small_flow(small))
    results = {}
    widens = {
        "S": lambda near, far: widen_out(near, far, info, SHRINK_ORDERS, 0, 8, 1),
        "E": lambda near, far: widen_out(near, far, info, EXPAND_ORDERS, 0, 12, 4),
    }
    for name in SEQUENCE:
        if name == "o":
            output = line.run(partial(join_rows, info=info), out_own, out_got)
        elif name == "u":
            sums, time_weight_grad, time_bias_grad = line.run(
                partial(unpack_small, pair=pair, width=width, code_width=time_code.shape[1]),
                results["R"],
            )
        elif name == "i":
            input_grad = line.run(partial(join_rows, info=info), grad_own, grad_got)
        elif name in "SEMR":
            results[name] = line.advance(name)
        else:
            name = name.upper()
            results[name] = line.run(widens[name], *results[name])
    mixing_near, mixing_far = results["M"]
    return (
        output,
        input_grad,
        time_weight_grad,
        time_bias_grad[0],
        widen_out(mixing_near, mixing_far, info, MIXING_ORDERS, 0, 9, 3),
        sums[0],
        sums[1],
        widen_out(mixing_near, mixing_far, info, MIXING_ORDERS, 9, 3, 1),
        sums[2],
        sums[3],
        sums[4],
        results["E"],
        sums[8:12].reshape(-1),
        results["S"],
        sums[5],
        sums[6],
        sums[7],
    )


SEQUENCE = "ESoMESMRESMiESMRESMRESMsEMREReuM"


def solution(mesh):
    pairs = mesh.shape["blk"] == 2 and mesh.shape["dp"] == 16
    return jax.shard_map(
        pair_shards if pairs else general_shards,
        mesh=mesh,
        in_specs=(
            P("blk", "dp", None),
            P("dp"),
            P("dp"),
            P("dp"),
            P("blk", "dp", None),
            P(),
            P(),
            P(),
            P(),
            P(),
            P(),
            P(),
            P(),
            P(),
            P(),
            P(),
            P(),
            P(),
            P(),
            P(),
        ),
        out_specs=(
            P("blk", "dp", None),
            P("blk", "dp", None),
            P(),
            P(),
            P(),
            P(),
            P(),
            P(),
            P(),
            P(),
            P(),
            P(),
            P(),
            P(),
            P(),
            P(),
            P(),
        ),
        check_vma=False,
    )
```

```python
from functools import partial
import math
from types import SimpleNamespace

import jax
import jax.numpy as jnp
from jax import lax
from jax.experimental import pallas as pl
from jax.experimental.pallas import tpu as pltpu
from jax.sharding import PartitionSpec as P

HEADS = 12
HEAD = 64


epsilon = 1e-05


def sinusoid(step_ids, code_width):
    half_width = code_width // 2
    frequency = jnp.exp(-math.log(10000.0) * jnp.arange(half_width, dtype=jnp.float32) / half_width)
    angles = step_ids.astype(jnp.float32)[:, None] * frequency[None, :]
    return jnp.concatenate([jnp.cos(angles), jnp.sin(angles)], axis=-1)


def layer_norm(inputs, norm_gain, norm_shift):
    centred = inputs - jnp.mean(inputs, axis=-1, keepdims=True)
    variance = jnp.mean(centred * centred, axis=-1, keepdims=True)
    return centred * lax.rsqrt(variance + epsilon) * norm_gain + norm_shift


def reduce_dp(parts):
    shares = (
        lax.psum_scatter(
            parts[0].astype(jnp.bfloat16), "dp", scatter_dimension=1, tiled=True
        ).astype(jnp.float32),
        lax.psum_scatter(
            parts[1].astype(jnp.bfloat16), "dp", scatter_dimension=0, tiled=True
        ).astype(jnp.float32),
        lax.psum_scatter(
            parts[2].astype(jnp.bfloat16), "dp", scatter_dimension=0, tiled=True
        ).astype(jnp.float32),
        lax.psum_scatter(
            parts[3].astype(jnp.bfloat16), "dp", scatter_dimension=0, tiled=True
        ).astype(jnp.float32),
        lax.psum_scatter(
            parts[4].astype(jnp.bfloat16), "dp", scatter_dimension=0, tiled=True
        ).astype(jnp.float32),
        lax.psum_scatter(
            parts[5].astype(jnp.bfloat16), "dp", scatter_dimension=0, tiled=True
        ).astype(jnp.float32),
        lax.psum_scatter(
            parts[6].astype(jnp.bfloat16), "dp", scatter_dimension=0, tiled=True
        ).astype(jnp.float32),
        lax.psum_scatter(
            parts[7].astype(jnp.bfloat16), "dp", scatter_dimension=0, tiled=True
        ).astype(jnp.float32),
        lax.psum_scatter(
            parts[8].astype(jnp.bfloat16), "dp", scatter_dimension=0, tiled=True
        ).astype(jnp.float32),
        lax.psum_scatter(
            parts[9].astype(jnp.bfloat16), "dp", scatter_dimension=0, tiled=True
        ).astype(jnp.float32),
        lax.psum_scatter(
            parts[10].astype(jnp.bfloat16), "dp", scatter_dimension=0, tiled=True
        ).astype(jnp.float32),
        lax.psum_scatter(
            parts[11].astype(jnp.bfloat16), "dp", scatter_dimension=0, tiled=True
        ).astype(jnp.float32),
        lax.psum_scatter(
            parts[12].astype(jnp.bfloat16), "dp", scatter_dimension=0, tiled=True
        ).astype(jnp.float32),
        lax.psum_scatter(
            parts[13].astype(jnp.bfloat16), "dp", scatter_dimension=0, tiled=True
        ).astype(jnp.float32),
        lax.psum_scatter(
            parts[14].astype(jnp.bfloat16), "dp", scatter_dimension=0, tiled=True
        ).astype(jnp.float32),
    )
    summed = (
        lax.psum(shares[0].astype(jnp.bfloat16), "blk").astype(jnp.float32),
        lax.psum(shares[1].astype(jnp.bfloat16), "blk").astype(jnp.float32),
        lax.psum(shares[2].astype(jnp.bfloat16), "blk").astype(jnp.float32),
        lax.psum(shares[3].astype(jnp.bfloat16), "blk").astype(jnp.float32),
        lax.psum(shares[4].astype(jnp.bfloat16), "blk").astype(jnp.float32),
        lax.psum(shares[5].astype(jnp.bfloat16), "blk").astype(jnp.float32),
        lax.psum(shares[6].astype(jnp.bfloat16), "blk").astype(jnp.float32),
        lax.psum(shares[7].astype(jnp.bfloat16), "blk").astype(jnp.float32),
        lax.psum(shares[8].astype(jnp.bfloat16), "blk").astype(jnp.float32),
        lax.psum(shares[9].astype(jnp.bfloat16), "blk").astype(jnp.float32),
        lax.psum(shares[10].astype(jnp.bfloat16), "blk").astype(jnp.float32),
        lax.psum(shares[11].astype(jnp.bfloat16), "blk").astype(jnp.float32),
        lax.psum(shares[12].astype(jnp.bfloat16), "blk").astype(jnp.float32),
        lax.psum(shares[13].astype(jnp.bfloat16), "blk").astype(jnp.float32),
        lax.psum(shares[14].astype(jnp.bfloat16), "blk").astype(jnp.float32),
    )
    return (
        lax.all_gather(summed[0].astype(jnp.bfloat16), "dp", axis=1, tiled=True).astype(
            jnp.float32
        ),
        lax.all_gather(summed[1].astype(jnp.bfloat16), "dp", axis=0, tiled=True).astype(
            jnp.float32
        ),
        lax.all_gather(summed[2].astype(jnp.bfloat16), "dp", axis=0, tiled=True).astype(
            jnp.float32
        ),
        lax.all_gather(summed[3].astype(jnp.bfloat16), "dp", axis=0, tiled=True).astype(
            jnp.float32
        ),
        lax.all_gather(summed[4].astype(jnp.bfloat16), "dp", axis=0, tiled=True).astype(
            jnp.float32
        ),
        lax.all_gather(summed[5].astype(jnp.bfloat16), "dp", axis=0, tiled=True).astype(
            jnp.float32
        ),
        lax.all_gather(summed[6].astype(jnp.bfloat16), "dp", axis=0, tiled=True).astype(
            jnp.float32
        ),
        lax.all_gather(summed[7].astype(jnp.bfloat16), "dp", axis=0, tiled=True).astype(
            jnp.float32
        ),
        lax.all_gather(summed[8].astype(jnp.bfloat16), "dp", axis=0, tiled=True).astype(
            jnp.float32
        ),
        lax.all_gather(summed[9].astype(jnp.bfloat16), "dp", axis=0, tiled=True).astype(
            jnp.float32
        ),
        lax.all_gather(summed[10].astype(jnp.bfloat16), "dp", axis=0, tiled=True).astype(
            jnp.float32
        ),
        lax.all_gather(summed[11].astype(jnp.bfloat16), "dp", axis=0, tiled=True).astype(
            jnp.float32
        ),
        lax.all_gather(summed[12].astype(jnp.bfloat16), "dp", axis=0, tiled=True).astype(
            jnp.float32
        ),
        lax.all_gather(summed[13].astype(jnp.bfloat16), "dp", axis=0, tiled=True).astype(
            jnp.float32
        ),
        lax.all_gather(summed[14].astype(jnp.bfloat16), "dp", axis=0, tiled=True).astype(
            jnp.float32
        ),
    )


def general_shards(
    tokens,
    timesteps,
    boundary,
    importance,
    cotangent,
    time_weight,
    time_bias,
    mixing_weight,
    query_bias,
    value_bias,
    output_weight,
    output_bias,
    first_gain,
    first_shift,
    widen_weight,
    widen_bias,
    narrow_weight,
    narrow_bias,
    second_gain,
    second_shift,
):
    model_width = tokens.shape[2]
    score_scale = 1.0 / math.sqrt(HEAD)
    inputs, upstream = (tokens, cotangent)
    step_ids, bounds, weights = (timesteps, boundary, importance)
    offset = lax.axis_index("blk") * tokens.shape[0]
    row_count = inputs.shape[0]
    group_count = inputs.shape[1]
    time_code = sinusoid(step_ids, time_weight.shape[0]).astype(jnp.bfloat16)
    time_embed = jnp.dot(
        time_code, time_weight, preferred_element_type=jnp.float32
    ) + time_bias.astype(jnp.float32)
    hidden = inputs.astype(jnp.float32) + time_embed[None]
    hidden_low = hidden.astype(jnp.bfloat16)
    bias_pack = jnp.concatenate(
        [
            query_bias.astype(jnp.float32),
            jnp.zeros((model_width,), jnp.float32),
            value_bias.astype(jnp.float32),
        ]
    )
    packed = (
        jnp.einsum("lsd,de->lse", hidden_low, mixing_weight, preferred_element_type=jnp.float32)
        + bias_pack
    ).astype(jnp.bfloat16)
    queries = packed[..., :model_width].reshape(row_count, group_count, HEADS, HEAD)
    keys_values = packed[..., model_width:]
    both_all = lax.all_gather(keys_values, "blk", axis=0, tiled=True)
    total_rows = both_all.shape[0]
    keys_all = both_all[..., :model_width].reshape(total_rows, group_count, HEADS, HEAD)
    values_all = both_all[..., model_width:].reshape(total_rows, group_count, HEADS, HEAD)
    scores = (
        jnp.einsum("qshe,kshe->shqk", queries, keys_all, preferred_element_type=jnp.float32)
        * score_scale
    )
    row_peak = jnp.max(scores, axis=-1, keepdims=True)
    powered = jnp.exp(scores - row_peak)
    totals_soft = jnp.sum(powered, axis=-1, keepdims=True)
    probs_low = (powered / totals_soft).astype(jnp.bfloat16)
    log_total = row_peak + jnp.log(totals_soft)
    context = jnp.einsum(
        "shqk,kshe->qshe", probs_low, values_all, preferred_element_type=jnp.float32
    )
    context_low = context.reshape(row_count, group_count, model_width).astype(jnp.bfloat16)
    gain_one = first_gain.astype(jnp.float32)
    shift_one = first_shift.astype(jnp.float32)
    gain_two = second_gain.astype(jnp.float32)
    shift_two = second_shift.astype(jnp.float32)
    first_sum = (
        hidden
        + jnp.einsum("lsd,de->lse", context_low, output_weight, preferred_element_type=jnp.float32)
        + output_bias.astype(jnp.float32)
    )
    leading_norm, first_back = jax.vjp(layer_norm, first_sum, gain_one, shift_one)
    norm_reduced = leading_norm.astype(jnp.bfloat16)
    before_activation = jnp.einsum(
        "ikg,gv->ikv", norm_reduced, widen_weight, preferred_element_type=jnp.float32
    ) + widen_bias.astype(jnp.float32)
    activated, gelu_back = jax.vjp(partial(jax.nn.gelu, approximate=False), before_activation)
    activation_reduced = activated.astype(jnp.bfloat16)
    residual_sum = (
        leading_norm
        + jnp.einsum(
            "ema,aw->emw", activation_reduced, narrow_weight, preferred_element_type=jnp.float32
        )
        + narrow_bias.astype(jnp.float32)
    )
    out_full, second_back = jax.vjp(layer_norm, residual_sum, gain_two, shift_two)
    output = out_full.astype(jnp.bfloat16)
    positions = jnp.arange(row_count, dtype=jnp.int32) + offset
    row_weight = jnp.where(positions[:, None] >= bounds[None, :], weights[None, :], 0.0)
    out_grad = upstream.astype(jnp.float32) * row_weight[:, :, None]
    second_grad, second_gain_grad, second_shift_grad = second_back(out_grad)
    shrink_bias_grad = jnp.sum(second_grad, axis=(0, 1))
    narrow_reduced = second_grad.astype(jnp.bfloat16)
    shrink_weight_grad = jnp.einsum(
        "egk,egy->ky", activation_reduced, narrow_reduced, preferred_element_type=jnp.float32
    )
    act_grad = jnp.einsum(
        "ztv,ov->zto", narrow_reduced, narrow_weight, preferred_element_type=jnp.float32
    )
    pre_grad = gelu_back(act_grad)[0]
    expand_bias_grad = jnp.sum(pre_grad, axis=(0, 1))
    before_reduced = pre_grad.astype(jnp.bfloat16)
    expand_weight_grad = jnp.einsum(
        "thk,thr->kr", norm_reduced, before_reduced, preferred_element_type=jnp.float32
    )
    norm_grad = second_grad + jnp.einsum(
        "xcu,pu->xcp", before_reduced, widen_weight, preferred_element_type=jnp.float32
    )
    first_grad, first_gain_grad, first_shift_grad = first_back(norm_grad)
    output_bias_grad = jnp.sum(first_grad, axis=(0, 1))
    attn_low = first_grad.astype(jnp.bfloat16)
    output_weight_grad = jnp.einsum(
        "lsd,lse->de", context_low, attn_low, preferred_element_type=jnp.float32
    )
    context_grad = jnp.einsum(
        "lse,de->lsd", attn_low, output_weight, preferred_element_type=jnp.float32
    )
    context_grad = context_grad.astype(jnp.bfloat16).reshape(row_count, group_count, HEADS, HEAD)
    again = (
        jnp.einsum("qshe,kshe->shqk", queries, keys_all, preferred_element_type=jnp.float32)
        * score_scale
    )
    soft_probs = jnp.exp(again - log_total)
    prob_grad = jnp.einsum(
        "qshe,kshe->shqk", context_grad, values_all, preferred_element_type=jnp.float32
    )
    row_dot = jnp.sum(soft_probs * prob_grad, axis=-1, keepdims=True)
    score_low = (soft_probs * (prob_grad - row_dot)).astype(jnp.bfloat16)
    query_grad = (
        jnp.einsum("shqk,kshe->qshe", score_low, keys_all, preferred_element_type=jnp.float32)
        * score_scale
    )
    query_every, cgrad_every = (
        lax.all_gather(queries, "blk", axis=0, tiled=True),
        lax.all_gather(context_grad, "blk", axis=0, tiled=True),
    )
    total_every, dot_every = (
        lax.all_gather(log_total, "blk", axis=2, tiled=True),
        lax.all_gather(row_dot, "blk", axis=2, tiled=True),
    )
    own_keys = packed[..., model_width : 2 * model_width].reshape(
        row_count, group_count, HEADS, HEAD
    )
    own_values = packed[..., 2 * model_width :].reshape(row_count, group_count, HEADS, HEAD)
    local_scores = (
        jnp.einsum("qshe,kshe->shqk", query_every, own_keys, preferred_element_type=jnp.float32)
        * score_scale
    )
    local_probs = jnp.exp(local_scores - total_every)
    local_low = local_probs.astype(jnp.bfloat16)
    local_grad = jnp.einsum(
        "qshe,kshe->shqk", cgrad_every, own_values, preferred_element_type=jnp.float32
    )
    local_score_low = (local_probs * (local_grad - dot_every)).astype(jnp.bfloat16)
    value_own = jnp.einsum(
        "shqk,qshe->kshe", local_low, cgrad_every, preferred_element_type=jnp.float32
    )
    key_own = (
        jnp.einsum(
            "shqk,qshe->kshe", local_score_low, query_every, preferred_element_type=jnp.float32
        )
        * score_scale
    )
    key_here = jnp.concatenate(
        [
            key_own.reshape(row_count, group_count, model_width),
            value_own.reshape(row_count, group_count, model_width),
        ],
        axis=-1,
    )
    packed_grad = jnp.concatenate(
        [query_grad.reshape(row_count, group_count, model_width), key_here], axis=-1
    )
    query_bias_grad = jnp.sum(packed_grad[..., :model_width], axis=(0, 1))
    value_bias_grad = jnp.sum(packed_grad[..., 2 * model_width :], axis=(0, 1))
    packed_low = packed_grad.astype(jnp.bfloat16)
    mixing_weight_grad = jnp.einsum(
        "lsd,lse->de", hidden_low, packed_low, preferred_element_type=jnp.float32
    )
    hidden_grad = first_grad + jnp.einsum(
        "lse,de->lsd", packed_low, mixing_weight, preferred_element_type=jnp.float32
    )
    input_grad = hidden_grad.astype(jnp.bfloat16)
    time_total = jnp.sum(hidden_grad, axis=0)
    time_bias_grad = jnp.sum(time_total, axis=0)
    time_weight_grad = jnp.dot(
        time_code.astype(jnp.float32).T, time_total, precision=lax.Precision.HIGHEST
    )
    parts = (
        time_weight_grad,
        time_bias_grad,
        mixing_weight_grad,
        query_bias_grad,
        value_bias_grad,
        output_weight_grad,
        output_bias_grad,
        first_gain_grad,
        first_shift_grad,
        expand_weight_grad,
        expand_bias_grad,
        shrink_weight_grad,
        shrink_bias_grad,
        second_gain_grad,
        second_shift_grad,
    )
    summed = reduce_dp(parts)
    return (
        output,
        input_grad,
        summed[0],
        summed[1],
        summed[2],
        summed[3],
        summed[4],
        summed[5],
        summed[6],
        summed[7],
        summed[8],
        summed[9],
        summed[10],
        summed[11],
        summed[12],
        summed[13],
        summed[14],
    )


LOW = jnp.bfloat16
FULL = jnp.float32
PLACES = {"c": ("dp", 1), "y": ("dp", 2), "z": ("dp", 4), "w": ("dp", 8), "x": ("blk", 1)}
SHRINK_ORDERS = (("zxy", "xyz"),)
EXPAND_ORDERS = (("zxy", "xyz"),)
MIXING_ORDERS = (("xyz", "yxz"), ("yzx", "zyx"))
ALL_ORDERS = tuple(dict.fromkeys(SHRINK_ORDERS + EXPAND_ORDERS + MIXING_ORDERS))
CORE, SIDE, NUMBERS = 0, 1, 2
WIDTH = 768
GRAD_ROWS = 3072


def swap(value, places):
    count = {axis: lax.axis_size(axis) for axis in ("dp", "blk")}
    pairs = []
    for group in range(count["dp"]):
        for side in range(count["blk"]):
            axis, bit = PLACES[places[group % 2 if len(places) == 2 else 0]]
            there = (group ^ bit, side) if axis == "dp" else (group, side ^ bit)
            pairs.append((group * count["blk"] + side, there[0] * count["blk"] + there[1]))
    return lax.ppermute(value, ("dp", "blk"), pairs)


def place_bit(place):
    axis, bit = PLACES[place]
    return (lax.axis_index(axis) // bit) % 2


def device_info():
    core = place_bit("c")
    own, other = [], []
    for orders in ALL_ORDERS:
        both = []
        for order in orders:
            number = 0
            for place in order:
                number = number * 2 + place_bit(place)
            both.append(number)
        own.append(jnp.where(core == 0, both[0], both[1]))
        other.append(jnp.where(core == 0, both[1], both[0]))
    return jnp.stack([core, lax.axis_index("blk")] + own + other).astype(jnp.int32)


def order_number(info_ref, orders, unit, mine):
    places = [NUMBERS + ALL_ORDERS.index(o) + (0 if mine else len(ALL_ORDERS)) for o in orders]
    number = info_ref[places[0]]
    for k in range(1, len(orders)):
        number = jnp.where(unit == k, info_ref[places[k]], number)
    return number


def weight_half(left, right, info, orders, left_of, right_of, got=None):
    units = len(orders)
    block = GRAD_ROWS // units // 16
    tile_rows = 4 * block
    mine = got is not None

    def body(info_ref, left_ref, right_ref, *refs):
        core = info_ref[CORE]
        side = core if mine else 1 - core
        for step in range(2 * units):
            unit, part = step // 2, step % 2
            tile = 4 * unit + 2 * side + part
            number = order_number(info_ref, orders, unit, mine)
            column = pl.multiple_of(left_of(tile) * tile_rows, 128)
            place = pl.multiple_of(right_of(tile) * WIDTH, 128)
            product = turned_times(
                left_ref[:, pl.ds(column, tile_rows)], right_ref[:, pl.ds(place, WIDTH)]
            )
            spots = [((4 * part + i) ^ number) & 7 for i in range(4)]
            rows = [pl.multiple_of((8 * unit + spot) * block, 16) for spot in spots]
            pieces = [product[i * block : (i + 1) * block, :] for i in range(4)]
            if not mine:
                for row, piece in zip(rows, pieces):
                    refs[0][pl.ds(row, block), :] = piece.astype(LOW)
                continue
            got_ref, upper_ref, lower_ref = refs[0], refs[1 + unit], refs[-1]
            pieces = [
                (piece + got_ref[pl.ds(row, block), :].astype(FULL)).astype(LOW)
                for row, piece in zip(rows, pieces)
            ]
            upper = part ^ ((number // 4) % 2)

            @pl.when(upper == 0)
            def _(pieces=pieces, spots=spots, lower_ref=lower_ref, unit=unit):
                for spot, piece in zip(spots, pieces):
                    row = pl.multiple_of((4 * unit + (spot & 3)) * block, 16)
                    lower_ref[pl.ds(row, block), :] = piece

            @pl.when(upper == 1)
            def _(pieces=pieces, spots=spots, upper_ref=upper_ref):
                for spot, piece in zip(spots, pieces):
                    row = pl.multiple_of((spot & 3) * block, 16)
                    upper_ref[pl.ds(row, block), :] = piece

    rows = left.shape[0]
    counts = [4 * block] * units + [4 * units * block] if mine else [8 * units * block]
    vmem = pl.BlockSpec(memory_space=pltpu.VMEM)
    found = pl.pallas_call(
        body,
        in_specs=[pl.BlockSpec(memory_space=pltpu.SMEM)] + [vmem] * (3 if mine else 2),
        out_specs=[vmem] * len(counts),
        out_shape=[jax.ShapeDtypeStruct((c, WIDTH), LOW) for c in counts],
        compiler_params=kernel_params(),
        cost_estimate=cost(2.8),
    )(info, left, right, *([got] if mine else []))
    return found if mine else found[0]


def widen_out(near, far, info, orders, first_tile, tile_count, columns):
    units = len(orders)
    block = GRAD_ROWS // units // 16
    part = 64 if block % 64 == 0 else block
    tall = 4 * block * tile_count // columns
    pieces = 4 if columns == 1 else 1
    start = 4 * first_tile * block

    def body(info_ref, near_ref, far_ref, out_ref):
        step = pl.program_id(0)
        for column in range(columns):
            for piece in range(pieces):
                first = start + column * tall + (step * pieces + piece) * part
                index = first // block
                unit = index // 16
                own = (index % 16) // 8 == info_ref[CORE]
                rows = []
                for mine in (True, False):
                    number = order_number(info_ref, orders, unit, mine)
                    row = (unit * 8 + ((index ^ number) & 7)) * block + first % block
                    rows.append(pl.multiple_of(row, 16))
                near_row, far_row = rows
                target = (
                    slice(piece * part, (piece + 1) * part),
                    slice(column * WIDTH, (column + 1) * WIDTH),
                )

                @pl.when(own)
                def _(row=near_row, target=target):
                    out_ref[target] = near_ref[pl.ds(row, part), :].astype(FULL)

                @pl.when(jnp.logical_not(own))
                def _(row=far_row, target=target):
                    out_ref[target] = far_ref[pl.ds(row, part), :].astype(FULL)

    whole = pl.BlockSpec(near.shape, lambda t, p: (0, 0), pipeline_mode=ONE)
    return pl.pallas_call(
        body,
        grid_spec=pltpu.PrefetchScalarGridSpec(
            num_scalar_prefetch=1,
            grid=(tall // (pieces * part),),
            in_specs=[whole, whole],
            out_specs=pl.BlockSpec((pieces * part, columns * WIDTH), lambda t, p: (t, 0)),
        ),
        out_shape=jax.ShapeDtypeStruct((tall, columns * WIDTH), FULL),
        compiler_params=kernel_params(),
        cost_estimate=cost(6.0, 60),
    )(info, near, far)


def widen_half(source, info, orders, mine, base=None):
    units = len(orders)
    block = GRAD_ROWS // units // 16
    count = 8 * units

    def body(info_ref, source_ref, *refs):
        mix_ref, out_ref, stage_ref, sems = refs[-4:]
        core = info_ref[CORE]
        half = core if mine else 1 - core
        moves = []
        for k in range(count):
            unit, spot = k // 8, k % 8
            number = order_number(info_ref, orders, unit, mine)
            first = (16 * unit + 8 * half + (spot ^ (number & 7))) * block
            matrix = first // WIDTH
            row = pl.multiple_of(first % WIDTH, 16)
            column = pl.multiple_of(jnp.minimum(matrix, 2) * WIDTH, 128)
            here = slice(k * block, (k + 1) * block)
            stage_ref[here, :] = source_ref[here, :].astype(FULL)
            mixed = pltpu.make_async_copy(
                stage_ref.at[here, :],
                mix_ref.at[pl.ds(row, block), pl.ds(column, WIDTH)],
                sems.at[k],
            )
            output = pltpu.make_async_copy(
                stage_ref.at[here, :], out_ref.at[pl.ds(row, block), :], sems.at[k]
            )
            moves.append((matrix, mixed, output))
            pl.when(matrix < 3)(mixed.start)
            pl.when(matrix >= 3)(output.start)
        for matrix, mixed, output in moves:
            pl.when(matrix < 3)(mixed.wait)
            pl.when(matrix >= 3)(output.wait)

    hbm = pl.BlockSpec(memory_space=pltpu.HBM)
    operands = [info, source] + ([] if base is None else list(base))
    return pl.pallas_call(
        body,
        in_specs=[
            pl.BlockSpec(memory_space=pltpu.SMEM),
            pl.BlockSpec(memory_space=pltpu.VMEM),
        ]
        + [hbm] * (len(operands) - 2),
        out_specs=[hbm, hbm],
        out_shape=[
            jax.ShapeDtypeStruct((WIDTH, 3 * WIDTH), FULL),
            jax.ShapeDtypeStruct((WIDTH, WIDTH), FULL),
        ],
        scratch_shapes=[
            pltpu.VMEM((count * block, WIDTH), FULL),
            pltpu.SemaphoreType.DMA((count,)),
        ],
        input_output_aliases={} if base is None else {2: 0, 3: 1},
        compiler_params=kernel_params(),
        cost_estimate=cost(3.0, 30),
    )(*operands)


def combine(outputs):
    arrays = []

    def number(array):
        for k, known in enumerate(arrays):
            if known is array:
                return k
        arrays.append(array)
        return len(arrays) - 1

    plan = [
        [[(number(array), row, rows) for array, row, rows in piece] for piece in pieces]
        for pieces in outputs
    ]
    heights = [sum(piece[0][2] for piece in pieces) for pieces in outputs]

    def body(*refs):
        sources, targets = refs[: len(arrays)], refs[len(arrays) :]
        for pieces, target in zip(plan, targets):
            place = 0
            for piece in pieces:
                rows = piece[0][2]
                for first in range(0, rows, 128):
                    count = min(128, rows - first)
                    values = [sources[k][row + first : row + first + count, :] for k, row, _ in piece]
                    total = values[0] if len(values) == 1 else values[0] + values[1]
                    target[place + first : place + first + count, :] = total
                place += rows

    vmem = pl.BlockSpec(memory_space=pltpu.VMEM)
    return pl.pallas_call(
        body,
        in_specs=[vmem] * len(arrays),
        out_specs=[vmem] * len(outputs),
        out_shape=[jax.ShapeDtypeStruct((h, WIDTH), LOW) for h in heights],
        compiler_params=kernel_params(),
        cost_estimate=cost(0.4, 12),
    )(*arrays)


class Rider:
    def __init__(self, packed):
        self.packed = packed
        self.filled = 1

    def rows(self):
        return self.packed.shape[0]

    def pieces(self):
        return [((self.packed, 0, self.rows()),)]

    def take(self, got, row):
        packed, rows, filled = self.packed, self.rows(), self.filled
        if filled >= RIDER_LANES:
            (self.packed,) = combine(
                [
                    [
                        ((packed, 0, 16), (got, row, 16)),
                        ((packed, 16, rows - 16),),
                        ((got, row + 16, rows - 16),),
                    ]
                ]
            )
            return

        def body(packed_ref, got_ref, out_ref):
            out_ref[:16, :] = packed_ref[:16, :] + got_ref[row : row + 16, :]
            out_ref[16:, : filled * 128] = packed_ref[16:, : filled * 128]
            out_ref[16:, filled * 128 : 2 * filled * 128] = got_ref[
                row + 16 : row + 32, : filled * 128
            ]
            out_ref[16:, 2 * filled * 128 :] = packed_ref[16:, 2 * filled * 128 :]

        vmem = pl.BlockSpec(memory_space=pltpu.VMEM)
        self.packed = pl.pallas_call(
            body,
            in_specs=[vmem, vmem],
            out_specs=vmem,
            out_shape=jax.ShapeDtypeStruct(packed.shape, LOW),
            compiler_params=kernel_params(),
            cost_estimate=cost(0.4),
            name="ride",
        )(packed, got)
        self.filled = 2 * filled


def flow(orders, uppers, lower, rider=None):
    units = len(orders)
    size = lower.shape[0] // units
    mine = [(lower, k * size, size) for k in range(units)]

    def cut(view, part):
        array, row, rows = view
        return array, row + part * rows // 2, rows // 2

    def places_at(level):
        return [first[level] + second[level] for first, second in orders]

    got = yield list(zip(places_at(0), uppers))
    for level in (1, 2):
        views = [(g, 0, size) for g in got]
        away = [[(cut(m, 1), cut(v, 1))] for m, v in zip(mine, views)]
        kept = [(cut(m, 0), cut(v, 0)) for m, v in zip(mine, views)]
        size = size // 2
        *sends, rest = combine(away + [kept])
        mine = [(rest, k * size, size) for k in range(units)]
        got = yield list(zip(places_at(level), sends))

    rider = None if rider is None else rider()

    def riding():
        return [] if rider is None else rider.pieces()

    (joined,) = combine([[(m, (g, 0, size)) for m, g in zip(mine, got)] + riding()])
    (other,) = yield [("w", joined)]
    values = combine([[((joined, k * size, size), (other, k * size, size))] for k in range(units)])
    if rider is not None:
        rider.take(other, units * size)
    for level in (2, 1, 0):
        sends = list(values)
        if rider is not None:
            (sends[0],) = combine([[((values[0], 0, size),)] + rider.pieces()])
        got = yield list(zip(places_at(level), sends))
        if rider is not None:
            rider.take(got[0], size)
        pieces = [[((v, 0, size),), ((g, 0, size),)] for v, g in zip(values, got)]
        size = 2 * size
        if level > 0:
            values = combine(pieces)
    (near,) = combine([sum(pieces, []) + riding()])
    (far,) = yield [("c", near)]
    if rider is not None:
        rider.take(far, units * size)
    return near, far


RIDER_LANES = 4


def pack_small(sums_zero, sums_one, sums_two, expand_bias, time_total, time_code):
    pair, code_width = time_code.shape
    width = sums_one.shape[1]
    blocks = width // 128

    def body(zero_ref, one_ref, two_ref, bias_ref, total_ref, code_ref, out_ref):
        bias = [bias_ref[:, k * width : (k + 1) * width] for k in range(4)]
        out_ref[:16, :] = jnp.concatenate(
            [zero_ref[0] + zero_ref[1], one_ref[:3, :], two_ref[:3, :]]
            + bias
            + [jnp.zeros((4, width), FULL)],
            axis=0,
        ).astype(LOW)
        totals = [
            total_ref[s, :, 128 * j : 128 * j + 128] for s in range(pair) for j in range(blocks)
        ]
        codes = code_ref[...].astype(FULL)
        out_ref[16:, :] = jnp.zeros((16, width), LOW)
        out_ref[16:, :128] = jnp.concatenate(
            totals + [codes, jnp.zeros((16 - pair * (blocks + 1), 128), FULL)], axis=0
        ).astype(LOW)

    return pl.pallas_call(
        body,
        out_shape=jax.ShapeDtypeStruct((32, width), LOW),
        compiler_params=kernel_params(),
        cost_estimate=cost(0.6),
    )(sums_zero, sums_one, sums_two, expand_bias, time_total, time_code)


def unpack_small(packed, pair, code_width):
    count, width = packed.shape
    blocks = width // 128
    groups = (count - 16) // 16

    def body(packed_ref, sums_ref, weight_ref, bias_ref, wide_ref):
        sums_ref[...] = packed_ref[:16, :].astype(FULL)
        for lane in range(RIDER_LANES):
            wide_ref[lane] = packed_ref[16:, 128 * lane : 128 * lane + 128].astype(FULL)

        def every(row):
            return jnp.concatenate(
                [wide_ref[lane, pl.ds(row, groups, stride=16), :] for lane in range(RIDER_LANES)],
                axis=0,
            )

        codes = [every(pair * blocks + s).astype(LOW) for s in range(pair)]
        for j in range(blocks):
            columns = slice(128 * j, 128 * j + 128)
            totals = [every(s * blocks + j) for s in range(pair)]
            weight_ref[:, columns] = sum(
                turned_times(c, t.astype(LOW)) for c, t in zip(codes, totals)
            )
            bias_ref[:, columns] = jnp.sum(sum(totals), axis=0, keepdims=True)

    return pl.pallas_call(
        body,
        out_shape=[
            jax.ShapeDtypeStruct((16, width), FULL),
            jax.ShapeDtypeStruct((code_width, width), FULL),
            jax.ShapeDtypeStruct((1, width), FULL),
        ],
        scratch_shapes=[pltpu.VMEM((RIDER_LANES, count - 16, 128), FULL)],
        compiler_params=kernel_params(),
        cost_estimate=cost(1.0),
    )(packed)


class Order:
    def __init__(self):
        self.token = None
        self.flows = {}
        self.sent = {}

    def after(self, *values):
        if self.token is None:
            return values
        return lax.optimization_barrier((self.token,) + tuple(values))[1:]

    def run(self, function, *values, token=0):
        found = function(*self.after(*values))
        self.token = found[token] if isinstance(found, (tuple, list)) else found
        return found

    def begin(self, name, steps):
        pairs = next(steps)
        self.flows[name] = steps, [swap(value, place) for place, value in pairs]

    def advance(self, name):
        steps, got = self.flows[name]
        try:
            pairs = steps.send(list(self.after(*got)))
        except StopIteration as stop:
            return stop.value
        self.token = pairs[0][1]
        self.sent[name] = pairs[0][1]
        self.flows[name] = steps, [swap(value, place) for place, value in pairs]
        return None


VMEM_LIMIT = 8 * 1024 * 1024
ONE = pl.Buffered(1)
SCALE = 600000000


def cost(microseconds, megabytes=0):
    return pl.CostEstimate(
        flops=int(microseconds * SCALE),
        bytes_accessed=1 + int(megabytes * 1000000),
        transcendentals=0,
    )


def kernel_params():
    return pltpu.CompilerParams(vmem_limit_bytes=VMEM_LIMIT)


def times(left, right):
    return jnp.dot(left, right, preferred_element_type=FULL)


def times_turned(left, right):
    return lax.dot_general(left, right, (((1,), (1,)), ((), ())), preferred_element_type=FULL)


def turned_times(left, right):
    return lax.dot_general(left, right, (((0,), (0,)), ((), ())), preferred_element_type=FULL)


def split_rows(values, info):
    near, group, width = values.shape
    pair = group // 2
    count = near * group

    def body(info_ref, values_ref, away_ref, own_ref):
        side = info_ref[SIDE]
        rows = values_ref[...].reshape(count, width)
        row = lax.broadcasted_iota(jnp.int32, (count, count), 0)
        column = lax.broadcasted_iota(jnp.int32, (count, count), 1)
        half = pair * near
        first = jnp.where(row < half, pair * (1 - side), pair * side)
        place = jnp.where(row < half, row, row - half)
        source = (place % near) * group + first + place // near
        pick = (source == column).astype(FULL).astype(LOW)
        moved = times(pick, rows).astype(LOW)
        away_ref[...] = moved[:half].reshape(pair, near, width)
        own_ref[...] = moved[half:].reshape(pair, near, width)

    shape = jax.ShapeDtypeStruct((pair, near, width), values.dtype)
    return pl.pallas_call(
        body,
        in_specs=[
            pl.BlockSpec(memory_space=pltpu.SMEM),
            pl.BlockSpec(memory_space=pltpu.VMEM),
        ],
        out_shape=[shape, shape],
        compiler_params=kernel_params(),
        cost_estimate=cost(16.0),
    )(info, values)


def lay_out(vectors, weights, after):
    count = len(weights)

    def body(*refs):
        refs[-1][...] = refs[0][...]

    vmem = pl.BlockSpec(memory_space=pltpu.VMEM)
    return pl.pallas_call(
        body,
        in_specs=[vmem] * (1 + count) + [pl.BlockSpec(memory_space=pl.ANY)],
        out_specs=vmem,
        out_shape=jax.ShapeDtypeStruct(vectors.shape, vectors.dtype),
        compiler_params=kernel_params(),
        cost_estimate=cost(8.0, 60),
    )(vectors, *weights, after)


def join_rows(own, got, info):
    pair, near, width = own.shape
    group = 2 * pair
    count = near * group

    def body(info_ref, own_ref, got_ref, out_ref):
        side = info_ref[SIDE]
        row = lax.broadcasted_iota(jnp.int32, (count, count), 0)
        column = lax.broadcasted_iota(jnp.int32, (count, count), 1)
        half = pair * near
        sequence = row % group
        position = row // group
        from_own = sequence // pair == side
        source = jnp.where(from_own, 0, half) + (sequence % pair) * near + position
        pick = (source == column).astype(FULL).astype(LOW)
        rows = jnp.concatenate(
            [own_ref[...].reshape(half, width), got_ref[...].reshape(half, width)], axis=0
        )
        out_ref[...] = times(pick, rows).astype(LOW).reshape(near, group, width)

    return pl.pallas_call(
        body,
        in_specs=[
            pl.BlockSpec(memory_space=pltpu.SMEM),
            pl.BlockSpec(memory_space=pltpu.VMEM),
            pl.BlockSpec(memory_space=pltpu.VMEM),
        ],
        out_shape=jax.ShapeDtypeStruct((near, group, width), own.dtype),
        compiler_params=kernel_params(),
        cost_estimate=cost(2.0),
    )(info, own, got)


QUERY_BIAS, VALUE_BIAS, OUTPUT_BIAS, FIRST_GAIN, FIRST_SHIFT = range(5)
NARROW_BIAS, SECOND_GAIN, SECOND_SHIFT = range(5, 8)


def head_masks(scale):
    lane = lax.broadcasted_iota(jnp.int32, (1, 2 * HEAD), 1)
    first = jnp.where(lane < HEAD, scale, 0.0).astype(LOW)
    second = jnp.where(lane < HEAD, 0.0, scale).astype(LOW)
    return first, second


def attend(own, got, embed, mixing_weight, output_weight, vectors):
    pair, near, width = own.shape
    length = 2 * near
    scale = 1.0 / math.sqrt(HEAD)
    duo = 2 * HEAD

    def body(own_ref, got_ref, embed_ref, mix_ref, wout_ref, vec_ref, left_ref, packed_ref,
             probs_ref, centred_ref, scale_ref, norm_ref):
        for s in range(pair):
            here = slice(s * length, (s + 1) * length)
            hidden = jnp.concatenate([own_ref[s], got_ref[s]], axis=0).astype(FULL) + embed_ref[s]
            hidden_low = hidden.astype(LOW)
            left_ref[here, :width] = hidden_low
            for part, bias in ((0, QUERY_BIAS), (1, None), (2, VALUE_BIAS)):
                columns = slice(part * width, (part + 1) * width)
                product = times(hidden_low, mix_ref[:, columns])
                if bias is not None:
                    product = product + vec_ref[bias : bias + 1, :]
                packed_ref[here, columns] = product.astype(LOW)
            masks = head_masks(scale)
            lane = lax.broadcasted_iota(jnp.int32, (length, duo), 1)
            for j in range(width // duo):
                query = packed_ref[here, j * duo : (j + 1) * duo]
                key = packed_ref[here, width + j * duo : width + (j + 1) * duo]
                value = packed_ref[here, 2 * width + j * duo : 2 * width + (j + 1) * duo]
                found = []
                for head in range(2):
                    scores = times_turned(query * masks[head], key)
                    peak = jnp.max(scores, axis=-1, keepdims=True)
                    powered = jnp.exp(scores - peak)
                    total = jnp.sum(powered, axis=-1, keepdims=True)
                    low = (powered * (1.0 / total)).astype(LOW)
                    probs_ref[s, 2 * j + head] = low
                    found.append(times(low, value))
                left_ref[here, width + j * duo : width + (j + 1) * duo] = jnp.where(
                    lane < HEAD, found[0], found[1]
                ).astype(LOW)
            first_sum = (
                hidden
                + times(left_ref[here, width:], wout_ref[...])
                + vec_ref[OUTPUT_BIAS : OUTPUT_BIAS + 1, :]
            )
            centred = first_sum - jnp.mean(first_sum, axis=-1, keepdims=True)
            variance = jnp.mean(centred * centred, axis=-1, keepdims=True)
            inverse = lax.rsqrt(variance + epsilon)
            centred = centred * inverse
            centred_ref[here, :] = centred
            scale_ref[here, :] = jnp.broadcast_to(inverse, (length, 128))
            norm_ref[here, :] = (
                centred * vec_ref[FIRST_GAIN : FIRST_GAIN + 1, :]
                + vec_ref[FIRST_SHIFT : FIRST_SHIFT + 1, :]
            ).astype(LOW)

    rows = pair * length
    vmem = pl.BlockSpec(memory_space=pltpu.VMEM)
    return pl.pallas_call(
        body,
        in_specs=[vmem] * 6,
        out_specs=[vmem] * 6,
        out_shape=[
            jax.ShapeDtypeStruct((rows, 2 * width), LOW),
            jax.ShapeDtypeStruct((rows, 3 * width), LOW),
            jax.ShapeDtypeStruct((pair, HEADS, length, length), LOW),
            jax.ShapeDtypeStruct((rows, width), FULL),
            jax.ShapeDtypeStruct((rows, 128), FULL),
            jax.ShapeDtypeStruct((rows, width), LOW),
        ],
        compiler_params=kernel_params(),
        cost_estimate=cost(25.0),
    )(own, got, embed, mixing_weight, output_weight, vectors)


def gelu_parts(value):
    t = 1.0 / (1.0 + (0.3275911 * math.sqrt(0.5)) * jnp.abs(value))
    series = (0.254829592, -0.284496736, 1.421413741, -1.453152027, 1.061405429)
    tail = jnp.full_like(value, 0.5 * series[-1])
    for factor in series[-2::-1]:
        tail = tail * t + 0.5 * factor
    power = jnp.exp(-0.5 * value * value)
    tail = tail * t * power
    return jnp.where(value < 0, tail, 1.0 - tail), power * (1.0 / math.sqrt(2.0 * math.pi))


STRIP = 512
LONG = 128
PART = 768
BACK_PART = 768
UNROLL = 1


def sum_eights(value):
    return jnp.sum(value.reshape(-1, 8, value.shape[-1]), axis=0)


def feed(norm_low, centred, widen_weight, widen_bias, narrow_weight, vectors, own_cot, got_cot,
         info, bounds, weights):
    rows, width = norm_low.shape
    pair, near, _ = own_cot.shape
    length = 2 * near
    inner = widen_weight.shape[1]

    def body(info_ref, bound_ref, weight_ref, norm_ref, centred_ref, wide_ref, wbias_ref, narrow_ref, vec_ref,
             own_ref, got_ref, act_ref, slope_ref, out_own_ref, out_away_ref, grad_ref, low_ref,
             sums_ref, total_ref):
        def widen(k, carry):
            columns = pl.ds(pl.multiple_of(k * PART, 128), PART)
            value = times(norm_ref[...], wide_ref[:, columns]) + wbias_ref[:, columns]
            below, density = gelu_parts(value)
            act_ref[:, columns] = (value * below).astype(LOW)
            slope_ref[:, columns] = (below + value * density).astype(LOW)
            return carry

        lax.fori_loop(0, inner // PART, widen, 0)
        total_ref[...] = times(act_ref[...], narrow_ref[...])
        side = info_ref[SIDE]

        def vector(k):
            return vec_ref[k : k + 1, :]

        zero = jnp.zeros((8, width), FULL)
        sums = (zero, zero, zero)
        for quarter in range(2 * pair):
            sequence, far = quarter // 2, quarter % 2
            cot_ref = got_ref if far else own_ref
            back_ref = out_away_ref if far else out_own_ref
            bound = bound_ref[pair * side + sequence]
            weight = weight_ref[pair * side + sequence]
            start = jnp.where(side == far, 0, near)

            def finish(i, sums, quarter=quarter, sequence=sequence, cot_ref=cot_ref,
                       back_ref=back_ref, bound=bound, weight=weight, start=start):
                inside = pl.multiple_of(i * LONG, LONG)
                row = pl.multiple_of(quarter * near + i * LONG, LONG)
                first_norm = (
                    centred_ref[pl.ds(row, LONG), :] * vector(FIRST_GAIN) + vector(FIRST_SHIFT)
                )
                total = first_norm + total_ref[pl.ds(row, LONG), :] + vector(NARROW_BIAS)
                level = total - jnp.mean(total, axis=-1, keepdims=True)
                inverse = lax.rsqrt(jnp.mean(level * level, axis=-1, keepdims=True) + epsilon)
                level = level * inverse
                back_ref[sequence, pl.ds(inside, LONG), :] = (
                    level * vector(SECOND_GAIN) + vector(SECOND_SHIFT)
                ).astype(LOW)
                place = start + inside + lax.broadcasted_iota(jnp.int32, (LONG, 1), 0)
                factor = jnp.where(place >= bound, weight, 0.0)
                upstream = cot_ref[sequence, pl.ds(inside, LONG), :].astype(FULL) * factor
                gained = upstream * vector(SECOND_GAIN)
                mean = jnp.mean(gained, axis=-1, keepdims=True)
                along = jnp.mean(gained * level, axis=-1, keepdims=True)
                grad = inverse * (gained - mean - level * along)
                grad_ref[pl.ds(row, LONG), :] = grad
                low_ref[pl.ds(row, LONG), :] = grad.astype(LOW)
                return (
                    sums[0] + sum_eights(grad),
                    sums[1] + sum_eights(upstream * level),
                    sums[2] + sum_eights(upstream),
                )

            sums = lax.fori_loop(0, near // LONG, finish, sums)
        sums_ref[...] = jnp.concatenate(
            [jnp.sum(v, axis=0, keepdims=True) for v in sums] + [jnp.zeros((5, width), FULL)],
            axis=0,
        )

    half = (pair, near, width)
    smem = pl.BlockSpec(memory_space=pltpu.SMEM)
    vmem = pl.BlockSpec(memory_space=pltpu.VMEM)
    return pl.pallas_call(
        body,
        in_specs=[smem] * 3 + [vmem] * 8,
        out_specs=[vmem] * 7,
        scratch_shapes=[pltpu.VMEM((rows, width), FULL)],
        out_shape=[
            jax.ShapeDtypeStruct((rows, inner), LOW),
            jax.ShapeDtypeStruct((rows, inner), LOW),
            jax.ShapeDtypeStruct(half, LOW),
            jax.ShapeDtypeStruct(half, LOW),
            jax.ShapeDtypeStruct((rows, width), FULL),
            jax.ShapeDtypeStruct((rows, width), LOW),
            jax.ShapeDtypeStruct((8, width), FULL),
        ],
        compiler_params=kernel_params(),
        cost_estimate=cost(40.0),
    )(info, bounds, weights, norm_low, centred, widen_weight, widen_bias, narrow_weight, vectors,
      own_cot, got_cot)


def feed_back(shrink_low, second_grad, slope, centred, inverse, widen_weight, narrow_weight, vectors):
    rows, width = shrink_low.shape
    inner = slope.shape[1]

    def body(low_ref, grad_ref, slope_ref, centred_ref, inverse_ref, wide_ref, narrow_ref, vec_ref,
             pre_ref, bias_ref, first_ref, attn_ref, sums_ref, total_ref):
        total = None
        for c in range(0, inner, BACK_PART):
            columns = slice(c, c + BACK_PART)
            value = times_turned(low_ref[...], narrow_ref[columns, :])
            value = value * slope_ref[:, columns].astype(FULL)
            low = value.astype(LOW)
            pre_ref[:, columns] = low
            bias_ref[:, columns] = jnp.sum(sum_eights(value), axis=0, keepdims=True)
            term = times_turned(low, wide_ref[:, columns])
            total = term if total is None else total + term
        total_ref[...] = total
        gain = vec_ref[FIRST_GAIN : FIRST_GAIN + 1, :]

        def finish(i, sums):
            row = pl.multiple_of(i * LONG, LONG)
            upstream = grad_ref[pl.ds(row, LONG), :] + total_ref[pl.ds(row, LONG), :]
            level = centred_ref[pl.ds(row, LONG), :]
            gained = upstream * gain
            mean = jnp.mean(gained, axis=-1, keepdims=True)
            along = jnp.mean(gained * level, axis=-1, keepdims=True)
            grad = inverse_ref[pl.ds(row, LONG), :1] * (gained - mean - level * along)
            first_ref[pl.ds(row, LONG), :] = grad
            attn_ref[pl.ds(row, LONG), :] = grad.astype(LOW)
            return (
                sums[0] + sum_eights(grad),
                sums[1] + sum_eights(upstream * level),
                sums[2] + sum_eights(upstream),
            )

        zero = jnp.zeros((8, width), FULL)
        sums = lax.fori_loop(0, rows // LONG, finish, (zero, zero, zero))
        sums_ref[...] = jnp.concatenate(
            [jnp.sum(v, axis=0, keepdims=True) for v in sums] + [jnp.zeros((5, width), FULL)],
            axis=0,
        )

    vmem = pl.BlockSpec(memory_space=pltpu.VMEM)
    return pl.pallas_call(
        body,
        in_specs=[vmem] * 8,
        out_specs=[vmem] * 5,
        out_shape=[
            jax.ShapeDtypeStruct((rows, inner), LOW),
            jax.ShapeDtypeStruct((1, inner), FULL),
            jax.ShapeDtypeStruct((rows, width), FULL),
            jax.ShapeDtypeStruct((rows, width), LOW),
            jax.ShapeDtypeStruct((8, width), FULL),
        ],
        scratch_shapes=[pltpu.VMEM((rows, width), FULL)],
        compiler_params=kernel_params(),
        cost_estimate=cost(8.6),
    )(shrink_low, second_grad, slope, centred, inverse, widen_weight, narrow_weight, vectors)


def attend_back(attn_low, packed, probs, output_weight):
    pair, _, length, _ = probs.shape
    width = attn_low.shape[1]
    rows = attn_low.shape[0]
    scale = 1.0 / math.sqrt(HEAD)
    duo = 2 * HEAD

    def body(attn_ref, packed_ref, probs_ref, wout_ref, right_ref, sums_ref, context_ref):
        for s in range(pair):
            here = slice(s * length, (s + 1) * length)
            context_ref[...] = times_turned(attn_ref[here, :], wout_ref[...]).astype(LOW)
            masks = head_masks(1.0)
            lane = lax.broadcasted_iota(jnp.int32, (length, duo), 1)
            for j in range(width // duo):
                query = packed_ref[here, j * duo : (j + 1) * duo]
                key = packed_ref[here, width + j * duo : width + (j + 1) * duo]
                value = packed_ref[here, 2 * width + j * duo : 2 * width + (j + 1) * duo]
                upstream = context_ref[:, j * duo : (j + 1) * duo]
                parts = []
                for head in range(2):
                    low = probs_ref[s, 2 * j + head]
                    probs_full = low.astype(FULL)
                    slope = times_turned(upstream * masks[head], value)
                    dot = jnp.sum(probs_full * slope, axis=-1, keepdims=True)
                    score = (probs_full * (slope - dot)).astype(LOW)
                    parts.append(
                        (times(score, key), turned_times(score, query), turned_times(low, upstream))
                    )
                first, second = parts
                query_grad = jnp.where(lane < HEAD, first[0], second[0]) * scale
                key_grad = jnp.where(lane < HEAD, first[1], second[1]) * scale
                value_grad = jnp.where(lane < HEAD, first[2], second[2])
                right_ref[here, j * duo : (j + 1) * duo] = query_grad.astype(LOW)
                right_ref[here, width + j * duo : width + (j + 1) * duo] = key_grad.astype(LOW)
                right_ref[here, 2 * width + j * duo : 2 * width + (j + 1) * duo] = value_grad.astype(LOW)
                sums_ref[s, 0:1, j * duo : (j + 1) * duo] = jnp.sum(query_grad, axis=0, keepdims=True)
                sums_ref[s, 1:2, j * duo : (j + 1) * duo] = jnp.sum(value_grad, axis=0, keepdims=True)
            right_ref[here, 3 * width :] = attn_ref[here, :]

    vmem = pl.BlockSpec(memory_space=pltpu.VMEM)
    return pl.pallas_call(
        body,
        in_specs=[vmem] * 4,
        out_specs=[vmem] * 2,
        out_shape=[
            jax.ShapeDtypeStruct((rows, 4 * width), LOW),
            jax.ShapeDtypeStruct((pair, 2, width), FULL),
        ],
        scratch_shapes=[pltpu.VMEM((length, width), LOW)],
        compiler_params=kernel_params(),
        cost_estimate=cost(10),
    )(attn_low, packed, probs, output_weight)


def hidden_back(right, first_grad, mixing_weight, pair):
    rows, width = first_grad.shape
    length = rows // pair
    near = length // 2

    def body(right_ref, grad_ref, mix_ref, own_ref, away_ref, total_ref):
        for s in range(pair):
            here = slice(s * length, (s + 1) * length)
            hidden = grad_ref[here, :] + times_turned(right_ref[here, : 3 * width], mix_ref[...])
            low = hidden.astype(LOW)
            own_ref[s] = low[:near]
            away_ref[s] = low[near:]
            total_ref[s] = jnp.sum(hidden, axis=0, keepdims=True)

    vmem = pl.BlockSpec(memory_space=pltpu.VMEM)
    return pl.pallas_call(
        body,
        in_specs=[vmem] * 3,
        out_specs=[vmem] * 3,
        out_shape=[
            jax.ShapeDtypeStruct((pair, near, width), LOW),
            jax.ShapeDtypeStruct((pair, near, width), LOW),
            jax.ShapeDtypeStruct((pair, 1, width), FULL),
        ],
        compiler_params=kernel_params(),
        cost_estimate=cost(2.5),
    )(right, first_grad, mixing_weight)


(
    S_SEND, FEED_BACK, S_KEEP, E_SEND, E_KEEP, ATTEND_BACK, M_SEND, HIDDEN_BACK, M_KEEP, OUT_GOT,
    GRAD_GOT, OUT_JOIN, GRAD_JOIN, M_NEAR, UNPACK, S_WIDEN, E_WIDEN, S, E, M,
) = range(20)


def pair_shards(
    tokens,
    timesteps,
    boundary,
    importance,
    cotangent,
    time_weight,
    time_bias,
    mixing_weight,
    query_bias,
    value_bias,
    output_weight,
    output_bias,
    first_gain,
    first_shift,
    widen_weight,
    widen_bias,
    narrow_weight,
    narrow_bias,
    second_gain,
    second_shift,
):
    near, group, width = tokens.shape
    pair = group // 2
    side = lax.axis_index("blk")
    info = device_info()

    away, own = split_rows(tokens, info)
    got = swap(away, "x")
    away_cot, own_cot = split_rows(cotangent, info)
    got_cot = swap(away_cot, "x")
    vectors = jnp.stack(
        [
            query_bias,
            value_bias,
            output_bias,
            first_gain,
            first_shift,
            narrow_bias,
            second_gain,
            second_shift,
        ]
    ).astype(FULL)
    time_code = sinusoid(
        lax.dynamic_slice_in_dim(timesteps, side * pair, pair, 0), time_weight.shape[0]
    ).astype(LOW)
    embed = jnp.dot(time_code, time_weight, preferred_element_type=FULL) + time_bias.astype(FULL)

    vectors = lay_out(
        vectors, (mixing_weight, output_weight, widen_weight, narrow_weight), away_cot
    )
    left, packed, probs, centred, inverse, norm_low = attend(
        own, got, embed[:, None], mixing_weight, output_weight, vectors
    )
    (act_low, slope, out_own, out_away, second_grad, shrink_low, sums_two) = feed(
        norm_low,
        centred,
        widen_weight,
        widen_bias.astype(FULL)[None],
        narrow_weight,
        vectors,
        own_cot,
        got_cot,
        info,
        boundary,
        importance,
    )
    expand_tall, mixing_tall = len(EXPAND_ORDERS), len(MIXING_ORDERS)
    shrink_of = (SHRINK_ORDERS, lambda t: t, lambda t: 0)
    expand_of = (EXPAND_ORDERS, lambda t: t % expand_tall, lambda t: t // expand_tall)
    mixing_of = (
        MIXING_ORDERS,
        lambda t: t % mixing_tall + mixing_tall * (t // (3 * mixing_tall)),
        lambda t: t // mixing_tall,
    )

    def send_half(left, right, of):
        return weight_half(left, right, info, *of)

    def keep_half(left, right, got, of):
        found = weight_half(left, right, info, *of, got=got)
        return found[:-1], found[-1]

    line = Order()
    v = SimpleNamespace()
    done = {}

    def event(name):
        if name == S_SEND:
            v.s_away = line.run(partial(send_half, of=shrink_of), act_low, shrink_low)
            v.s_got = swap(v.s_away, "c")
            v.out_got = swap(out_away, "x")
        elif name == FEED_BACK:
            v.pre_low, v.expand_bias, v.first_grad, v.attn_low, v.sums_one = line.run(
                    feed_back, shrink_low, second_grad, slope, centred, inverse, widen_weight,
                    narrow_weight, vectors, token=4
                )
        elif name == S_KEEP:
            found = line.run(
                partial(keep_half, of=shrink_of), act_low, shrink_low, v.s_got, token=1
            )
            line.begin(S, flow(SHRINK_ORDERS, *found))
        elif name == E_SEND:
            v.e_away = line.run(partial(send_half, of=expand_of), norm_low, v.pre_low)
            v.e_got = swap(v.e_away, "c")
        elif name == E_KEEP:
            found = line.run(
                partial(keep_half, of=expand_of), norm_low, v.pre_low, v.e_got, token=1
            )
            line.begin(E, flow(EXPAND_ORDERS, *found[:-1], found[-1], lambda: v.rider))
        elif name == ATTEND_BACK:
            v.right, v.sums_zero = line.run(attend_back, v.attn_low, packed, probs, output_weight, token=1)
        elif name == M_SEND:
            v.m_away = line.run(partial(send_half, of=mixing_of), left, v.right)
            v.m_got = swap(v.m_away, "c")
        elif name == HIDDEN_BACK:
            v.grad_own, v.grad_away, v.time_total = line.run(
                    partial(hidden_back, pair=pair), v.right, v.first_grad, mixing_weight,
                    token=2
                )
            v.grad_got = swap(v.grad_away, "x")
            v.rider = Rider(
                line.run(
                    pack_small, v.sums_zero, v.sums_one, sums_two, v.expand_bias,
                    v.time_total, time_code
                )
            )
        elif name == M_KEEP:
            found = line.run(
                partial(keep_half, of=mixing_of), left, v.right, v.m_got, token=1
            )
            line.begin(M, flow(MIXING_ORDERS, *found))
        elif name == OUT_GOT:
            (v.out_got,) = line.after(v.out_got)
            line.token = v.out_got
        elif name == GRAD_GOT:
            (v.grad_got,) = line.after(v.grad_got)
            line.token = v.grad_got
        elif name == OUT_JOIN:
            v.output = line.run(partial(join_rows, info=info), out_own, v.out_got)
        elif name == GRAD_JOIN:
            v.input_grad = line.run(partial(join_rows, info=info), v.grad_own, v.grad_got)
        elif name == M_NEAR:
            v.mixed = line.run(
                lambda near: widen_half(near, info, MIXING_ORDERS, True), line.sent[M]
            )
        elif name == UNPACK:
            v.small = line.run(
                partial(unpack_small, pair=pair, code_width=time_code.shape[1]), v.rider.packed
            )
        elif name == S_WIDEN:
            v.shrink = line.run(
                lambda near, far: widen_out(near, far, info, SHRINK_ORDERS, 0, 4 * len(SHRINK_ORDERS), 1),
                *done[S]
            )
        elif name == E_WIDEN:
            v.expand = line.run(
                lambda near, far: widen_out(near, far, info, EXPAND_ORDERS, 0, 4 * expand_tall, 4),
                *done[E]
            )
        else:
            done[name] = line.advance(name)

    for name in SEQUENCE:
        event(name)
    sums, time_weight_grad, time_bias_grad = v.small
    mixing_grad, output_grad = widen_half(
        done[M][1], info, MIXING_ORDERS, False, v.mixed
    )
    return (
        v.output,
        v.input_grad,
        time_weight_grad,
        time_bias_grad[0],
        mixing_grad,
        sums[0],
        sums[1],
        output_grad,
        sums[2],
        sums[3],
        sums[4],
        v.expand,
        sums[8:12].reshape(-1),
        v.shrink,
        sums[5],
        sums[6],
        sums[7],
    )


SEQUENCE = (
    S_SEND, FEED_BACK, S_KEEP, OUT_GOT, ATTEND_BACK, E_SEND, S, M_SEND, E_KEEP, HIDDEN_BACK, S,
    M_KEEP, S, E, M, S, E, S, M, E, GRAD_GOT, S, M, E, E, M, OUT_JOIN, M, E, S, GRAD_JOIN, S,
    S_WIDEN, M, E, E, UNPACK, E_WIDEN, M, M_NEAR, M,
)


def solution(mesh):
    pairs = mesh.shape["blk"] == 2 and mesh.shape["dp"] == 16
    return jax.shard_map(
        pair_shards if pairs else general_shards,
        mesh=mesh,
        in_specs=(
            P("blk", "dp", None),
            P("dp"),
            P("dp"),
            P("dp"),
            P("blk", "dp", None),
            P(),
            P(),
            P(),
            P(),
            P(),
            P(),
            P(),
            P(),
            P(),
            P(),
            P(),
            P(),
            P(),
            P(),
            P(),
        ),
        out_specs=(
            P("blk", "dp", None),
            P("blk", "dp", None),
            P(),
            P(),
            P(),
            P(),
            P(),
            P(),
            P(),
            P(),
            P(),
            P(),
            P(),
            P(),
            P(),
            P(),
            P(),
        ),
        check_vma=False,
    )
```

```python
from functools import partial
import math
from types import SimpleNamespace

import jax
import jax.numpy as jnp
from jax import lax
from jax.experimental import pallas as pl
from jax.experimental.pallas import tpu as pltpu
from jax.sharding import PartitionSpec as P

HEADS = 12
HEAD = 64


epsilon = 1e-05


def sinusoid(step_ids, code_width):
    half_width = code_width // 2
    frequency = jnp.exp(-math.log(10000.0) * jnp.arange(half_width, dtype=jnp.float32) / half_width)
    angles = step_ids.astype(jnp.float32)[:, None] * frequency[None, :]
    return jnp.concatenate([jnp.cos(angles), jnp.sin(angles)], axis=-1)


def layer_norm(inputs, norm_gain, norm_shift):
    centred = inputs - jnp.mean(inputs, axis=-1, keepdims=True)
    variance = jnp.mean(centred * centred, axis=-1, keepdims=True)
    return centred * lax.rsqrt(variance + epsilon) * norm_gain + norm_shift


def reduce_dp(parts):
    shares = (
        lax.psum_scatter(
            parts[0].astype(jnp.bfloat16), "dp", scatter_dimension=1, tiled=True
        ).astype(jnp.float32),
        lax.psum_scatter(
            parts[1].astype(jnp.bfloat16), "dp", scatter_dimension=0, tiled=True
        ).astype(jnp.float32),
        lax.psum_scatter(
            parts[2].astype(jnp.bfloat16), "dp", scatter_dimension=0, tiled=True
        ).astype(jnp.float32),
        lax.psum_scatter(
            parts[3].astype(jnp.bfloat16), "dp", scatter_dimension=0, tiled=True
        ).astype(jnp.float32),
        lax.psum_scatter(
            parts[4].astype(jnp.bfloat16), "dp", scatter_dimension=0, tiled=True
        ).astype(jnp.float32),
        lax.psum_scatter(
            parts[5].astype(jnp.bfloat16), "dp", scatter_dimension=0, tiled=True
        ).astype(jnp.float32),
        lax.psum_scatter(
            parts[6].astype(jnp.bfloat16), "dp", scatter_dimension=0, tiled=True
        ).astype(jnp.float32),
        lax.psum_scatter(
            parts[7].astype(jnp.bfloat16), "dp", scatter_dimension=0, tiled=True
        ).astype(jnp.float32),
        lax.psum_scatter(
            parts[8].astype(jnp.bfloat16), "dp", scatter_dimension=0, tiled=True
        ).astype(jnp.float32),
        lax.psum_scatter(
            parts[9].astype(jnp.bfloat16), "dp", scatter_dimension=0, tiled=True
        ).astype(jnp.float32),
        lax.psum_scatter(
            parts[10].astype(jnp.bfloat16), "dp", scatter_dimension=0, tiled=True
        ).astype(jnp.float32),
        lax.psum_scatter(
            parts[11].astype(jnp.bfloat16), "dp", scatter_dimension=0, tiled=True
        ).astype(jnp.float32),
        lax.psum_scatter(
            parts[12].astype(jnp.bfloat16), "dp", scatter_dimension=0, tiled=True
        ).astype(jnp.float32),
        lax.psum_scatter(
            parts[13].astype(jnp.bfloat16), "dp", scatter_dimension=0, tiled=True
        ).astype(jnp.float32),
        lax.psum_scatter(
            parts[14].astype(jnp.bfloat16), "dp", scatter_dimension=0, tiled=True
        ).astype(jnp.float32),
    )
    summed = (
        lax.psum(shares[0].astype(jnp.bfloat16), "blk").astype(jnp.float32),
        lax.psum(shares[1].astype(jnp.bfloat16), "blk").astype(jnp.float32),
        lax.psum(shares[2].astype(jnp.bfloat16), "blk").astype(jnp.float32),
        lax.psum(shares[3].astype(jnp.bfloat16), "blk").astype(jnp.float32),
        lax.psum(shares[4].astype(jnp.bfloat16), "blk").astype(jnp.float32),
        lax.psum(shares[5].astype(jnp.bfloat16), "blk").astype(jnp.float32),
        lax.psum(shares[6].astype(jnp.bfloat16), "blk").astype(jnp.float32),
        lax.psum(shares[7].astype(jnp.bfloat16), "blk").astype(jnp.float32),
        lax.psum(shares[8].astype(jnp.bfloat16), "blk").astype(jnp.float32),
        lax.psum(shares[9].astype(jnp.bfloat16), "blk").astype(jnp.float32),
        lax.psum(shares[10].astype(jnp.bfloat16), "blk").astype(jnp.float32),
        lax.psum(shares[11].astype(jnp.bfloat16), "blk").astype(jnp.float32),
        lax.psum(shares[12].astype(jnp.bfloat16), "blk").astype(jnp.float32),
        lax.psum(shares[13].astype(jnp.bfloat16), "blk").astype(jnp.float32),
        lax.psum(shares[14].astype(jnp.bfloat16), "blk").astype(jnp.float32),
    )
    return (
        lax.all_gather(summed[0].astype(jnp.bfloat16), "dp", axis=1, tiled=True).astype(
            jnp.float32
        ),
        lax.all_gather(summed[1].astype(jnp.bfloat16), "dp", axis=0, tiled=True).astype(
            jnp.float32
        ),
        lax.all_gather(summed[2].astype(jnp.bfloat16), "dp", axis=0, tiled=True).astype(
            jnp.float32
        ),
        lax.all_gather(summed[3].astype(jnp.bfloat16), "dp", axis=0, tiled=True).astype(
            jnp.float32
        ),
        lax.all_gather(summed[4].astype(jnp.bfloat16), "dp", axis=0, tiled=True).astype(
            jnp.float32
        ),
        lax.all_gather(summed[5].astype(jnp.bfloat16), "dp", axis=0, tiled=True).astype(
            jnp.float32
        ),
        lax.all_gather(summed[6].astype(jnp.bfloat16), "dp", axis=0, tiled=True).astype(
            jnp.float32
        ),
        lax.all_gather(summed[7].astype(jnp.bfloat16), "dp", axis=0, tiled=True).astype(
            jnp.float32
        ),
        lax.all_gather(summed[8].astype(jnp.bfloat16), "dp", axis=0, tiled=True).astype(
            jnp.float32
        ),
        lax.all_gather(summed[9].astype(jnp.bfloat16), "dp", axis=0, tiled=True).astype(
            jnp.float32
        ),
        lax.all_gather(summed[10].astype(jnp.bfloat16), "dp", axis=0, tiled=True).astype(
            jnp.float32
        ),
        lax.all_gather(summed[11].astype(jnp.bfloat16), "dp", axis=0, tiled=True).astype(
            jnp.float32
        ),
        lax.all_gather(summed[12].astype(jnp.bfloat16), "dp", axis=0, tiled=True).astype(
            jnp.float32
        ),
        lax.all_gather(summed[13].astype(jnp.bfloat16), "dp", axis=0, tiled=True).astype(
            jnp.float32
        ),
        lax.all_gather(summed[14].astype(jnp.bfloat16), "dp", axis=0, tiled=True).astype(
            jnp.float32
        ),
    )


def general_shards(
    tokens,
    timesteps,
    boundary,
    importance,
    cotangent,
    time_weight,
    time_bias,
    mixing_weight,
    query_bias,
    value_bias,
    output_weight,
    output_bias,
    first_gain,
    first_shift,
    widen_weight,
    widen_bias,
    narrow_weight,
    narrow_bias,
    second_gain,
    second_shift,
):
    model_width = tokens.shape[2]
    score_scale = 1.0 / math.sqrt(HEAD)
    inputs, upstream = (tokens, cotangent)
    step_ids, bounds, weights = (timesteps, boundary, importance)
    offset = lax.axis_index("blk") * tokens.shape[0]
    row_count = inputs.shape[0]
    group_count = inputs.shape[1]
    time_code = sinusoid(step_ids, time_weight.shape[0]).astype(jnp.bfloat16)
    time_embed = jnp.dot(
        time_code, time_weight, preferred_element_type=jnp.float32
    ) + time_bias.astype(jnp.float32)
    hidden = inputs.astype(jnp.float32) + time_embed[None]
    hidden_low = hidden.astype(jnp.bfloat16)
    bias_pack = jnp.concatenate(
        [
            query_bias.astype(jnp.float32),
            jnp.zeros((model_width,), jnp.float32),
            value_bias.astype(jnp.float32),
        ]
    )
    packed = (
        jnp.einsum("lsd,de->lse", hidden_low, mixing_weight, preferred_element_type=jnp.float32)
        + bias_pack
    ).astype(jnp.bfloat16)
    queries = packed[..., :model_width].reshape(row_count, group_count, HEADS, HEAD)
    keys_values = packed[..., model_width:]
    both_all = lax.all_gather(keys_values, "blk", axis=0, tiled=True)
    total_rows = both_all.shape[0]
    keys_all = both_all[..., :model_width].reshape(total_rows, group_count, HEADS, HEAD)
    values_all = both_all[..., model_width:].reshape(total_rows, group_count, HEADS, HEAD)
    scores = (
        jnp.einsum("qshe,kshe->shqk", queries, keys_all, preferred_element_type=jnp.float32)
        * score_scale
    )
    row_peak = jnp.max(scores, axis=-1, keepdims=True)
    powered = jnp.exp(scores - row_peak)
    totals_soft = jnp.sum(powered, axis=-1, keepdims=True)
    probs_low = (powered / totals_soft).astype(jnp.bfloat16)
    log_total = row_peak + jnp.log(totals_soft)
    context = jnp.einsum(
        "shqk,kshe->qshe", probs_low, values_all, preferred_element_type=jnp.float32
    )
    context_low = context.reshape(row_count, group_count, model_width).astype(jnp.bfloat16)
    gain_one = first_gain.astype(jnp.float32)
    shift_one = first_shift.astype(jnp.float32)
    gain_two = second_gain.astype(jnp.float32)
    shift_two = second_shift.astype(jnp.float32)
    first_sum = (
        hidden
        + jnp.einsum("lsd,de->lse", context_low, output_weight, preferred_element_type=jnp.float32)
        + output_bias.astype(jnp.float32)
    )
    leading_norm, first_back = jax.vjp(layer_norm, first_sum, gain_one, shift_one)
    norm_reduced = leading_norm.astype(jnp.bfloat16)
    before_activation = jnp.einsum(
        "ikg,gv->ikv", norm_reduced, widen_weight, preferred_element_type=jnp.float32
    ) + widen_bias.astype(jnp.float32)
    activated, gelu_back = jax.vjp(partial(jax.nn.gelu, approximate=False), before_activation)
    activation_reduced = activated.astype(jnp.bfloat16)
    residual_sum = (
        leading_norm
        + jnp.einsum(
            "ema,aw->emw", activation_reduced, narrow_weight, preferred_element_type=jnp.float32
        )
        + narrow_bias.astype(jnp.float32)
    )
    out_full, second_back = jax.vjp(layer_norm, residual_sum, gain_two, shift_two)
    output = out_full.astype(jnp.bfloat16)
    positions = jnp.arange(row_count, dtype=jnp.int32) + offset
    row_weight = jnp.where(positions[:, None] >= bounds[None, :], weights[None, :], 0.0)
    out_grad = upstream.astype(jnp.float32) * row_weight[:, :, None]
    second_grad, second_gain_grad, second_shift_grad = second_back(out_grad)
    shrink_bias_grad = jnp.sum(second_grad, axis=(0, 1))
    narrow_reduced = second_grad.astype(jnp.bfloat16)
    shrink_weight_grad = jnp.einsum(
        "egk,egy->ky", activation_reduced, narrow_reduced, preferred_element_type=jnp.float32
    )
    act_grad = jnp.einsum(
        "ztv,ov->zto", narrow_reduced, narrow_weight, preferred_element_type=jnp.float32
    )
    pre_grad = gelu_back(act_grad)[0]
    expand_bias_grad = jnp.sum(pre_grad, axis=(0, 1))
    before_reduced = pre_grad.astype(jnp.bfloat16)
    expand_weight_grad = jnp.einsum(
        "thk,thr->kr", norm_reduced, before_reduced, preferred_element_type=jnp.float32
    )
    norm_grad = second_grad + jnp.einsum(
        "xcu,pu->xcp", before_reduced, widen_weight, preferred_element_type=jnp.float32
    )
    first_grad, first_gain_grad, first_shift_grad = first_back(norm_grad)
    output_bias_grad = jnp.sum(first_grad, axis=(0, 1))
    attn_low = first_grad.astype(jnp.bfloat16)
    output_weight_grad = jnp.einsum(
        "lsd,lse->de", context_low, attn_low, preferred_element_type=jnp.float32
    )
    context_grad = jnp.einsum(
        "lse,de->lsd", attn_low, output_weight, preferred_element_type=jnp.float32
    )
    context_grad = context_grad.astype(jnp.bfloat16).reshape(row_count, group_count, HEADS, HEAD)
    again = (
        jnp.einsum("qshe,kshe->shqk", queries, keys_all, preferred_element_type=jnp.float32)
        * score_scale
    )
    soft_probs = jnp.exp(again - log_total)
    prob_grad = jnp.einsum(
        "qshe,kshe->shqk", context_grad, values_all, preferred_element_type=jnp.float32
    )
    row_dot = jnp.sum(soft_probs * prob_grad, axis=-1, keepdims=True)
    score_low = (soft_probs * (prob_grad - row_dot)).astype(jnp.bfloat16)
    query_grad = (
        jnp.einsum("shqk,kshe->qshe", score_low, keys_all, preferred_element_type=jnp.float32)
        * score_scale
    )
    query_every, cgrad_every = (
        lax.all_gather(queries, "blk", axis=0, tiled=True),
        lax.all_gather(context_grad, "blk", axis=0, tiled=True),
    )
    total_every, dot_every = (
        lax.all_gather(log_total, "blk", axis=2, tiled=True),
        lax.all_gather(row_dot, "blk", axis=2, tiled=True),
    )
    own_keys = packed[..., model_width : 2 * model_width].reshape(
        row_count, group_count, HEADS, HEAD
    )
    own_values = packed[..., 2 * model_width :].reshape(row_count, group_count, HEADS, HEAD)
    local_scores = (
        jnp.einsum("qshe,kshe->shqk", query_every, own_keys, preferred_element_type=jnp.float32)
        * score_scale
    )
    local_probs = jnp.exp(local_scores - total_every)
    local_low = local_probs.astype(jnp.bfloat16)
    local_grad = jnp.einsum(
        "qshe,kshe->shqk", cgrad_every, own_values, preferred_element_type=jnp.float32
    )
    local_score_low = (local_probs * (local_grad - dot_every)).astype(jnp.bfloat16)
    value_own = jnp.einsum(
        "shqk,qshe->kshe", local_low, cgrad_every, preferred_element_type=jnp.float32
    )
    key_own = (
        jnp.einsum(
            "shqk,qshe->kshe", local_score_low, query_every, preferred_element_type=jnp.float32
        )
        * score_scale
    )
    key_here = jnp.concatenate(
        [
            key_own.reshape(row_count, group_count, model_width),
            value_own.reshape(row_count, group_count, model_width),
        ],
        axis=-1,
    )
    packed_grad = jnp.concatenate(
        [query_grad.reshape(row_count, group_count, model_width), key_here], axis=-1
    )
    query_bias_grad = jnp.sum(packed_grad[..., :model_width], axis=(0, 1))
    value_bias_grad = jnp.sum(packed_grad[..., 2 * model_width :], axis=(0, 1))
    packed_low = packed_grad.astype(jnp.bfloat16)
    mixing_weight_grad = jnp.einsum(
        "lsd,lse->de", hidden_low, packed_low, preferred_element_type=jnp.float32
    )
    hidden_grad = first_grad + jnp.einsum(
        "lse,de->lsd", packed_low, mixing_weight, preferred_element_type=jnp.float32
    )
    input_grad = hidden_grad.astype(jnp.bfloat16)
    time_total = jnp.sum(hidden_grad, axis=0)
    time_bias_grad = jnp.sum(time_total, axis=0)
    time_weight_grad = jnp.dot(
        time_code.astype(jnp.float32).T, time_total, precision=lax.Precision.HIGHEST
    )
    parts = (
        time_weight_grad,
        time_bias_grad,
        mixing_weight_grad,
        query_bias_grad,
        value_bias_grad,
        output_weight_grad,
        output_bias_grad,
        first_gain_grad,
        first_shift_grad,
        expand_weight_grad,
        expand_bias_grad,
        shrink_weight_grad,
        shrink_bias_grad,
        second_gain_grad,
        second_shift_grad,
    )
    summed = reduce_dp(parts)
    return (
        output,
        input_grad,
        summed[0],
        summed[1],
        summed[2],
        summed[3],
        summed[4],
        summed[5],
        summed[6],
        summed[7],
        summed[8],
        summed[9],
        summed[10],
        summed[11],
        summed[12],
        summed[13],
        summed[14],
    )


LOW = jnp.bfloat16
FULL = jnp.float32
PLACES = {"c": ("dp", 1), "y": ("dp", 2), "z": ("dp", 4), "w": ("dp", 8), "x": ("blk", 1)}
SHRINK_ORDERS = (("zxy", "xyz"),)
EXPAND_ORDERS = (("zxy", "xyz"),)
MIXING_ORDERS = (("xyz", "yxz"),)
ALL_ORDERS = tuple(dict.fromkeys(SHRINK_ORDERS + EXPAND_ORDERS + MIXING_ORDERS))
CORE, SIDE, NUMBERS = 0, 1, 2
WIDTH = 768
GRAD_ROWS = 3072


def swap(value, places):
    count = {axis: lax.axis_size(axis) for axis in ("dp", "blk")}
    pairs = []
    for group in range(count["dp"]):
        for side in range(count["blk"]):
            axis, bit = PLACES[places[group % 2 if len(places) == 2 else 0]]
            there = (group ^ bit, side) if axis == "dp" else (group, side ^ bit)
            pairs.append((group * count["blk"] + side, there[0] * count["blk"] + there[1]))
    return lax.ppermute(value, ("dp", "blk"), pairs)


def place_bit(place):
    axis, bit = PLACES[place]
    return (lax.axis_index(axis) // bit) % 2


def device_info():
    core = place_bit("c")
    own, other = [], []
    for orders in ALL_ORDERS:
        both = []
        for order in orders:
            number = 0
            for place in order:
                number = number * 2 + place_bit(place)
            both.append(number)
        own.append(jnp.where(core == 0, both[0], both[1]))
        other.append(jnp.where(core == 0, both[1], both[0]))
    return jnp.stack([core, lax.axis_index("blk")] + own + other).astype(jnp.int32)


def order_number(info_ref, orders, unit, mine):
    places = [NUMBERS + ALL_ORDERS.index(o) + (0 if mine else len(ALL_ORDERS)) for o in orders]
    number = info_ref[places[0]]
    for k in range(1, len(orders)):
        number = jnp.where(unit == k, info_ref[places[k]], number)
    return number


def weight_half(left, right, info, orders, left_of, right_of, got=None):
    units = len(orders)
    block = GRAD_ROWS // units // 16
    tile_rows = 4 * block
    mine = got is not None

    def body(info_ref, left_ref, right_ref, *refs):
        core = info_ref[CORE]
        side = core if mine else 1 - core
        for step in range(2 * units):
            unit, part = step // 2, step % 2
            tile = 4 * unit + 2 * side + part
            number = order_number(info_ref, orders, unit, mine)
            column = pl.multiple_of(left_of(tile) * tile_rows, 128)
            place = pl.multiple_of(right_of(tile) * WIDTH, 128)
            product = turned_times(
                left_ref[:, pl.ds(column, tile_rows)], right_ref[:, pl.ds(place, WIDTH)]
            )
            spots = [((4 * part + i) ^ number) & 7 for i in range(4)]
            rows = [pl.multiple_of((8 * unit + spot) * block, 16) for spot in spots]
            pieces = [product[i * block : (i + 1) * block, :] for i in range(4)]
            if not mine:
                for row, piece in zip(rows, pieces):
                    refs[0][pl.ds(row, block), :] = piece.astype(LOW)
                continue
            got_ref, upper_ref, lower_ref = refs[0], refs[1 + unit], refs[-1]
            pieces = [
                (piece + got_ref[pl.ds(row, block), :].astype(FULL)).astype(LOW)
                for row, piece in zip(rows, pieces)
            ]
            upper = part ^ ((number // 4) % 2)

            @pl.when(upper == 0)
            def _(pieces=pieces, spots=spots, lower_ref=lower_ref, unit=unit):
                for spot, piece in zip(spots, pieces):
                    row = pl.multiple_of((4 * unit + (spot & 3)) * block, 16)
                    lower_ref[pl.ds(row, block), :] = piece

            @pl.when(upper == 1)
            def _(pieces=pieces, spots=spots, upper_ref=upper_ref):
                for spot, piece in zip(spots, pieces):
                    row = pl.multiple_of((spot & 3) * block, 16)
                    upper_ref[pl.ds(row, block), :] = piece

    rows = left.shape[0]
    counts = [4 * block] * units + [4 * units * block] if mine else [8 * units * block]
    vmem = pl.BlockSpec(memory_space=pltpu.VMEM)
    found = pl.pallas_call(
        body,
        in_specs=[pl.BlockSpec(memory_space=pltpu.SMEM)] + [vmem] * (3 if mine else 2),
        out_specs=[vmem] * len(counts),
        out_shape=[jax.ShapeDtypeStruct((c, WIDTH), LOW) for c in counts],
        compiler_params=kernel_params(),
        cost_estimate=cost(2.8),
    )(info, left, right, *([got] if mine else []))
    return found if mine else found[0]


def widen_out(near, far, info, orders, first_tile, tile_count, columns):
    units = len(orders)
    block = GRAD_ROWS // units // 16
    part = 64 if block % 64 == 0 else block
    tall = 4 * block * tile_count // columns
    pieces = 4 if columns == 1 else 1
    start = 4 * first_tile * block

    def body(info_ref, near_ref, far_ref, out_ref):
        step = pl.program_id(0)
        for column in range(columns):
            for piece in range(pieces):
                first = start + column * tall + (step * pieces + piece) * part
                index = first // block
                unit = index // 16
                own = (index % 16) // 8 == info_ref[CORE]
                rows = []
                for mine in (True, False):
                    number = order_number(info_ref, orders, unit, mine)
                    row = (unit * 8 + ((index ^ number) & 7)) * block + first % block
                    rows.append(pl.multiple_of(row, 16))
                near_row, far_row = rows
                target = (
                    slice(piece * part, (piece + 1) * part),
                    slice(column * WIDTH, (column + 1) * WIDTH),
                )

                @pl.when(own)
                def _(row=near_row, target=target):
                    out_ref[target] = near_ref[pl.ds(row, part), :].astype(FULL)

                @pl.when(jnp.logical_not(own))
                def _(row=far_row, target=target):
                    out_ref[target] = far_ref[pl.ds(row, part), :].astype(FULL)

    whole = pl.BlockSpec(near.shape, lambda t, p: (0, 0), pipeline_mode=ONE)
    return pl.pallas_call(
        body,
        grid_spec=pltpu.PrefetchScalarGridSpec(
            num_scalar_prefetch=1,
            grid=(tall // (pieces * part),),
            in_specs=[whole, whole],
            out_specs=pl.BlockSpec((pieces * part, columns * WIDTH), lambda t, p: (t, 0)),
        ),
        out_shape=jax.ShapeDtypeStruct((tall, columns * WIDTH), FULL),
        compiler_params=kernel_params(),
        cost_estimate=cost(6.0, 60),
    )(info, near, far)


def widen_half(source, info, orders, mine, base=None):
    units = len(orders)
    block = GRAD_ROWS // units // 16
    count = 8 * units

    def body(info_ref, source_ref, *refs):
        mix_ref, out_ref, stage_ref, sems = refs[-4:]
        core = info_ref[CORE]
        half = core if mine else 1 - core
        moves = []
        for k in range(count):
            unit, spot = k // 8, k % 8
            number = order_number(info_ref, orders, unit, mine)
            first = (16 * unit + 8 * half + (spot ^ (number & 7))) * block
            matrix = first // WIDTH
            row = pl.multiple_of(first % WIDTH, 16)
            column = pl.multiple_of(jnp.minimum(matrix, 2) * WIDTH, 128)
            here = slice(k * block, (k + 1) * block)
            stage_ref[here, :] = source_ref[here, :].astype(FULL)
            mixed = pltpu.make_async_copy(
                stage_ref.at[here, :],
                mix_ref.at[pl.ds(row, block), pl.ds(column, WIDTH)],
                sems.at[k],
            )
            output = pltpu.make_async_copy(
                stage_ref.at[here, :], out_ref.at[pl.ds(row, block), :], sems.at[k]
            )
            moves.append((matrix, mixed, output))
            pl.when(matrix < 3)(mixed.start)
            pl.when(matrix >= 3)(output.start)
        for matrix, mixed, output in moves:
            pl.when(matrix < 3)(mixed.wait)
            pl.when(matrix >= 3)(output.wait)

    hbm = pl.BlockSpec(memory_space=pltpu.HBM)
    operands = [info, source] + ([] if base is None else list(base))
    return pl.pallas_call(
        body,
        in_specs=[
            pl.BlockSpec(memory_space=pltpu.SMEM),
            pl.BlockSpec(memory_space=pltpu.VMEM),
        ]
        + [hbm] * (len(operands) - 2),
        out_specs=[hbm, hbm],
        out_shape=[
            jax.ShapeDtypeStruct((WIDTH, 3 * WIDTH), FULL),
            jax.ShapeDtypeStruct((WIDTH, WIDTH), FULL),
        ],
        scratch_shapes=[
            pltpu.VMEM((count * block, WIDTH), FULL),
            pltpu.SemaphoreType.DMA((count,)),
        ],
        input_output_aliases={} if base is None else {2: 0, 3: 1},
        compiler_params=kernel_params(),
        cost_estimate=cost(3.0, 30),
    )(*operands)


def combine(outputs):
    arrays = []

    def number(array):
        for k, known in enumerate(arrays):
            if known is array:
                return k
        arrays.append(array)
        return len(arrays) - 1

    plan = [
        [[(number(array), row, rows) for array, row, rows in piece] for piece in pieces]
        for pieces in outputs
    ]
    heights = [sum(piece[0][2] for piece in pieces) for pieces in outputs]

    def body(*refs):
        sources, targets = refs[: len(arrays)], refs[len(arrays) :]
        for pieces, target in zip(plan, targets):
            place = 0
            for piece in pieces:
                rows = piece[0][2]
                for first in range(0, rows, 128):
                    count = min(128, rows - first)
                    values = [sources[k][row + first : row + first + count, :] for k, row, _ in piece]
                    total = values[0] if len(values) == 1 else values[0] + values[1]
                    target[place + first : place + first + count, :] = total
                place += rows

    vmem = pl.BlockSpec(memory_space=pltpu.VMEM)
    return pl.pallas_call(
        body,
        in_specs=[vmem] * len(arrays),
        out_specs=[vmem] * len(outputs),
        out_shape=[jax.ShapeDtypeStruct((h, WIDTH), LOW) for h in heights],
        compiler_params=kernel_params(),
        cost_estimate=cost(0.4, 12),
    )(*arrays)


class Rider:
    def __init__(self, packed):
        self.packed = packed
        self.filled = 1

    def rows(self):
        return self.packed.shape[0]

    def pieces(self):
        return [((self.packed, 0, self.rows()),)]

    def take(self, got, row):
        packed, rows, filled = self.packed, self.rows(), self.filled
        if filled >= RIDER_LANES:
            (self.packed,) = combine(
                [
                    [
                        ((packed, 0, 16), (got, row, 16)),
                        ((packed, 16, rows - 16),),
                        ((got, row + 16, rows - 16),),
                    ]
                ]
            )
            return

        def body(packed_ref, got_ref, out_ref):
            out_ref[:16, :] = packed_ref[:16, :] + got_ref[row : row + 16, :]
            out_ref[16:, : filled * 128] = packed_ref[16:, : filled * 128]
            out_ref[16:, filled * 128 : 2 * filled * 128] = got_ref[
                row + 16 : row + 32, : filled * 128
            ]
            out_ref[16:, 2 * filled * 128 :] = packed_ref[16:, 2 * filled * 128 :]

        vmem = pl.BlockSpec(memory_space=pltpu.VMEM)
        self.packed = pl.pallas_call(
            body,
            in_specs=[vmem, vmem],
            out_specs=vmem,
            out_shape=jax.ShapeDtypeStruct(packed.shape, LOW),
            compiler_params=kernel_params(),
            cost_estimate=cost(0.4),
            name="ride",
        )(packed, got)
        self.filled = 2 * filled


def flow(orders, uppers, lower, rider=None):
    units = len(orders)
    size = lower.shape[0] // units
    mine = [(lower, k * size, size) for k in range(units)]

    def cut(view, part):
        array, row, rows = view
        return array, row + part * rows // 2, rows // 2

    def places_at(level):
        return [first[level] + second[level] for first, second in orders]

    got = yield list(zip(places_at(0), uppers))
    for level in (1, 2):
        views = [(g, 0, size) for g in got]
        away = [[(cut(m, 1), cut(v, 1))] for m, v in zip(mine, views)]
        kept = [(cut(m, 0), cut(v, 0)) for m, v in zip(mine, views)]
        size = size // 2
        *sends, rest = combine(away + [kept])
        mine = [(rest, k * size, size) for k in range(units)]
        got = yield list(zip(places_at(level), sends))

    rider = None if rider is None else rider()

    def riding():
        return [] if rider is None else rider.pieces()

    (joined,) = combine([[(m, (g, 0, size)) for m, g in zip(mine, got)] + riding()])
    (other,) = yield [("w", joined)]
    values = combine([[((joined, k * size, size), (other, k * size, size))] for k in range(units)])
    if rider is not None:
        rider.take(other, units * size)
    for level in (2, 1, 0):
        sends = list(values)
        if rider is not None:
            (sends[0],) = combine([[((values[0], 0, size),)] + rider.pieces()])
        got = yield list(zip(places_at(level), sends))
        if rider is not None:
            rider.take(got[0], size)
        pieces = [[((v, 0, size),), ((g, 0, size),)] for v, g in zip(values, got)]
        size = 2 * size
        if level > 0:
            values = combine(pieces)
    (near,) = combine([sum(pieces, []) + riding()])
    (far,) = yield [("c", near)]
    if rider is not None:
        rider.take(far, units * size)
    return near, far


RIDER_LANES = 4


def pack_small(sums_zero, sums_one, sums_two, expand_bias, time_total, time_code):
    pair, code_width = time_code.shape
    width = sums_one.shape[1]
    blocks = width // 128

    def body(zero_ref, one_ref, two_ref, bias_ref, total_ref, code_ref, out_ref):
        bias = [bias_ref[:, k * width : (k + 1) * width] for k in range(4)]
        out_ref[:16, :] = jnp.concatenate(
            [zero_ref[0] + zero_ref[1], one_ref[:3, :], two_ref[:3, :]]
            + bias
            + [jnp.zeros((4, width), FULL)],
            axis=0,
        ).astype(LOW)
        totals = [
            total_ref[s, :, 128 * j : 128 * j + 128] for s in range(pair) for j in range(blocks)
        ]
        codes = code_ref[...].astype(FULL)
        out_ref[16:, :] = jnp.zeros((16, width), LOW)
        out_ref[16:, :128] = jnp.concatenate(
            totals + [codes, jnp.zeros((16 - pair * (blocks + 1), 128), FULL)], axis=0
        ).astype(LOW)

    return pl.pallas_call(
        body,
        out_shape=jax.ShapeDtypeStruct((32, width), LOW),
        compiler_params=kernel_params(),
        cost_estimate=cost(0.6),
    )(sums_zero, sums_one, sums_two, expand_bias, time_total, time_code)


def unpack_small(packed, pair, code_width):
    count, width = packed.shape
    blocks = width // 128
    groups = (count - 16) // 16

    def body(packed_ref, sums_ref, weight_ref, bias_ref, wide_ref):
        sums_ref[...] = packed_ref[:16, :].astype(FULL)
        for lane in range(RIDER_LANES):
            wide_ref[lane] = packed_ref[16:, 128 * lane : 128 * lane + 128].astype(FULL)

        def every(row):
            return jnp.concatenate(
                [wide_ref[lane, pl.ds(row, groups, stride=16), :] for lane in range(RIDER_LANES)],
                axis=0,
            )

        codes = [every(pair * blocks + s).astype(LOW) for s in range(pair)]
        for j in range(blocks):
            columns = slice(128 * j, 128 * j + 128)
            totals = [every(s * blocks + j) for s in range(pair)]
            weight_ref[:, columns] = sum(
                turned_times(c, t.astype(LOW)) for c, t in zip(codes, totals)
            )
            bias_ref[:, columns] = jnp.sum(sum(totals), axis=0, keepdims=True)

    return pl.pallas_call(
        body,
        out_shape=[
            jax.ShapeDtypeStruct((16, width), FULL),
            jax.ShapeDtypeStruct((code_width, width), FULL),
            jax.ShapeDtypeStruct((1, width), FULL),
        ],
        scratch_shapes=[pltpu.VMEM((RIDER_LANES, count - 16, 128), FULL)],
        compiler_params=kernel_params(),
        cost_estimate=cost(1.0),
    )(packed)


class Order:
    def __init__(self):
        self.token = None
        self.flows = {}
        self.sent = {}

    def after(self, *values):
        if self.token is None:
            return values
        return lax.optimization_barrier((self.token,) + tuple(values))[1:]

    def run(self, function, *values, token=0):
        found = function(*self.after(*values))
        self.token = found[token] if isinstance(found, (tuple, list)) else found
        return found

    def begin(self, name, steps):
        pairs = next(steps)
        self.flows[name] = steps, [swap(value, place) for place, value in pairs]

    def advance(self, name):
        steps, got = self.flows[name]
        try:
            pairs = steps.send(list(self.after(*got)))
        except StopIteration as stop:
            return stop.value
        self.token = pairs[0][1]
        self.sent[name] = pairs[0][1]
        self.flows[name] = steps, [swap(value, place) for place, value in pairs]
        return None


VMEM_LIMIT = 8 * 1024 * 1024
ONE = pl.Buffered(1)
SCALE = 600000000


def cost(microseconds, megabytes=0):
    return pl.CostEstimate(
        flops=int(microseconds * SCALE),
        bytes_accessed=1 + int(megabytes * 1000000),
        transcendentals=0,
    )


def kernel_params():
    return pltpu.CompilerParams(vmem_limit_bytes=VMEM_LIMIT)


def times(left, right):
    return jnp.dot(left, right, preferred_element_type=FULL)


def times_turned(left, right):
    return lax.dot_general(left, right, (((1,), (1,)), ((), ())), preferred_element_type=FULL)


def turned_times(left, right):
    return lax.dot_general(left, right, (((0,), (0,)), ((), ())), preferred_element_type=FULL)


def split_rows(values, info):
    near, group, width = values.shape
    pair = group // 2
    count = near * group

    def body(info_ref, values_ref, away_ref, own_ref):
        side = info_ref[SIDE]
        rows = values_ref[...].reshape(count, width)
        row = lax.broadcasted_iota(jnp.int32, (count, count), 0)
        column = lax.broadcasted_iota(jnp.int32, (count, count), 1)
        half = pair * near
        first = jnp.where(row < half, pair * (1 - side), pair * side)
        place = jnp.where(row < half, row, row - half)
        source = (place % near) * group + first + place // near
        pick = (source == column).astype(FULL).astype(LOW)
        moved = times(pick, rows).astype(LOW)
        away_ref[...] = moved[:half].reshape(pair, near, width)
        own_ref[...] = moved[half:].reshape(pair, near, width)

    shape = jax.ShapeDtypeStruct((pair, near, width), values.dtype)
    return pl.pallas_call(
        body,
        in_specs=[
            pl.BlockSpec(memory_space=pltpu.SMEM),
            pl.BlockSpec(memory_space=pltpu.VMEM),
        ],
        out_shape=[shape, shape],
        compiler_params=kernel_params(),
        cost_estimate=cost(16.0),
    )(info, values)


def lay_out(vectors, weights, after):
    count = len(weights)

    def body(*refs):
        refs[-1][...] = refs[0][...]

    vmem = pl.BlockSpec(memory_space=pltpu.VMEM)
    return pl.pallas_call(
        body,
        in_specs=[vmem] * (1 + count) + [pl.BlockSpec(memory_space=pl.ANY)],
        out_specs=vmem,
        out_shape=jax.ShapeDtypeStruct(vectors.shape, vectors.dtype),
        compiler_params=kernel_params(),
        cost_estimate=cost(8.0, 60),
    )(vectors, *weights, after)


def join_rows(own, got, info):
    pair, near, width = own.shape
    group = 2 * pair
    count = near * group

    def body(info_ref, own_ref, got_ref, out_ref):
        side = info_ref[SIDE]
        row = lax.broadcasted_iota(jnp.int32, (count, count), 0)
        column = lax.broadcasted_iota(jnp.int32, (count, count), 1)
        half = pair * near
        sequence = row % group
        position = row // group
        from_own = sequence // pair == side
        source = jnp.where(from_own, 0, half) + (sequence % pair) * near + position
        pick = (source == column).astype(FULL).astype(LOW)
        rows = jnp.concatenate(
            [own_ref[...].reshape(half, width), got_ref[...].reshape(half, width)], axis=0
        )
        out_ref[...] = times(pick, rows).astype(LOW).reshape(near, group, width)

    return pl.pallas_call(
        body,
        in_specs=[
            pl.BlockSpec(memory_space=pltpu.SMEM),
            pl.BlockSpec(memory_space=pltpu.VMEM),
            pl.BlockSpec(memory_space=pltpu.VMEM),
        ],
        out_shape=jax.ShapeDtypeStruct((near, group, width), own.dtype),
        compiler_params=kernel_params(),
        cost_estimate=cost(2.0),
    )(info, own, got)


QUERY_BIAS, VALUE_BIAS, OUTPUT_BIAS, FIRST_GAIN, FIRST_SHIFT = range(5)
NARROW_BIAS, SECOND_GAIN, SECOND_SHIFT = range(5, 8)


def head_masks(scale):
    lane = lax.broadcasted_iota(jnp.int32, (1, 2 * HEAD), 1)
    first = jnp.where(lane < HEAD, scale, 0.0).astype(LOW)
    second = jnp.where(lane < HEAD, 0.0, scale).astype(LOW)
    return first, second


def attend(own, got, embed, mixing_weight, output_weight, vectors):
    pair, near, width = own.shape
    length = 2 * near
    scale = 1.0 / math.sqrt(HEAD)
    duo = 2 * HEAD

    def body(own_ref, got_ref, embed_ref, mix_ref, wout_ref, vec_ref, left_ref, packed_ref,
             probs_ref, centred_ref, scale_ref, norm_ref):
        for s in range(pair):
            here = slice(s * length, (s + 1) * length)
            hidden = jnp.concatenate([own_ref[s], got_ref[s]], axis=0).astype(FULL) + embed_ref[s]
            hidden_low = hidden.astype(LOW)
            left_ref[here, :width] = hidden_low
            for part, bias in ((0, QUERY_BIAS), (1, None), (2, VALUE_BIAS)):
                columns = slice(part * width, (part + 1) * width)
                product = times(hidden_low, mix_ref[:, columns])
                if bias is not None:
                    product = product + vec_ref[bias : bias + 1, :]
                packed_ref[here, columns] = product.astype(LOW)
            masks = head_masks(scale)
            lane = lax.broadcasted_iota(jnp.int32, (length, duo), 1)
            for j in range(width // duo):
                query = packed_ref[here, j * duo : (j + 1) * duo]
                key = packed_ref[here, width + j * duo : width + (j + 1) * duo]
                value = packed_ref[here, 2 * width + j * duo : 2 * width + (j + 1) * duo]
                found = []
                for head in range(2):
                    scores = times_turned(query * masks[head], key)
                    peak = jnp.max(scores, axis=-1, keepdims=True)
                    powered = jnp.exp(scores - peak)
                    total = jnp.sum(powered, axis=-1, keepdims=True)
                    low = (powered * (1.0 / total)).astype(LOW)
                    probs_ref[s, 2 * j + head] = low
                    found.append(times(low, value))
                left_ref[here, width + j * duo : width + (j + 1) * duo] = jnp.where(
                    lane < HEAD, found[0], found[1]
                ).astype(LOW)
            first_sum = (
                hidden
                + times(left_ref[here, width:], wout_ref[...])
                + vec_ref[OUTPUT_BIAS : OUTPUT_BIAS + 1, :]
            )
            centred = first_sum - jnp.mean(first_sum, axis=-1, keepdims=True)
            variance = jnp.mean(centred * centred, axis=-1, keepdims=True)
            inverse = lax.rsqrt(variance + epsilon)
            centred = centred * inverse
            centred_ref[here, :] = centred
            scale_ref[here, :] = jnp.broadcast_to(inverse, (length, 128))
            norm_ref[here, :] = (
                centred * vec_ref[FIRST_GAIN : FIRST_GAIN + 1, :]
                + vec_ref[FIRST_SHIFT : FIRST_SHIFT + 1, :]
            ).astype(LOW)

    rows = pair * length
    vmem = pl.BlockSpec(memory_space=pltpu.VMEM)
    return pl.pallas_call(
        body,
        in_specs=[vmem] * 6,
        out_specs=[vmem] * 6,
        out_shape=[
            jax.ShapeDtypeStruct((rows, 2 * width), LOW),
            jax.ShapeDtypeStruct((rows, 3 * width), LOW),
            jax.ShapeDtypeStruct((pair, HEADS, length, length), LOW),
            jax.ShapeDtypeStruct((rows, width), FULL),
            jax.ShapeDtypeStruct((rows, 128), FULL),
            jax.ShapeDtypeStruct((rows, width), LOW),
        ],
        compiler_params=kernel_params(),
        cost_estimate=cost(25.0),
    )(own, got, embed, mixing_weight, output_weight, vectors)


def gelu_parts(value):
    t = 1.0 / (1.0 + (0.3275911 * math.sqrt(0.5)) * jnp.abs(value))
    series = (0.254829592, -0.284496736, 1.421413741, -1.453152027, 1.061405429)
    tail = jnp.full_like(value, 0.5 * series[-1])
    for factor in series[-2::-1]:
        tail = tail * t + 0.5 * factor
    power = jnp.exp(-0.5 * value * value)
    tail = tail * t * power
    return jnp.where(value < 0, tail, 1.0 - tail), power * (1.0 / math.sqrt(2.0 * math.pi))


STRIP = 512
LONG = 128
PART = 768
BACK_PART = 768
UNROLL = 1


def sum_eights(value):
    return jnp.sum(value.reshape(-1, 8, value.shape[-1]), axis=0)


def feed(norm_low, centred, widen_weight, widen_bias, narrow_weight, vectors, own_cot, got_cot,
         info, bounds, weights):
    rows, width = norm_low.shape
    pair, near, _ = own_cot.shape
    length = 2 * near
    inner = widen_weight.shape[1]

    def body(info_ref, bound_ref, weight_ref, norm_ref, centred_ref, wide_ref, wbias_ref, narrow_ref, vec_ref,
             own_ref, got_ref, act_ref, slope_ref, out_own_ref, out_away_ref, grad_ref, low_ref,
             sums_ref, total_ref):
        def widen(k, carry):
            columns = pl.ds(pl.multiple_of(k * PART, 128), PART)
            value = times(norm_ref[...], wide_ref[:, columns]) + wbias_ref[:, columns]
            below, density = gelu_parts(value)
            act_ref[:, columns] = (value * below).astype(LOW)
            slope_ref[:, columns] = (below + value * density).astype(LOW)
            return carry

        lax.fori_loop(0, inner // PART, widen, 0)
        total_ref[...] = times(act_ref[...], narrow_ref[...])
        side = info_ref[SIDE]

        def vector(k):
            return vec_ref[k : k + 1, :]

        zero = jnp.zeros((8, width), FULL)
        sums = (zero, zero, zero)
        for quarter in range(2 * pair):
            sequence, far = quarter // 2, quarter % 2
            cot_ref = got_ref if far else own_ref
            back_ref = out_away_ref if far else out_own_ref
            bound = bound_ref[pair * side + sequence]
            weight = weight_ref[pair * side + sequence]
            start = jnp.where(side == far, 0, near)

            def finish(i, sums, quarter=quarter, sequence=sequence, cot_ref=cot_ref,
                       back_ref=back_ref, bound=bound, weight=weight, start=start):
                inside = pl.multiple_of(i * LONG, LONG)
                row = pl.multiple_of(quarter * near + i * LONG, LONG)
                first_norm = (
                    centred_ref[pl.ds(row, LONG), :] * vector(FIRST_GAIN) + vector(FIRST_SHIFT)
                )
                total = first_norm + total_ref[pl.ds(row, LONG), :] + vector(NARROW_BIAS)
                level = total - jnp.mean(total, axis=-1, keepdims=True)
                inverse = lax.rsqrt(jnp.mean(level * level, axis=-1, keepdims=True) + epsilon)
                level = level * inverse
                back_ref[sequence, pl.ds(inside, LONG), :] = (
                    level * vector(SECOND_GAIN) + vector(SECOND_SHIFT)
                ).astype(LOW)
                place = start + inside + lax.broadcasted_iota(jnp.int32, (LONG, 1), 0)
                factor = jnp.where(place >= bound, weight, 0.0)
                upstream = cot_ref[sequence, pl.ds(inside, LONG), :].astype(FULL) * factor
                gained = upstream * vector(SECOND_GAIN)
                mean = jnp.mean(gained, axis=-1, keepdims=True)
                along = jnp.mean(gained * level, axis=-1, keepdims=True)
                grad = inverse * (gained - mean - level * along)
                grad_ref[pl.ds(row, LONG), :] = grad
                low_ref[pl.ds(row, LONG), :] = grad.astype(LOW)
                return (
                    sums[0] + sum_eights(grad),
                    sums[1] + sum_eights(upstream * level),
                    sums[2] + sum_eights(upstream),
                )

            sums = lax.fori_loop(0, near // LONG, finish, sums)
        sums_ref[...] = jnp.concatenate(
            [jnp.sum(v, axis=0, keepdims=True) for v in sums] + [jnp.zeros((5, width), FULL)],
            axis=0,
        )

    half = (pair, near, width)
    smem = pl.BlockSpec(memory_space=pltpu.SMEM)
    vmem = pl.BlockSpec(memory_space=pltpu.VMEM)
    return pl.pallas_call(
        body,
        in_specs=[smem] * 3 + [vmem] * 8,
        out_specs=[vmem] * 7,
        scratch_shapes=[pltpu.VMEM((rows, width), FULL)],
        out_shape=[
            jax.ShapeDtypeStruct((rows, inner), LOW),
            jax.ShapeDtypeStruct((rows, inner), LOW),
            jax.ShapeDtypeStruct(half, LOW),
            jax.ShapeDtypeStruct(half, LOW),
            jax.ShapeDtypeStruct((rows, width), FULL),
            jax.ShapeDtypeStruct((rows, width), LOW),
            jax.ShapeDtypeStruct((8, width), FULL),
        ],
        compiler_params=kernel_params(),
        cost_estimate=cost(40.0),
    )(info, bounds, weights, norm_low, centred, widen_weight, widen_bias, narrow_weight, vectors,
      own_cot, got_cot)


def feed_back(shrink_low, second_grad, slope, centred, inverse, widen_weight, narrow_weight, vectors):
    rows, width = shrink_low.shape
    inner = slope.shape[1]

    def body(low_ref, grad_ref, slope_ref, centred_ref, inverse_ref, wide_ref, narrow_ref, vec_ref,
             pre_ref, bias_ref, first_ref, attn_ref, sums_ref, total_ref):
        total = None
        for c in range(0, inner, BACK_PART):
            columns = slice(c, c + BACK_PART)
            value = times_turned(low_ref[...], narrow_ref[columns, :])
            value = value * slope_ref[:, columns].astype(FULL)
            low = value.astype(LOW)
            pre_ref[:, columns] = low
            bias_ref[:, columns] = jnp.sum(sum_eights(value), axis=0, keepdims=True)
            term = times_turned(low, wide_ref[:, columns])
            total = term if total is None else total + term
        total_ref[...] = total
        gain = vec_ref[FIRST_GAIN : FIRST_GAIN + 1, :]

        def finish(i, sums):
            row = pl.multiple_of(i * LONG, LONG)
            upstream = grad_ref[pl.ds(row, LONG), :] + total_ref[pl.ds(row, LONG), :]
            level = centred_ref[pl.ds(row, LONG), :]
            gained = upstream * gain
            mean = jnp.mean(gained, axis=-1, keepdims=True)
            along = jnp.mean(gained * level, axis=-1, keepdims=True)
            grad = inverse_ref[pl.ds(row, LONG), :1] * (gained - mean - level * along)
            first_ref[pl.ds(row, LONG), :] = grad
            attn_ref[pl.ds(row, LONG), :] = grad.astype(LOW)
            return (
                sums[0] + sum_eights(grad),
                sums[1] + sum_eights(upstream * level),
                sums[2] + sum_eights(upstream),
            )

        zero = jnp.zeros((8, width), FULL)
        sums = lax.fori_loop(0, rows // LONG, finish, (zero, zero, zero))
        sums_ref[...] = jnp.concatenate(
            [jnp.sum(v, axis=0, keepdims=True) for v in sums] + [jnp.zeros((5, width), FULL)],
            axis=0,
        )

    vmem = pl.BlockSpec(memory_space=pltpu.VMEM)
    return pl.pallas_call(
        body,
        in_specs=[vmem] * 8,
        out_specs=[vmem] * 5,
        out_shape=[
            jax.ShapeDtypeStruct((rows, inner), LOW),
            jax.ShapeDtypeStruct((1, inner), FULL),
            jax.ShapeDtypeStruct((rows, width), FULL),
            jax.ShapeDtypeStruct((rows, width), LOW),
            jax.ShapeDtypeStruct((8, width), FULL),
        ],
        scratch_shapes=[pltpu.VMEM((rows, width), FULL)],
        compiler_params=kernel_params(),
        cost_estimate=cost(8.6),
    )(shrink_low, second_grad, slope, centred, inverse, widen_weight, narrow_weight, vectors)


def attend_back(attn_low, packed, probs, output_weight):
    pair, _, length, _ = probs.shape
    width = attn_low.shape[1]
    rows = attn_low.shape[0]
    scale = 1.0 / math.sqrt(HEAD)
    duo = 2 * HEAD

    def body(attn_ref, packed_ref, probs_ref, wout_ref, right_ref, sums_ref, context_ref):
        for s in range(pair):
            here = slice(s * length, (s + 1) * length)
            context_ref[...] = times_turned(attn_ref[here, :], wout_ref[...]).astype(LOW)
            masks = head_masks(1.0)
            lane = lax.broadcasted_iota(jnp.int32, (length, duo), 1)
            for j in range(width // duo):
                query = packed_ref[here, j * duo : (j + 1) * duo]
                key = packed_ref[here, width + j * duo : width + (j + 1) * duo]
                value = packed_ref[here, 2 * width + j * duo : 2 * width + (j + 1) * duo]
                upstream = context_ref[:, j * duo : (j + 1) * duo]
                parts = []
                for head in range(2):
                    low = probs_ref[s, 2 * j + head]
                    probs_full = low.astype(FULL)
                    slope = times_turned(upstream * masks[head], value)
                    dot = jnp.sum(probs_full * slope, axis=-1, keepdims=True)
                    score = (probs_full * (slope - dot)).astype(LOW)
                    parts.append(
                        (times(score, key), turned_times(score, query), turned_times(low, upstream))
                    )
                first, second = parts
                query_grad = jnp.where(lane < HEAD, first[0], second[0]) * scale
                key_grad = jnp.where(lane < HEAD, first[1], second[1]) * scale
                value_grad = jnp.where(lane < HEAD, first[2], second[2])
                right_ref[here, j * duo : (j + 1) * duo] = query_grad.astype(LOW)
                right_ref[here, width + j * duo : width + (j + 1) * duo] = key_grad.astype(LOW)
                right_ref[here, 2 * width + j * duo : 2 * width + (j + 1) * duo] = value_grad.astype(LOW)
                sums_ref[s, 0:1, j * duo : (j + 1) * duo] = jnp.sum(query_grad, axis=0, keepdims=True)
                sums_ref[s, 1:2, j * duo : (j + 1) * duo] = jnp.sum(value_grad, axis=0, keepdims=True)
            right_ref[here, 3 * width :] = attn_ref[here, :]

    vmem = pl.BlockSpec(memory_space=pltpu.VMEM)
    return pl.pallas_call(
        body,
        in_specs=[vmem] * 4,
        out_specs=[vmem] * 2,
        out_shape=[
            jax.ShapeDtypeStruct((rows, 4 * width), LOW),
            jax.ShapeDtypeStruct((pair, 2, width), FULL),
        ],
        scratch_shapes=[pltpu.VMEM((length, width), LOW)],
        compiler_params=kernel_params(),
        cost_estimate=cost(10),
    )(attn_low, packed, probs, output_weight)


def hidden_back(right, first_grad, mixing_weight, pair):
    rows, width = first_grad.shape
    length = rows // pair
    near = length // 2

    def body(right_ref, grad_ref, mix_ref, own_ref, away_ref, total_ref):
        for s in range(pair):
            here = slice(s * length, (s + 1) * length)
            hidden = grad_ref[here, :] + times_turned(right_ref[here, : 3 * width], mix_ref[...])
            low = hidden.astype(LOW)
            own_ref[s] = low[:near]
            away_ref[s] = low[near:]
            total_ref[s] = jnp.sum(hidden, axis=0, keepdims=True)

    vmem = pl.BlockSpec(memory_space=pltpu.VMEM)
    return pl.pallas_call(
        body,
        in_specs=[vmem] * 3,
        out_specs=[vmem] * 3,
        out_shape=[
            jax.ShapeDtypeStruct((pair, near, width), LOW),
            jax.ShapeDtypeStruct((pair, near, width), LOW),
            jax.ShapeDtypeStruct((pair, 1, width), FULL),
        ],
        compiler_params=kernel_params(),
        cost_estimate=cost(2.5),
    )(right, first_grad, mixing_weight)


(
    S_SEND, FEED_BACK, S_KEEP, E_SEND, E_KEEP, ATTEND_BACK, M_SEND, HIDDEN_BACK, M_KEEP, OUT_GOT,
    GRAD_GOT, OUT_JOIN, GRAD_JOIN, M_NEAR, UNPACK, S_WIDEN, E_WIDEN, S, E, M,
) = range(20)


def pair_shards(
    tokens,
    timesteps,
    boundary,
    importance,
    cotangent,
    time_weight,
    time_bias,
    mixing_weight,
    query_bias,
    value_bias,
    output_weight,
    output_bias,
    first_gain,
    first_shift,
    widen_weight,
    widen_bias,
    narrow_weight,
    narrow_bias,
    second_gain,
    second_shift,
):
    near, group, width = tokens.shape
    pair = group // 2
    side = lax.axis_index("blk")
    info = device_info()

    away, own = split_rows(tokens, info)
    got = swap(away, "x")
    away_cot, own_cot = split_rows(cotangent, info)
    got_cot = swap(away_cot, "x")
    vectors = jnp.stack(
        [
            query_bias,
            value_bias,
            output_bias,
            first_gain,
            first_shift,
            narrow_bias,
            second_gain,
            second_shift,
        ]
    ).astype(FULL)
    time_code = sinusoid(
        lax.dynamic_slice_in_dim(timesteps, side * pair, pair, 0), time_weight.shape[0]
    ).astype(LOW)
    embed = jnp.dot(time_code, time_weight, preferred_element_type=FULL) + time_bias.astype(FULL)

    vectors = lay_out(
        vectors, (mixing_weight, output_weight, widen_weight, narrow_weight), away_cot
    )
    left, packed, probs, centred, inverse, norm_low = attend(
        own, got, embed[:, None], mixing_weight, output_weight, vectors
    )
    (act_low, slope, out_own, out_away, second_grad, shrink_low, sums_two) = feed(
        norm_low,
        centred,
        widen_weight,
        widen_bias.astype(FULL)[None],
        narrow_weight,
        vectors,
        own_cot,
        got_cot,
        info,
        boundary,
        importance,
    )
    expand_tall, mixing_tall = len(EXPAND_ORDERS), len(MIXING_ORDERS)
    shrink_of = (SHRINK_ORDERS, lambda t: t, lambda t: 0)
    expand_of = (EXPAND_ORDERS, lambda t: t % expand_tall, lambda t: t // expand_tall)
    mixing_of = (
        MIXING_ORDERS,
        lambda t: t % mixing_tall + mixing_tall * (t // (3 * mixing_tall)),
        lambda t: t // mixing_tall,
    )

    def send_half(left, right, of):
        return weight_half(left, right, info, *of)

    def keep_half(left, right, got, of):
        found = weight_half(left, right, info, *of, got=got)
        return found[:-1], found[-1]

    line = Order()
    v = SimpleNamespace()
    done = {}

    def event(name):
        if name == S_SEND:
            v.s_away = line.run(partial(send_half, of=shrink_of), act_low, shrink_low)
            v.s_got = swap(v.s_away, "c")
            v.out_got = swap(out_away, "x")
        elif name == FEED_BACK:
            v.pre_low, v.expand_bias, v.first_grad, v.attn_low, v.sums_one = line.run(
                    feed_back, shrink_low, second_grad, slope, centred, inverse, widen_weight,
                    narrow_weight, vectors, token=4
                )
        elif name == S_KEEP:
            found = line.run(
                partial(keep_half, of=shrink_of), act_low, shrink_low, v.s_got, token=1
            )
            line.begin(S, flow(SHRINK_ORDERS, *found))
        elif name == E_SEND:
            v.e_away = line.run(partial(send_half, of=expand_of), norm_low, v.pre_low)
            v.e_got = swap(v.e_away, "c")
        elif name == E_KEEP:
            found = line.run(
                partial(keep_half, of=expand_of), norm_low, v.pre_low, v.e_got, token=1
            )
            line.begin(E, flow(EXPAND_ORDERS, *found[:-1], found[-1], lambda: v.rider))
        elif name == ATTEND_BACK:
            v.right, v.sums_zero = line.run(attend_back, v.attn_low, packed, probs, output_weight, token=1)
        elif name == M_SEND:
            v.m_away = line.run(partial(send_half, of=mixing_of), left, v.right)
            v.m_got = swap(v.m_away, "c")
        elif name == HIDDEN_BACK:
            v.grad_own, v.grad_away, v.time_total = line.run(
                    partial(hidden_back, pair=pair), v.right, v.first_grad, mixing_weight,
                    token=2
                )
            v.grad_got = swap(v.grad_away, "x")
            v.rider = Rider(
                line.run(
                    pack_small, v.sums_zero, v.sums_one, sums_two, v.expand_bias,
                    v.time_total, time_code
                )
            )
        elif name == M_KEEP:
            found = line.run(
                partial(keep_half, of=mixing_of), left, v.right, v.m_got, token=1
            )
            line.begin(M, flow(MIXING_ORDERS, *found))
        elif name == OUT_GOT:
            (v.out_got,) = line.after(v.out_got)
            line.token = v.out_got
        elif name == GRAD_GOT:
            (v.grad_got,) = line.after(v.grad_got)
            line.token = v.grad_got
        elif name == OUT_JOIN:
            v.output = line.run(partial(join_rows, info=info), out_own, v.out_got)
        elif name == GRAD_JOIN:
            v.input_grad = line.run(partial(join_rows, info=info), v.grad_own, v.grad_got)
        elif name == M_NEAR:
            v.mixed = line.run(
                lambda near: widen_half(near, info, MIXING_ORDERS, True), line.sent[M]
            )
        elif name == UNPACK:
            sums, weight, bias = line.run(
                partial(unpack_small, pair=pair, code_width=time_code.shape[1]), v.rider.packed
            )
            vectors_out = [sums[k] for k in range(8)] + [sums[8:12].reshape(-1), bias[0]]
            v.small = lax.optimization_barrier((weight,) + tuple(vectors_out))
            line.token = v.small[1]
        elif name == S_WIDEN:
            v.shrink = line.run(
                lambda near, far: widen_out(near, far, info, SHRINK_ORDERS, 0, 4 * len(SHRINK_ORDERS), 1),
                *done[S]
            )
        elif name == E_WIDEN:
            v.expand = line.run(
                lambda near, far: widen_out(near, far, info, EXPAND_ORDERS, 0, 4 * expand_tall, 4),
                *done[E]
            )
        else:
            done[name] = line.advance(name)

    for name in SEQUENCE:
        event(name)
    time_weight_grad, *sums, time_bias_grad = v.small
    mixing_grad, output_grad = widen_half(
        done[M][1], info, MIXING_ORDERS, False, v.mixed
    )
    return (
        v.output,
        v.input_grad,
        time_weight_grad,
        time_bias_grad,
        mixing_grad,
        sums[0],
        sums[1],
        output_grad,
        sums[2],
        sums[3],
        sums[4],
        v.expand,
        sums[8],
        v.shrink,
        sums[5],
        sums[6],
        sums[7],
    )


SEQUENCE = (
    S_SEND, FEED_BACK, S_KEEP, OUT_GOT, ATTEND_BACK, E_SEND, S, M_SEND, E_KEEP, HIDDEN_BACK,
    M_KEEP, S, E, S, M, S, E, S, M, E, GRAD_GOT, S, M, E, E, M, OUT_JOIN, M, E, S, GRAD_JOIN, S,
    S_WIDEN, M, E, E, E_WIDEN, UNPACK, M, M_NEAR, M,
)


def solution(mesh):
    pairs = mesh.shape["blk"] == 2 and mesh.shape["dp"] == 16
    return jax.shard_map(
        pair_shards if pairs else general_shards,
        mesh=mesh,
        in_specs=(
            P("blk", "dp", None),
            P("dp"),
            P("dp"),
            P("dp"),
            P("blk", "dp", None),
            P(),
            P(),
            P(),
            P(),
            P(),
            P(),
            P(),
            P(),
            P(),
            P(),
            P(),
            P(),
            P(),
            P(),
            P(),
        ),
        out_specs=(
            P("blk", "dp", None),
            P("blk", "dp", None),
            P(),
            P(),
            P(),
            P(),
            P(),
            P(),
            P(),
            P(),
            P(),
            P(),
            P(),
            P(),
            P(),
            P(),
            P(),
        ),
        check_vma=False,
    )
```

```python
from functools import partial
import math
from types import SimpleNamespace

import jax
import jax.numpy as jnp
from jax import lax
from jax.experimental import pallas as pl
from jax.experimental.pallas import tpu as pltpu
from jax.sharding import PartitionSpec as P

HEADS = 12
HEAD = 64


epsilon = 1e-05


def sinusoid(step_ids, code_width):
    half_width = code_width // 2
    frequency = jnp.exp(-math.log(10000.0) * jnp.arange(half_width, dtype=jnp.float32) / half_width)
    angles = step_ids.astype(jnp.float32)[:, None] * frequency[None, :]
    return jnp.concatenate([jnp.cos(angles), jnp.sin(angles)], axis=-1)


def layer_norm(inputs, norm_gain, norm_shift):
    centred = inputs - jnp.mean(inputs, axis=-1, keepdims=True)
    variance = jnp.mean(centred * centred, axis=-1, keepdims=True)
    return centred * lax.rsqrt(variance + epsilon) * norm_gain + norm_shift


def reduce_dp(parts):
    shares = (
        lax.psum_scatter(
            parts[0].astype(jnp.bfloat16), "dp", scatter_dimension=1, tiled=True
        ).astype(jnp.float32),
        lax.psum_scatter(
            parts[1].astype(jnp.bfloat16), "dp", scatter_dimension=0, tiled=True
        ).astype(jnp.float32),
        lax.psum_scatter(
            parts[2].astype(jnp.bfloat16), "dp", scatter_dimension=0, tiled=True
        ).astype(jnp.float32),
        lax.psum_scatter(
            parts[3].astype(jnp.bfloat16), "dp", scatter_dimension=0, tiled=True
        ).astype(jnp.float32),
        lax.psum_scatter(
            parts[4].astype(jnp.bfloat16), "dp", scatter_dimension=0, tiled=True
        ).astype(jnp.float32),
        lax.psum_scatter(
            parts[5].astype(jnp.bfloat16), "dp", scatter_dimension=0, tiled=True
        ).astype(jnp.float32),
        lax.psum_scatter(
            parts[6].astype(jnp.bfloat16), "dp", scatter_dimension=0, tiled=True
        ).astype(jnp.float32),
        lax.psum_scatter(
            parts[7].astype(jnp.bfloat16), "dp", scatter_dimension=0, tiled=True
        ).astype(jnp.float32),
        lax.psum_scatter(
            parts[8].astype(jnp.bfloat16), "dp", scatter_dimension=0, tiled=True
        ).astype(jnp.float32),
        lax.psum_scatter(
            parts[9].astype(jnp.bfloat16), "dp", scatter_dimension=0, tiled=True
        ).astype(jnp.float32),
        lax.psum_scatter(
            parts[10].astype(jnp.bfloat16), "dp", scatter_dimension=0, tiled=True
        ).astype(jnp.float32),
        lax.psum_scatter(
            parts[11].astype(jnp.bfloat16), "dp", scatter_dimension=0, tiled=True
        ).astype(jnp.float32),
        lax.psum_scatter(
            parts[12].astype(jnp.bfloat16), "dp", scatter_dimension=0, tiled=True
        ).astype(jnp.float32),
        lax.psum_scatter(
            parts[13].astype(jnp.bfloat16), "dp", scatter_dimension=0, tiled=True
        ).astype(jnp.float32),
        lax.psum_scatter(
            parts[14].astype(jnp.bfloat16), "dp", scatter_dimension=0, tiled=True
        ).astype(jnp.float32),
    )
    summed = (
        lax.psum(shares[0].astype(jnp.bfloat16), "blk").astype(jnp.float32),
        lax.psum(shares[1].astype(jnp.bfloat16), "blk").astype(jnp.float32),
        lax.psum(shares[2].astype(jnp.bfloat16), "blk").astype(jnp.float32),
        lax.psum(shares[3].astype(jnp.bfloat16), "blk").astype(jnp.float32),
        lax.psum(shares[4].astype(jnp.bfloat16), "blk").astype(jnp.float32),
        lax.psum(shares[5].astype(jnp.bfloat16), "blk").astype(jnp.float32),
        lax.psum(shares[6].astype(jnp.bfloat16), "blk").astype(jnp.float32),
        lax.psum(shares[7].astype(jnp.bfloat16), "blk").astype(jnp.float32),
        lax.psum(shares[8].astype(jnp.bfloat16), "blk").astype(jnp.float32),
        lax.psum(shares[9].astype(jnp.bfloat16), "blk").astype(jnp.float32),
        lax.psum(shares[10].astype(jnp.bfloat16), "blk").astype(jnp.float32),
        lax.psum(shares[11].astype(jnp.bfloat16), "blk").astype(jnp.float32),
        lax.psum(shares[12].astype(jnp.bfloat16), "blk").astype(jnp.float32),
        lax.psum(shares[13].astype(jnp.bfloat16), "blk").astype(jnp.float32),
        lax.psum(shares[14].astype(jnp.bfloat16), "blk").astype(jnp.float32),
    )
    return (
        lax.all_gather(summed[0].astype(jnp.bfloat16), "dp", axis=1, tiled=True).astype(
            jnp.float32
        ),
        lax.all_gather(summed[1].astype(jnp.bfloat16), "dp", axis=0, tiled=True).astype(
            jnp.float32
        ),
        lax.all_gather(summed[2].astype(jnp.bfloat16), "dp", axis=0, tiled=True).astype(
            jnp.float32
        ),
        lax.all_gather(summed[3].astype(jnp.bfloat16), "dp", axis=0, tiled=True).astype(
            jnp.float32
        ),
        lax.all_gather(summed[4].astype(jnp.bfloat16), "dp", axis=0, tiled=True).astype(
            jnp.float32
        ),
        lax.all_gather(summed[5].astype(jnp.bfloat16), "dp", axis=0, tiled=True).astype(
            jnp.float32
        ),
        lax.all_gather(summed[6].astype(jnp.bfloat16), "dp", axis=0, tiled=True).astype(
            jnp.float32
        ),
        lax.all_gather(summed[7].astype(jnp.bfloat16), "dp", axis=0, tiled=True).astype(
            jnp.float32
        ),
        lax.all_gather(summed[8].astype(jnp.bfloat16), "dp", axis=0, tiled=True).astype(
            jnp.float32
        ),
        lax.all_gather(summed[9].astype(jnp.bfloat16), "dp", axis=0, tiled=True).astype(
            jnp.float32
        ),
        lax.all_gather(summed[10].astype(jnp.bfloat16), "dp", axis=0, tiled=True).astype(
            jnp.float32
        ),
        lax.all_gather(summed[11].astype(jnp.bfloat16), "dp", axis=0, tiled=True).astype(
            jnp.float32
        ),
        lax.all_gather(summed[12].astype(jnp.bfloat16), "dp", axis=0, tiled=True).astype(
            jnp.float32
        ),
        lax.all_gather(summed[13].astype(jnp.bfloat16), "dp", axis=0, tiled=True).astype(
            jnp.float32
        ),
        lax.all_gather(summed[14].astype(jnp.bfloat16), "dp", axis=0, tiled=True).astype(
            jnp.float32
        ),
    )


def general_shards(
    tokens,
    timesteps,
    boundary,
    importance,
    cotangent,
    time_weight,
    time_bias,
    mixing_weight,
    query_bias,
    value_bias,
    output_weight,
    output_bias,
    first_gain,
    first_shift,
    widen_weight,
    widen_bias,
    narrow_weight,
    narrow_bias,
    second_gain,
    second_shift,
):
    model_width = tokens.shape[2]
    score_scale = 1.0 / math.sqrt(HEAD)
    inputs, upstream = (tokens, cotangent)
    step_ids, bounds, weights = (timesteps, boundary, importance)
    offset = lax.axis_index("blk") * tokens.shape[0]
    row_count = inputs.shape[0]
    group_count = inputs.shape[1]
    time_code = sinusoid(step_ids, time_weight.shape[0]).astype(jnp.bfloat16)
    time_embed = jnp.dot(
        time_code, time_weight, preferred_element_type=jnp.float32
    ) + time_bias.astype(jnp.float32)
    hidden = inputs.astype(jnp.float32) + time_embed[None]
    hidden_low = hidden.astype(jnp.bfloat16)
    bias_pack = jnp.concatenate(
        [
            query_bias.astype(jnp.float32),
            jnp.zeros((model_width,), jnp.float32),
            value_bias.astype(jnp.float32),
        ]
    )
    packed = (
        jnp.einsum("lsd,de->lse", hidden_low, mixing_weight, preferred_element_type=jnp.float32)
        + bias_pack
    ).astype(jnp.bfloat16)
    queries = packed[..., :model_width].reshape(row_count, group_count, HEADS, HEAD)
    keys_values = packed[..., model_width:]
    both_all = lax.all_gather(keys_values, "blk", axis=0, tiled=True)
    total_rows = both_all.shape[0]
    keys_all = both_all[..., :model_width].reshape(total_rows, group_count, HEADS, HEAD)
    values_all = both_all[..., model_width:].reshape(total_rows, group_count, HEADS, HEAD)
    scores = (
        jnp.einsum("qshe,kshe->shqk", queries, keys_all, preferred_element_type=jnp.float32)
        * score_scale
    )
    row_peak = jnp.max(scores, axis=-1, keepdims=True)
    powered = jnp.exp(scores - row_peak)
    totals_soft = jnp.sum(powered, axis=-1, keepdims=True)
    probs_low = (powered / totals_soft).astype(jnp.bfloat16)
    log_total = row_peak + jnp.log(totals_soft)
    context = jnp.einsum(
        "shqk,kshe->qshe", probs_low, values_all, preferred_element_type=jnp.float32
    )
    context_low = context.reshape(row_count, group_count, model_width).astype(jnp.bfloat16)
    gain_one = first_gain.astype(jnp.float32)
    shift_one = first_shift.astype(jnp.float32)
    gain_two = second_gain.astype(jnp.float32)
    shift_two = second_shift.astype(jnp.float32)
    first_sum = (
        hidden
        + jnp.einsum("lsd,de->lse", context_low, output_weight, preferred_element_type=jnp.float32)
        + output_bias.astype(jnp.float32)
    )
    leading_norm, first_back = jax.vjp(layer_norm, first_sum, gain_one, shift_one)
    norm_reduced = leading_norm.astype(jnp.bfloat16)
    before_activation = jnp.einsum(
        "ikg,gv->ikv", norm_reduced, widen_weight, preferred_element_type=jnp.float32
    ) + widen_bias.astype(jnp.float32)
    activated, gelu_back = jax.vjp(partial(jax.nn.gelu, approximate=False), before_activation)
    activation_reduced = activated.astype(jnp.bfloat16)
    residual_sum = (
        leading_norm
        + jnp.einsum(
            "ema,aw->emw", activation_reduced, narrow_weight, preferred_element_type=jnp.float32
        )
        + narrow_bias.astype(jnp.float32)
    )
    out_full, second_back = jax.vjp(layer_norm, residual_sum, gain_two, shift_two)
    output = out_full.astype(jnp.bfloat16)
    positions = jnp.arange(row_count, dtype=jnp.int32) + offset
    row_weight = jnp.where(positions[:, None] >= bounds[None, :], weights[None, :], 0.0)
    out_grad = upstream.astype(jnp.float32) * row_weight[:, :, None]
    second_grad, second_gain_grad, second_shift_grad = second_back(out_grad)
    shrink_bias_grad = jnp.sum(second_grad, axis=(0, 1))
    narrow_reduced = second_grad.astype(jnp.bfloat16)
    shrink_weight_grad = jnp.einsum(
        "egk,egy->ky", activation_reduced, narrow_reduced, preferred_element_type=jnp.float32
    )
    act_grad = jnp.einsum(
        "ztv,ov->zto", narrow_reduced, narrow_weight, preferred_element_type=jnp.float32
    )
    pre_grad = gelu_back(act_grad)[0]
    expand_bias_grad = jnp.sum(pre_grad, axis=(0, 1))
    before_reduced = pre_grad.astype(jnp.bfloat16)
    expand_weight_grad = jnp.einsum(
        "thk,thr->kr", norm_reduced, before_reduced, preferred_element_type=jnp.float32
    )
    norm_grad = second_grad + jnp.einsum(
        "xcu,pu->xcp", before_reduced, widen_weight, preferred_element_type=jnp.float32
    )
    first_grad, first_gain_grad, first_shift_grad = first_back(norm_grad)
    output_bias_grad = jnp.sum(first_grad, axis=(0, 1))
    attn_low = first_grad.astype(jnp.bfloat16)
    output_weight_grad = jnp.einsum(
        "lsd,lse->de", context_low, attn_low, preferred_element_type=jnp.float32
    )
    context_grad = jnp.einsum(
        "lse,de->lsd", attn_low, output_weight, preferred_element_type=jnp.float32
    )
    context_grad = context_grad.astype(jnp.bfloat16).reshape(row_count, group_count, HEADS, HEAD)
    again = (
        jnp.einsum("qshe,kshe->shqk", queries, keys_all, preferred_element_type=jnp.float32)
        * score_scale
    )
    soft_probs = jnp.exp(again - log_total)
    prob_grad = jnp.einsum(
        "qshe,kshe->shqk", context_grad, values_all, preferred_element_type=jnp.float32
    )
    row_dot = jnp.sum(soft_probs * prob_grad, axis=-1, keepdims=True)
    score_low = (soft_probs * (prob_grad - row_dot)).astype(jnp.bfloat16)
    query_grad = (
        jnp.einsum("shqk,kshe->qshe", score_low, keys_all, preferred_element_type=jnp.float32)
        * score_scale
    )
    query_every, cgrad_every = (
        lax.all_gather(queries, "blk", axis=0, tiled=True),
        lax.all_gather(context_grad, "blk", axis=0, tiled=True),
    )
    total_every, dot_every = (
        lax.all_gather(log_total, "blk", axis=2, tiled=True),
        lax.all_gather(row_dot, "blk", axis=2, tiled=True),
    )
    own_keys = packed[..., model_width : 2 * model_width].reshape(
        row_count, group_count, HEADS, HEAD
    )
    own_values = packed[..., 2 * model_width :].reshape(row_count, group_count, HEADS, HEAD)
    local_scores = (
        jnp.einsum("qshe,kshe->shqk", query_every, own_keys, preferred_element_type=jnp.float32)
        * score_scale
    )
    local_probs = jnp.exp(local_scores - total_every)
    local_low = local_probs.astype(jnp.bfloat16)
    local_grad = jnp.einsum(
        "qshe,kshe->shqk", cgrad_every, own_values, preferred_element_type=jnp.float32
    )
    local_score_low = (local_probs * (local_grad - dot_every)).astype(jnp.bfloat16)
    value_own = jnp.einsum(
        "shqk,qshe->kshe", local_low, cgrad_every, preferred_element_type=jnp.float32
    )
    key_own = (
        jnp.einsum(
            "shqk,qshe->kshe", local_score_low, query_every, preferred_element_type=jnp.float32
        )
        * score_scale
    )
    key_here = jnp.concatenate(
        [
            key_own.reshape(row_count, group_count, model_width),
            value_own.reshape(row_count, group_count, model_width),
        ],
        axis=-1,
    )
    packed_grad = jnp.concatenate(
        [query_grad.reshape(row_count, group_count, model_width), key_here], axis=-1
    )
    query_bias_grad = jnp.sum(packed_grad[..., :model_width], axis=(0, 1))
    value_bias_grad = jnp.sum(packed_grad[..., 2 * model_width :], axis=(0, 1))
    packed_low = packed_grad.astype(jnp.bfloat16)
    mixing_weight_grad = jnp.einsum(
        "lsd,lse->de", hidden_low, packed_low, preferred_element_type=jnp.float32
    )
    hidden_grad = first_grad + jnp.einsum(
        "lse,de->lsd", packed_low, mixing_weight, preferred_element_type=jnp.float32
    )
    input_grad = hidden_grad.astype(jnp.bfloat16)
    time_total = jnp.sum(hidden_grad, axis=0)
    time_bias_grad = jnp.sum(time_total, axis=0)
    time_weight_grad = jnp.dot(
        time_code.astype(jnp.float32).T, time_total, precision=lax.Precision.HIGHEST
    )
    parts = (
        time_weight_grad,
        time_bias_grad,
        mixing_weight_grad,
        query_bias_grad,
        value_bias_grad,
        output_weight_grad,
        output_bias_grad,
        first_gain_grad,
        first_shift_grad,
        expand_weight_grad,
        expand_bias_grad,
        shrink_weight_grad,
        shrink_bias_grad,
        second_gain_grad,
        second_shift_grad,
    )
    summed = reduce_dp(parts)
    return (
        output,
        input_grad,
        summed[0],
        summed[1],
        summed[2],
        summed[3],
        summed[4],
        summed[5],
        summed[6],
        summed[7],
        summed[8],
        summed[9],
        summed[10],
        summed[11],
        summed[12],
        summed[13],
        summed[14],
    )


LOW = jnp.bfloat16
FULL = jnp.float32
PLACES = {"c": ("dp", 1), "y": ("dp", 2), "z": ("dp", 4), "w": ("dp", 8), "x": ("blk", 1)}
SHRINK_ORDERS = (("zxy", "xyz"),)
EXPAND_ORDERS = (("zxy", "xyz"),)
MIXING_ORDERS = (("xyz", "yxz"),)
ALL_ORDERS = tuple(dict.fromkeys(SHRINK_ORDERS + EXPAND_ORDERS + MIXING_ORDERS))
CORE, SIDE, NUMBERS = 0, 1, 2
WIDTH = 768
GRAD_ROWS = 3072


def swap(value, places):
    count = {axis: lax.axis_size(axis) for axis in ("dp", "blk")}
    pairs = []
    for group in range(count["dp"]):
        for side in range(count["blk"]):
            axis, bit = PLACES[places[group % 2 if len(places) == 2 else 0]]
            there = (group ^ bit, side) if axis == "dp" else (group, side ^ bit)
            pairs.append((group * count["blk"] + side, there[0] * count["blk"] + there[1]))
    return lax.ppermute(value, ("dp", "blk"), pairs)


def place_bit(place):
    axis, bit = PLACES[place]
    return (lax.axis_index(axis) // bit) % 2


def device_info():
    core = place_bit("c")
    own, other = [], []
    for orders in ALL_ORDERS:
        both = []
        for order in orders:
            number = 0
            for place in order:
                number = number * 2 + place_bit(place)
            both.append(number)
        own.append(jnp.where(core == 0, both[0], both[1]))
        other.append(jnp.where(core == 0, both[1], both[0]))
    return jnp.stack([core, lax.axis_index("blk")] + own + other).astype(jnp.int32)


def order_number(info_ref, orders, unit, mine):
    places = [NUMBERS + ALL_ORDERS.index(o) + (0 if mine else len(ALL_ORDERS)) for o in orders]
    number = info_ref[places[0]]
    for k in range(1, len(orders)):
        number = jnp.where(unit == k, info_ref[places[k]], number)
    return number


def weight_half(left, right, info, orders, left_of, right_of, got=None):
    units = len(orders)
    block = GRAD_ROWS // units // 16
    tile_rows = 4 * block
    mine = got is not None

    def body(info_ref, left_ref, right_ref, *refs):
        core = info_ref[CORE]
        side = core if mine else 1 - core
        for step in range(2 * units):
            unit, part = step // 2, step % 2
            tile = 4 * unit + 2 * side + part
            number = order_number(info_ref, orders, unit, mine)
            column = pl.multiple_of(left_of(tile) * tile_rows, 128)
            place = pl.multiple_of(right_of(tile) * WIDTH, 128)
            product = turned_times(
                left_ref[:, pl.ds(column, tile_rows)], right_ref[:, pl.ds(place, WIDTH)]
            )
            spots = [((4 * part + i) ^ number) & 7 for i in range(4)]
            rows = [pl.multiple_of((8 * unit + spot) * block, 16) for spot in spots]
            pieces = [product[i * block : (i + 1) * block, :] for i in range(4)]
            if not mine:
                for row, piece in zip(rows, pieces):
                    refs[0][pl.ds(row, block), :] = piece.astype(LOW)
                continue
            got_ref, upper_ref, lower_ref = refs[0], refs[1 + unit], refs[-1]
            pieces = [
                (piece + got_ref[pl.ds(row, block), :].astype(FULL)).astype(LOW)
                for row, piece in zip(rows, pieces)
            ]
            upper = part ^ ((number // 4) % 2)

            @pl.when(upper == 0)
            def _(pieces=pieces, spots=spots, lower_ref=lower_ref, unit=unit):
                for spot, piece in zip(spots, pieces):
                    row = pl.multiple_of((4 * unit + (spot & 3)) * block, 16)
                    lower_ref[pl.ds(row, block), :] = piece

            @pl.when(upper == 1)
            def _(pieces=pieces, spots=spots, upper_ref=upper_ref):
                for spot, piece in zip(spots, pieces):
                    row = pl.multiple_of((spot & 3) * block, 16)
                    upper_ref[pl.ds(row, block), :] = piece

    rows = left.shape[0]
    counts = [4 * block] * units + [4 * units * block] if mine else [8 * units * block]
    vmem = pl.BlockSpec(memory_space=pltpu.VMEM)
    found = pl.pallas_call(
        body,
        in_specs=[pl.BlockSpec(memory_space=pltpu.SMEM)] + [vmem] * (3 if mine else 2),
        out_specs=[vmem] * len(counts),
        out_shape=[jax.ShapeDtypeStruct((c, WIDTH), LOW) for c in counts],
        compiler_params=kernel_params(),
        cost_estimate=cost(2.8),
    )(info, left, right, *([got] if mine else []))
    return found if mine else found[0]


def widen_out(near, far, info, orders, first_tile, tile_count, columns):
    units = len(orders)
    block = GRAD_ROWS // units // 16
    part = 64 if block % 64 == 0 else block
    tall = 4 * block * tile_count // columns
    pieces = 4 if columns == 1 else 1
    start = 4 * first_tile * block

    def body(info_ref, near_ref, far_ref, out_ref):
        step = pl.program_id(0)
        for column in range(columns):
            for piece in range(pieces):
                first = start + column * tall + (step * pieces + piece) * part
                index = first // block
                unit = index // 16
                own = (index % 16) // 8 == info_ref[CORE]
                rows = []
                for mine in (True, False):
                    number = order_number(info_ref, orders, unit, mine)
                    row = (unit * 8 + ((index ^ number) & 7)) * block + first % block
                    rows.append(pl.multiple_of(row, 16))
                near_row, far_row = rows
                target = (
                    slice(piece * part, (piece + 1) * part),
                    slice(column * WIDTH, (column + 1) * WIDTH),
                )

                @pl.when(own)
                def _(row=near_row, target=target):
                    out_ref[target] = near_ref[pl.ds(row, part), :].astype(FULL)

                @pl.when(jnp.logical_not(own))
                def _(row=far_row, target=target):
                    out_ref[target] = far_ref[pl.ds(row, part), :].astype(FULL)

    whole = pl.BlockSpec(near.shape, lambda t, p: (0, 0), pipeline_mode=ONE)
    return pl.pallas_call(
        body,
        grid_spec=pltpu.PrefetchScalarGridSpec(
            num_scalar_prefetch=1,
            grid=(tall // (pieces * part),),
            in_specs=[whole, whole],
            out_specs=pl.BlockSpec((pieces * part, columns * WIDTH), lambda t, p: (t, 0)),
        ),
        out_shape=jax.ShapeDtypeStruct((tall, columns * WIDTH), FULL),
        compiler_params=kernel_params(),
        cost_estimate=cost(6.0, 60),
    )(info, near, far)


def widen_half(source, info, orders, mine, base=None):
    units = len(orders)
    block = GRAD_ROWS // units // 16
    count = 8 * units

    def body(info_ref, source_ref, *refs):
        mix_ref, out_ref, stage_ref, sems = refs[-4:]
        core = info_ref[CORE]
        half = core if mine else 1 - core
        moves = []
        for k in range(count):
            unit, spot = k // 8, k % 8
            number = order_number(info_ref, orders, unit, mine)
            first = (16 * unit + 8 * half + (spot ^ (number & 7))) * block
            matrix = first // WIDTH
            row = pl.multiple_of(first % WIDTH, 16)
            column = pl.multiple_of(jnp.minimum(matrix, 2) * WIDTH, 128)
            here = slice(k * block, (k + 1) * block)
            stage_ref[here, :] = source_ref[here, :].astype(FULL)
            mixed = pltpu.make_async_copy(
                stage_ref.at[here, :],
                mix_ref.at[pl.ds(row, block), pl.ds(column, WIDTH)],
                sems.at[k],
            )
            output = pltpu.make_async_copy(
                stage_ref.at[here, :], out_ref.at[pl.ds(row, block), :], sems.at[k]
            )
            moves.append((matrix, mixed, output))
            pl.when(matrix < 3)(mixed.start)
            pl.when(matrix >= 3)(output.start)
        for matrix, mixed, output in moves:
            pl.when(matrix < 3)(mixed.wait)
            pl.when(matrix >= 3)(output.wait)

    hbm = pl.BlockSpec(memory_space=pltpu.HBM)
    operands = [info, source] + ([] if base is None else list(base))
    return pl.pallas_call(
        body,
        in_specs=[
            pl.BlockSpec(memory_space=pltpu.SMEM),
            pl.BlockSpec(memory_space=pltpu.VMEM),
        ]
        + [hbm] * (len(operands) - 2),
        out_specs=[hbm, hbm],
        out_shape=[
            jax.ShapeDtypeStruct((WIDTH, 3 * WIDTH), FULL),
            jax.ShapeDtypeStruct((WIDTH, WIDTH), FULL),
        ],
        scratch_shapes=[
            pltpu.VMEM((count * block, WIDTH), FULL),
            pltpu.SemaphoreType.DMA((count,)),
        ],
        input_output_aliases={} if base is None else {2: 0, 3: 1},
        compiler_params=kernel_params(),
        cost_estimate=cost(3.0, 30),
    )(*operands)


def combine(outputs):
    arrays = []

    def number(array):
        for k, known in enumerate(arrays):
            if known is array:
                return k
        arrays.append(array)
        return len(arrays) - 1

    plan = [
        [[(number(array), row, rows) for array, row, rows in piece] for piece in pieces]
        for pieces in outputs
    ]
    heights = [sum(piece[0][2] for piece in pieces) for pieces in outputs]

    def body(*refs):
        sources, targets = refs[: len(arrays)], refs[len(arrays) :]
        for pieces, target in zip(plan, targets):
            place = 0
            for piece in pieces:
                rows = piece[0][2]
                for first in range(0, rows, 128):
                    count = min(128, rows - first)
                    values = [sources[k][row + first : row + first + count, :] for k, row, _ in piece]
                    total = values[0] if len(values) == 1 else values[0] + values[1]
                    target[place + first : place + first + count, :] = total
                place += rows

    vmem = pl.BlockSpec(memory_space=pltpu.VMEM)
    return pl.pallas_call(
        body,
        in_specs=[vmem] * len(arrays),
        out_specs=[vmem] * len(outputs),
        out_shape=[jax.ShapeDtypeStruct((h, WIDTH), LOW) for h in heights],
        compiler_params=kernel_params(),
        cost_estimate=cost(0.4, 12),
    )(*arrays)


class Rider:
    def __init__(self, packed):
        self.packed = packed
        self.filled = 1

    def rows(self):
        return self.packed.shape[0]

    def pieces(self):
        return [((self.packed, 0, self.rows()),)]

    def take(self, got, row):
        packed, rows, filled = self.packed, self.rows(), self.filled
        if filled >= RIDER_LANES:
            (self.packed,) = combine(
                [
                    [
                        ((packed, 0, 16), (got, row, 16)),
                        ((packed, 16, rows - 16),),
                        ((got, row + 16, rows - 16),),
                    ]
                ]
            )
            return

        def body(packed_ref, got_ref, out_ref):
            out_ref[:16, :] = packed_ref[:16, :] + got_ref[row : row + 16, :]
            out_ref[16:, : filled * 128] = packed_ref[16:, : filled * 128]
            out_ref[16:, filled * 128 : 2 * filled * 128] = got_ref[
                row + 16 : row + 32, : filled * 128
            ]
            out_ref[16:, 2 * filled * 128 :] = packed_ref[16:, 2 * filled * 128 :]

        vmem = pl.BlockSpec(memory_space=pltpu.VMEM)
        self.packed = pl.pallas_call(
            body,
            in_specs=[vmem, vmem],
            out_specs=vmem,
            out_shape=jax.ShapeDtypeStruct(packed.shape, LOW),
            compiler_params=kernel_params(),
            cost_estimate=cost(0.4),
            name="ride",
        )(packed, got)
        self.filled = 2 * filled


def flow(orders, uppers, lower, rider=None):
    units = len(orders)
    size = lower.shape[0] // units
    mine = [(lower, k * size, size) for k in range(units)]

    def cut(view, part):
        array, row, rows = view
        return array, row + part * rows // 2, rows // 2

    def places_at(level):
        return [first[level] + second[level] for first, second in orders]

    got = yield list(zip(places_at(0), uppers))
    for level in (1, 2):
        views = [(g, 0, size) for g in got]
        away = [[(cut(m, 1), cut(v, 1))] for m, v in zip(mine, views)]
        kept = [(cut(m, 0), cut(v, 0)) for m, v in zip(mine, views)]
        size = size // 2
        *sends, rest = combine(away + [kept])
        mine = [(rest, k * size, size) for k in range(units)]
        got = yield list(zip(places_at(level), sends))

    rider = None if rider is None else rider()

    def riding():
        return [] if rider is None else rider.pieces()

    (joined,) = combine([[(m, (g, 0, size)) for m, g in zip(mine, got)] + riding()])
    (other,) = yield [("w", joined)]
    values = combine([[((joined, k * size, size), (other, k * size, size))] for k in range(units)])
    if rider is not None:
        rider.take(other, units * size)
    for level in (2, 1, 0):
        sends = list(values)
        if rider is not None:
            (sends[0],) = combine([[((values[0], 0, size),)] + rider.pieces()])
        got = yield list(zip(places_at(level), sends))
        if rider is not None:
            rider.take(got[0], size)
        pieces = [[((v, 0, size),), ((g, 0, size),)] for v, g in zip(values, got)]
        size = 2 * size
        if level > 0:
            values = combine(pieces)
    (near,) = combine([sum(pieces, []) + riding()])
    (far,) = yield [("c", near)]
    if rider is not None:
        rider.take(far, units * size)
    return near, far


RIDER_LANES = 4


def pack_small(sums_zero, sums_one, sums_two, expand_bias, time_total, time_code):
    pair, code_width = time_code.shape
    width = sums_one.shape[1]
    blocks = width // 128

    def body(zero_ref, one_ref, two_ref, bias_ref, total_ref, code_ref, out_ref):
        bias = [bias_ref[:, k * width : (k + 1) * width] for k in range(4)]
        out_ref[:16, :] = jnp.concatenate(
            [zero_ref[0] + zero_ref[1], one_ref[:3, :], two_ref[:3, :]]
            + bias
            + [jnp.zeros((4, width), FULL)],
            axis=0,
        ).astype(LOW)
        totals = [
            total_ref[s, :, 128 * j : 128 * j + 128] for s in range(pair) for j in range(blocks)
        ]
        codes = code_ref[...].astype(FULL)
        out_ref[16:, :] = jnp.zeros((16, width), LOW)
        out_ref[16:, :128] = jnp.concatenate(
            totals + [codes, jnp.zeros((16 - pair * (blocks + 1), 128), FULL)], axis=0
        ).astype(LOW)

    return pl.pallas_call(
        body,
        out_shape=jax.ShapeDtypeStruct((32, width), LOW),
        compiler_params=kernel_params(),
        cost_estimate=cost(0.6),
    )(sums_zero, sums_one, sums_two, expand_bias, time_total, time_code)


def unpack_small(packed, pair, code_width):
    count, width = packed.shape
    blocks = width // 128
    groups = (count - 16) // 16

    def body(packed_ref, sums_ref, weight_ref, bias_ref, wide_ref):
        sums_ref[...] = packed_ref[:16, :].astype(FULL)
        for lane in range(RIDER_LANES):
            wide_ref[lane] = packed_ref[16:, 128 * lane : 128 * lane + 128].astype(FULL)

        def every(row):
            return jnp.concatenate(
                [wide_ref[lane, pl.ds(row, groups, stride=16), :] for lane in range(RIDER_LANES)],
                axis=0,
            )

        codes = [every(pair * blocks + s).astype(LOW) for s in range(pair)]
        for j in range(blocks):
            columns = slice(128 * j, 128 * j + 128)
            totals = [every(s * blocks + j) for s in range(pair)]
            weight_ref[:, columns] = sum(
                turned_times(c, t.astype(LOW)) for c, t in zip(codes, totals)
            )
            bias_ref[:, columns] = jnp.sum(sum(totals), axis=0, keepdims=True)

    return pl.pallas_call(
        body,
        out_shape=[
            jax.ShapeDtypeStruct((16, width), FULL),
            jax.ShapeDtypeStruct((code_width, width), FULL),
            jax.ShapeDtypeStruct((1, width), FULL),
        ],
        scratch_shapes=[pltpu.VMEM((RIDER_LANES, count - 16, 128), FULL)],
        compiler_params=kernel_params(),
        cost_estimate=cost(1.0),
    )(packed)


class Order:
    def __init__(self):
        self.token = None
        self.flows = {}
        self.sent = {}

    def after(self, *values):
        if self.token is None:
            return values
        return lax.optimization_barrier((self.token,) + tuple(values))[1:]

    def run(self, function, *values, token=0):
        found = function(*self.after(*values))
        self.token = found[token] if isinstance(found, (tuple, list)) else found
        return found

    def begin(self, name, steps):
        pairs = next(steps)
        self.flows[name] = steps, [swap(value, place) for place, value in pairs]

    def advance(self, name):
        steps, got = self.flows[name]
        try:
            pairs = steps.send(list(self.after(*got)))
        except StopIteration as stop:
            return stop.value
        self.token = pairs[0][1]
        self.sent[name] = pairs[0][1]
        self.flows[name] = steps, [swap(value, place) for place, value in pairs]
        return None


VMEM_LIMIT = 8 * 1024 * 1024
ONE = pl.Buffered(1)
SCALE = 600000000


def cost(microseconds, megabytes=0):
    return pl.CostEstimate(
        flops=int(microseconds * SCALE),
        bytes_accessed=1 + int(megabytes * 1000000),
        transcendentals=0,
    )


def kernel_params():
    return pltpu.CompilerParams(vmem_limit_bytes=VMEM_LIMIT)


def times(left, right):
    return jnp.dot(left, right, preferred_element_type=FULL)


def times_turned(left, right):
    return lax.dot_general(left, right, (((1,), (1,)), ((), ())), preferred_element_type=FULL)


def turned_times(left, right):
    return lax.dot_general(left, right, (((0,), (0,)), ((), ())), preferred_element_type=FULL)


def split_rows(values, info):
    near, group, width = values.shape
    pair = group // 2
    count = near * group

    def body(info_ref, values_ref, away_ref, own_ref):
        side = info_ref[SIDE]
        rows = values_ref[...].reshape(count, width)
        row = lax.broadcasted_iota(jnp.int32, (count, count), 0)
        column = lax.broadcasted_iota(jnp.int32, (count, count), 1)
        half = pair * near
        first = jnp.where(row < half, pair * (1 - side), pair * side)
        place = jnp.where(row < half, row, row - half)
        source = (place % near) * group + first + place // near
        pick = (source == column).astype(FULL).astype(LOW)
        moved = times(pick, rows).astype(LOW)
        away_ref[...] = moved[:half].reshape(pair, near, width)
        own_ref[...] = moved[half:].reshape(pair, near, width)

    shape = jax.ShapeDtypeStruct((pair, near, width), values.dtype)
    return pl.pallas_call(
        body,
        in_specs=[
            pl.BlockSpec(memory_space=pltpu.SMEM),
            pl.BlockSpec(memory_space=pltpu.VMEM),
        ],
        out_shape=[shape, shape],
        compiler_params=kernel_params(),
        cost_estimate=cost(16.0),
    )(info, values)


def lay_out(vectors, weights, after):
    count = len(weights)

    def body(*refs):
        refs[-1][...] = refs[0][...]

    vmem = pl.BlockSpec(memory_space=pltpu.VMEM)
    return pl.pallas_call(
        body,
        in_specs=[vmem] * (1 + count) + [pl.BlockSpec(memory_space=pl.ANY)],
        out_specs=vmem,
        out_shape=jax.ShapeDtypeStruct(vectors.shape, vectors.dtype),
        compiler_params=kernel_params(),
        cost_estimate=cost(8.0, 60),
    )(vectors, *weights, after)


def join_rows(own, got, info):
    pair, near, width = own.shape
    group = 2 * pair
    count = near * group

    def body(info_ref, own_ref, got_ref, out_ref):
        side = info_ref[SIDE]
        row = lax.broadcasted_iota(jnp.int32, (count, count), 0)
        column = lax.broadcasted_iota(jnp.int32, (count, count), 1)
        half = pair * near
        sequence = row % group
        position = row // group
        from_own = sequence // pair == side
        source = jnp.where(from_own, 0, half) + (sequence % pair) * near + position
        pick = (source == column).astype(FULL).astype(LOW)
        rows = jnp.concatenate(
            [own_ref[...].reshape(half, width), got_ref[...].reshape(half, width)], axis=0
        )
        out_ref[...] = times(pick, rows).astype(LOW).reshape(near, group, width)

    return pl.pallas_call(
        body,
        in_specs=[
            pl.BlockSpec(memory_space=pltpu.SMEM),
            pl.BlockSpec(memory_space=pltpu.VMEM),
            pl.BlockSpec(memory_space=pltpu.VMEM),
        ],
        out_shape=jax.ShapeDtypeStruct((near, group, width), own.dtype),
        compiler_params=kernel_params(),
        cost_estimate=cost(2.0),
    )(info, own, got)


QUERY_BIAS, VALUE_BIAS, OUTPUT_BIAS, FIRST_GAIN, FIRST_SHIFT = range(5)
NARROW_BIAS, SECOND_GAIN, SECOND_SHIFT = range(5, 8)


def head_masks(scale):
    lane = lax.broadcasted_iota(jnp.int32, (1, 2 * HEAD), 1)
    first = jnp.where(lane < HEAD, scale, 0.0).astype(LOW)
    second = jnp.where(lane < HEAD, 0.0, scale).astype(LOW)
    return first, second


def attend(own, got, embed, mixing_weight, output_weight, vectors):
    pair, near, width = own.shape
    length = 2 * near
    scale = 1.0 / math.sqrt(HEAD)
    duo = 2 * HEAD

    def body(own_ref, got_ref, embed_ref, mix_ref, wout_ref, vec_ref, left_ref, packed_ref,
             probs_ref, centred_ref, scale_ref, norm_ref):
        for s in range(pair):
            here = slice(s * length, (s + 1) * length)
            hidden = jnp.concatenate([own_ref[s], got_ref[s]], axis=0).astype(FULL) + embed_ref[s]
            hidden_low = hidden.astype(LOW)
            left_ref[here, :width] = hidden_low
            for part, bias in ((0, QUERY_BIAS), (1, None), (2, VALUE_BIAS)):
                columns = slice(part * width, (part + 1) * width)
                product = times(hidden_low, mix_ref[:, columns])
                if bias is not None:
                    product = product + vec_ref[bias : bias + 1, :]
                packed_ref[here, columns] = product.astype(LOW)
            masks = head_masks(scale)
            lane = lax.broadcasted_iota(jnp.int32, (length, duo), 1)
            for j in range(width // duo):
                query = packed_ref[here, j * duo : (j + 1) * duo]
                key = packed_ref[here, width + j * duo : width + (j + 1) * duo]
                value = packed_ref[here, 2 * width + j * duo : 2 * width + (j + 1) * duo]
                found = []
                for head in range(2):
                    scores = times_turned(query * masks[head], key)
                    peak = jnp.max(scores, axis=-1, keepdims=True)
                    powered = jnp.exp(scores - peak)
                    total = jnp.sum(powered, axis=-1, keepdims=True)
                    low = (powered * (1.0 / total)).astype(LOW)
                    probs_ref[s, 2 * j + head] = low
                    found.append(times(low, value))
                left_ref[here, width + j * duo : width + (j + 1) * duo] = jnp.where(
                    lane < HEAD, found[0], found[1]
                ).astype(LOW)
            first_sum = (
                hidden
                + times(left_ref[here, width:], wout_ref[...])
                + vec_ref[OUTPUT_BIAS : OUTPUT_BIAS + 1, :]
            )
            centred = first_sum - jnp.mean(first_sum, axis=-1, keepdims=True)
            variance = jnp.mean(centred * centred, axis=-1, keepdims=True)
            inverse = lax.rsqrt(variance + epsilon)
            centred = centred * inverse
            centred_ref[here, :] = centred
            scale_ref[here, :] = jnp.broadcast_to(inverse, (length, 128))
            norm_ref[here, :] = (
                centred * vec_ref[FIRST_GAIN : FIRST_GAIN + 1, :]
                + vec_ref[FIRST_SHIFT : FIRST_SHIFT + 1, :]
            ).astype(LOW)

    rows = pair * length
    vmem = pl.BlockSpec(memory_space=pltpu.VMEM)
    return pl.pallas_call(
        body,
        in_specs=[vmem] * 6,
        out_specs=[vmem] * 6,
        out_shape=[
            jax.ShapeDtypeStruct((rows, 2 * width), LOW),
            jax.ShapeDtypeStruct((rows, 3 * width), LOW),
            jax.ShapeDtypeStruct((pair, HEADS, length, length), LOW),
            jax.ShapeDtypeStruct((rows, width), FULL),
            jax.ShapeDtypeStruct((rows, 128), FULL),
            jax.ShapeDtypeStruct((rows, width), LOW),
        ],
        compiler_params=kernel_params(),
        cost_estimate=cost(25.0),
    )(own, got, embed, mixing_weight, output_weight, vectors)


def gelu_parts(value):
    t = 1.0 / (1.0 + (0.3275911 * math.sqrt(0.5)) * jnp.abs(value))
    series = (0.254829592, -0.284496736, 1.421413741, -1.453152027, 1.061405429)
    tail = jnp.full_like(value, 0.5 * series[-1])
    for factor in series[-2::-1]:
        tail = tail * t + 0.5 * factor
    power = jnp.exp(-0.5 * value * value)
    tail = tail * t * power
    return jnp.where(value < 0, tail, 1.0 - tail), power * (1.0 / math.sqrt(2.0 * math.pi))


STRIP = 512
LONG = 128
PART = 768
BACK_PART = 768
UNROLL = 1


def sum_eights(value):
    return jnp.sum(value.reshape(-1, 8, value.shape[-1]), axis=0)


def feed(norm_low, centred, widen_weight, widen_bias, narrow_weight, vectors, own_cot, got_cot,
         info, bounds, weights):
    rows, width = norm_low.shape
    pair, near, _ = own_cot.shape
    length = 2 * near
    inner = widen_weight.shape[1]

    def body(info_ref, bound_ref, weight_ref, norm_ref, centred_ref, wide_ref, wbias_ref, narrow_ref, vec_ref,
             own_ref, got_ref, act_ref, slope_ref, out_own_ref, out_away_ref, grad_ref, low_ref,
             sums_ref, total_ref):
        def widen(k, carry):
            columns = pl.ds(pl.multiple_of(k * PART, 128), PART)
            value = times(norm_ref[...], wide_ref[:, columns]) + wbias_ref[:, columns]
            below, density = gelu_parts(value)
            act_ref[:, columns] = (value * below).astype(LOW)
            slope_ref[:, columns] = (below + value * density).astype(LOW)
            return carry

        lax.fori_loop(0, inner // PART, widen, 0)
        total_ref[...] = times(act_ref[...], narrow_ref[...])
        side = info_ref[SIDE]

        def vector(k):
            return vec_ref[k : k + 1, :]

        zero = jnp.zeros((8, width), FULL)
        sums = (zero, zero, zero)
        for quarter in range(2 * pair):
            sequence, far = quarter // 2, quarter % 2
            cot_ref = got_ref if far else own_ref
            back_ref = out_away_ref if far else out_own_ref
            bound = bound_ref[pair * side + sequence]
            weight = weight_ref[pair * side + sequence]
            start = jnp.where(side == far, 0, near)

            def finish(i, sums, quarter=quarter, sequence=sequence, cot_ref=cot_ref,
                       back_ref=back_ref, bound=bound, weight=weight, start=start):
                inside = pl.multiple_of(i * LONG, LONG)
                row = pl.multiple_of(quarter * near + i * LONG, LONG)
                first_norm = (
                    centred_ref[pl.ds(row, LONG), :] * vector(FIRST_GAIN) + vector(FIRST_SHIFT)
                )
                total = first_norm + total_ref[pl.ds(row, LONG), :] + vector(NARROW_BIAS)
                level = total - jnp.mean(total, axis=-1, keepdims=True)
                inverse = lax.rsqrt(jnp.mean(level * level, axis=-1, keepdims=True) + epsilon)
                level = level * inverse
                back_ref[sequence, pl.ds(inside, LONG), :] = (
                    level * vector(SECOND_GAIN) + vector(SECOND_SHIFT)
                ).astype(LOW)
                place = start + inside + lax.broadcasted_iota(jnp.int32, (LONG, 1), 0)
                factor = jnp.where(place >= bound, weight, 0.0)
                upstream = cot_ref[sequence, pl.ds(inside, LONG), :].astype(FULL) * factor
                gained = upstream * vector(SECOND_GAIN)
                mean = jnp.mean(gained, axis=-1, keepdims=True)
                along = jnp.mean(gained * level, axis=-1, keepdims=True)
                grad = inverse * (gained - mean - level * along)
                grad_ref[pl.ds(row, LONG), :] = grad
                low_ref[pl.ds(row, LONG), :] = grad.astype(LOW)
                return (
                    sums[0] + sum_eights(grad),
                    sums[1] + sum_eights(upstream * level),
                    sums[2] + sum_eights(upstream),
                )

            sums = lax.fori_loop(0, near // LONG, finish, sums)
        sums_ref[...] = jnp.concatenate(
            [jnp.sum(v, axis=0, keepdims=True) for v in sums] + [jnp.zeros((5, width), FULL)],
            axis=0,
        )

    half = (pair, near, width)
    smem = pl.BlockSpec(memory_space=pltpu.SMEM)
    vmem = pl.BlockSpec(memory_space=pltpu.VMEM)
    return pl.pallas_call(
        body,
        in_specs=[smem] * 3 + [vmem] * 8,
        out_specs=[vmem] * 7,
        scratch_shapes=[pltpu.VMEM((rows, width), FULL)],
        out_shape=[
            jax.ShapeDtypeStruct((rows, inner), LOW),
            jax.ShapeDtypeStruct((rows, inner), LOW),
            jax.ShapeDtypeStruct(half, LOW),
            jax.ShapeDtypeStruct(half, LOW),
            jax.ShapeDtypeStruct((rows, width), FULL),
            jax.ShapeDtypeStruct((rows, width), LOW),
            jax.ShapeDtypeStruct((8, width), FULL),
        ],
        compiler_params=kernel_params(),
        cost_estimate=cost(40.0),
    )(info, bounds, weights, norm_low, centred, widen_weight, widen_bias, narrow_weight, vectors,
      own_cot, got_cot)


def feed_back(shrink_low, second_grad, slope, centred, inverse, widen_weight, narrow_weight, vectors):
    rows, width = shrink_low.shape
    inner = slope.shape[1]

    def body(low_ref, grad_ref, slope_ref, centred_ref, inverse_ref, wide_ref, narrow_ref, vec_ref,
             pre_ref, bias_ref, first_ref, attn_ref, sums_ref, total_ref):
        total = None
        for c in range(0, inner, BACK_PART):
            columns = slice(c, c + BACK_PART)
            value = times_turned(low_ref[...], narrow_ref[columns, :])
            value = value * slope_ref[:, columns].astype(FULL)
            low = value.astype(LOW)
            pre_ref[:, columns] = low
            bias_ref[:, columns] = jnp.sum(sum_eights(value), axis=0, keepdims=True)
            term = times_turned(low, wide_ref[:, columns])
            total = term if total is None else total + term
        total_ref[...] = total
        gain = vec_ref[FIRST_GAIN : FIRST_GAIN + 1, :]

        def finish(i, sums):
            row = pl.multiple_of(i * LONG, LONG)
            upstream = grad_ref[pl.ds(row, LONG), :] + total_ref[pl.ds(row, LONG), :]
            level = centred_ref[pl.ds(row, LONG), :]
            gained = upstream * gain
            mean = jnp.mean(gained, axis=-1, keepdims=True)
            along = jnp.mean(gained * level, axis=-1, keepdims=True)
            grad = inverse_ref[pl.ds(row, LONG), :1] * (gained - mean - level * along)
            first_ref[pl.ds(row, LONG), :] = grad
            attn_ref[pl.ds(row, LONG), :] = grad.astype(LOW)
            return (
                sums[0] + sum_eights(grad),
                sums[1] + sum_eights(upstream * level),
                sums[2] + sum_eights(upstream),
            )

        zero = jnp.zeros((8, width), FULL)
        sums = lax.fori_loop(0, rows // LONG, finish, (zero, zero, zero))
        sums_ref[...] = jnp.concatenate(
            [jnp.sum(v, axis=0, keepdims=True) for v in sums] + [jnp.zeros((5, width), FULL)],
            axis=0,
        )

    vmem = pl.BlockSpec(memory_space=pltpu.VMEM)
    return pl.pallas_call(
        body,
        in_specs=[vmem] * 8,
        out_specs=[vmem] * 5,
        out_shape=[
            jax.ShapeDtypeStruct((rows, inner), LOW),
            jax.ShapeDtypeStruct((1, inner), FULL),
            jax.ShapeDtypeStruct((rows, width), FULL),
            jax.ShapeDtypeStruct((rows, width), LOW),
            jax.ShapeDtypeStruct((8, width), FULL),
        ],
        scratch_shapes=[pltpu.VMEM((rows, width), FULL)],
        compiler_params=kernel_params(),
        cost_estimate=cost(8.6),
    )(shrink_low, second_grad, slope, centred, inverse, widen_weight, narrow_weight, vectors)


def attend_back(attn_low, packed, probs, output_weight):
    pair, _, length, _ = probs.shape
    width = attn_low.shape[1]
    rows = attn_low.shape[0]
    scale = 1.0 / math.sqrt(HEAD)
    duo = 2 * HEAD

    def body(attn_ref, packed_ref, probs_ref, wout_ref, right_ref, sums_ref, context_ref):
        for s in range(pair):
            here = slice(s * length, (s + 1) * length)
            context_ref[...] = times_turned(attn_ref[here, :], wout_ref[...]).astype(LOW)
            masks = head_masks(1.0)
            lane = lax.broadcasted_iota(jnp.int32, (length, duo), 1)
            for j in range(width // duo):
                query = packed_ref[here, j * duo : (j + 1) * duo]
                key = packed_ref[here, width + j * duo : width + (j + 1) * duo]
                value = packed_ref[here, 2 * width + j * duo : 2 * width + (j + 1) * duo]
                upstream = context_ref[:, j * duo : (j + 1) * duo]
                parts = []
                for head in range(2):
                    low = probs_ref[s, 2 * j + head]
                    probs_full = low.astype(FULL)
                    slope = times_turned(upstream * masks[head], value)
                    dot = jnp.sum(probs_full * slope, axis=-1, keepdims=True)
                    score = (probs_full * (slope - dot)).astype(LOW)
                    parts.append(
                        (times(score, key), turned_times(score, query), turned_times(low, upstream))
                    )
                first, second = parts
                query_grad = jnp.where(lane < HEAD, first[0], second[0]) * scale
                key_grad = jnp.where(lane < HEAD, first[1], second[1]) * scale
                value_grad = jnp.where(lane < HEAD, first[2], second[2])
                right_ref[here, j * duo : (j + 1) * duo] = query_grad.astype(LOW)
                right_ref[here, width + j * duo : width + (j + 1) * duo] = key_grad.astype(LOW)
                right_ref[here, 2 * width + j * duo : 2 * width + (j + 1) * duo] = value_grad.astype(LOW)
                sums_ref[s, 0:1, j * duo : (j + 1) * duo] = jnp.sum(query_grad, axis=0, keepdims=True)
                sums_ref[s, 1:2, j * duo : (j + 1) * duo] = jnp.sum(value_grad, axis=0, keepdims=True)
            right_ref[here, 3 * width :] = attn_ref[here, :]

    vmem = pl.BlockSpec(memory_space=pltpu.VMEM)
    return pl.pallas_call(
        body,
        in_specs=[vmem] * 4,
        out_specs=[vmem] * 2,
        out_shape=[
            jax.ShapeDtypeStruct((rows, 4 * width), LOW),
            jax.ShapeDtypeStruct((pair, 2, width), FULL),
        ],
        scratch_shapes=[pltpu.VMEM((length, width), LOW)],
        compiler_params=kernel_params(),
        cost_estimate=cost(10),
    )(attn_low, packed, probs, output_weight)


def hidden_back(right, first_grad, mixing_weight, pair):
    rows, width = first_grad.shape
    length = rows // pair
    near = length // 2

    def body(right_ref, grad_ref, mix_ref, own_ref, away_ref, total_ref):
        for s in range(pair):
            here = slice(s * length, (s + 1) * length)
            hidden = grad_ref[here, :] + times_turned(right_ref[here, : 3 * width], mix_ref[...])
            low = hidden.astype(LOW)
            own_ref[s] = low[:near]
            away_ref[s] = low[near:]
            total_ref[s] = jnp.sum(hidden, axis=0, keepdims=True)

    vmem = pl.BlockSpec(memory_space=pltpu.VMEM)
    return pl.pallas_call(
        body,
        in_specs=[vmem] * 3,
        out_specs=[vmem] * 3,
        out_shape=[
            jax.ShapeDtypeStruct((pair, near, width), LOW),
            jax.ShapeDtypeStruct((pair, near, width), LOW),
            jax.ShapeDtypeStruct((pair, 1, width), FULL),
        ],
        compiler_params=kernel_params(),
        cost_estimate=cost(2.5),
    )(right, first_grad, mixing_weight)


(
    S_SEND, FEED_BACK, S_KEEP, E_SEND, E_KEEP, ATTEND_BACK, M_SEND, HIDDEN_BACK, M_KEEP, OUT_GOT,
    GRAD_GOT, OUT_JOIN, GRAD_JOIN, M_NEAR, UNPACK, S_WIDEN, E_WIDEN, S, E, M,
) = range(20)


def pair_shards(
    tokens,
    timesteps,
    boundary,
    importance,
    cotangent,
    time_weight,
    time_bias,
    mixing_weight,
    query_bias,
    value_bias,
    output_weight,
    output_bias,
    first_gain,
    first_shift,
    widen_weight,
    widen_bias,
    narrow_weight,
    narrow_bias,
    second_gain,
    second_shift,
):
    near, group, width = tokens.shape
    pair = group // 2
    side = lax.axis_index("blk")
    info = device_info()

    away, own = split_rows(tokens, info)
    got = swap(away, "x")
    away_cot, own_cot = split_rows(cotangent, info)
    got_cot = swap(away_cot, "x")
    vectors = jnp.stack(
        [
            query_bias,
            value_bias,
            output_bias,
            first_gain,
            first_shift,
            narrow_bias,
            second_gain,
            second_shift,
        ]
    ).astype(FULL)
    time_code = sinusoid(
        lax.dynamic_slice_in_dim(timesteps, side * pair, pair, 0), time_weight.shape[0]
    ).astype(LOW)
    embed = jnp.dot(time_code, time_weight, preferred_element_type=FULL) + time_bias.astype(FULL)

    vectors = lay_out(
        vectors, (mixing_weight, output_weight, widen_weight, narrow_weight), away_cot
    )
    left, packed, probs, centred, inverse, norm_low = attend(
        own, got, embed[:, None], mixing_weight, output_weight, vectors
    )
    (act_low, slope, out_own, out_away, second_grad, shrink_low, sums_two) = feed(
        norm_low,
        centred,
        widen_weight,
        widen_bias.astype(FULL)[None],
        narrow_weight,
        vectors,
        own_cot,
        got_cot,
        info,
        boundary,
        importance,
    )
    expand_tall, mixing_tall = len(EXPAND_ORDERS), len(MIXING_ORDERS)
    shrink_of = (SHRINK_ORDERS, lambda t: t, lambda t: 0)
    expand_of = (EXPAND_ORDERS, lambda t: t % expand_tall, lambda t: t // expand_tall)
    mixing_of = (
        MIXING_ORDERS,
        lambda t: t % mixing_tall + mixing_tall * (t // (3 * mixing_tall)),
        lambda t: t // mixing_tall,
    )

    def send_half(left, right, of):
        return weight_half(left, right, info, *of)

    def keep_half(left, right, got, of):
        found = weight_half(left, right, info, *of, got=got)
        return found[:-1], found[-1]

    line = Order()
    v = SimpleNamespace()
    done = {}

    def event(name):
        if name == S_SEND:
            v.s_away = line.run(partial(send_half, of=shrink_of), act_low, shrink_low)
            v.s_got = swap(v.s_away, "c")
            v.out_got = swap(out_away, "x")
        elif name == FEED_BACK:
            v.pre_low, v.expand_bias, v.first_grad, v.attn_low, v.sums_one = line.run(
                    feed_back, shrink_low, second_grad, slope, centred, inverse, widen_weight,
                    narrow_weight, vectors, token=4
                )
        elif name == S_KEEP:
            found = line.run(
                partial(keep_half, of=shrink_of), act_low, shrink_low, v.s_got, token=1
            )
            line.begin(S, flow(SHRINK_ORDERS, *found))
        elif name == E_SEND:
            v.e_away = line.run(partial(send_half, of=expand_of), norm_low, v.pre_low)
            v.e_got = swap(v.e_away, "c")
        elif name == E_KEEP:
            found = line.run(
                partial(keep_half, of=expand_of), norm_low, v.pre_low, v.e_got, token=1
            )
            line.begin(E, flow(EXPAND_ORDERS, *found[:-1], found[-1], lambda: v.rider))
        elif name == ATTEND_BACK:
            v.right, v.sums_zero = line.run(attend_back, v.attn_low, packed, probs, output_weight, token=1)
        elif name == M_SEND:
            v.m_away = line.run(partial(send_half, of=mixing_of), left, v.right)
            v.m_got = swap(v.m_away, "c")
        elif name == HIDDEN_BACK:
            v.grad_own, v.grad_away, v.time_total = line.run(
                    partial(hidden_back, pair=pair), v.right, v.first_grad, mixing_weight,
                    token=2
                )
            v.grad_got = swap(v.grad_away, "x")
            v.rider = Rider(
                line.run(
                    pack_small, v.sums_zero, v.sums_one, sums_two, v.expand_bias,
                    v.time_total, time_code
                )
            )
        elif name == M_KEEP:
            found = line.run(
                partial(keep_half, of=mixing_of), left, v.right, v.m_got, token=1
            )
            line.begin(M, flow(MIXING_ORDERS, *found))
        elif name == OUT_GOT:
            (v.out_got,) = line.after(v.out_got)
            line.token = v.out_got
        elif name == GRAD_GOT:
            (v.grad_got,) = line.after(v.grad_got)
            line.token = v.grad_got
        elif name == OUT_JOIN:
            v.output = line.run(partial(join_rows, info=info), out_own, v.out_got)
        elif name == GRAD_JOIN:
            v.input_grad = line.run(partial(join_rows, info=info), v.grad_own, v.grad_got)
        elif name == M_NEAR:
            v.mixed = line.run(
                lambda near: widen_half(near, info, MIXING_ORDERS, True), line.sent[M]
            )
        elif name == UNPACK:
            sums, weight, bias = line.run(
                partial(unpack_small, pair=pair, code_width=time_code.shape[1]), v.rider.packed
            )
            vectors_out = [sums[k] for k in range(8)] + [sums[8:12].reshape(-1), bias[0]]
            v.small = lax.optimization_barrier((weight,) + tuple(vectors_out))
            line.token = v.small[1]
        elif name == S_WIDEN:
            v.shrink = line.run(
                lambda near, far: widen_out(near, far, info, SHRINK_ORDERS, 0, 4 * len(SHRINK_ORDERS), 1),
                *done[S]
            )
        elif name == E_WIDEN:
            v.expand = line.run(
                lambda near, far: widen_out(near, far, info, EXPAND_ORDERS, 0, 4 * expand_tall, 4),
                *done[E]
            )
        else:
            done[name] = line.advance(name)

    for name in SEQUENCE:
        event(name)
    time_weight_grad, *sums, time_bias_grad = v.small
    mixing_grad, output_grad = widen_half(
        done[M][1], info, MIXING_ORDERS, False, v.mixed
    )
    return (
        v.output,
        v.input_grad,
        time_weight_grad,
        time_bias_grad,
        mixing_grad,
        sums[0],
        sums[1],
        output_grad,
        sums[2],
        sums[3],
        sums[4],
        v.expand,
        sums[8],
        v.shrink,
        sums[5],
        sums[6],
        sums[7],
    )


SEQUENCE = (
    S_SEND, FEED_BACK, S_KEEP, OUT_GOT, ATTEND_BACK, E_SEND, S, M_SEND, E_KEEP, HIDDEN_BACK,
    M_KEEP, S, E, S, M, S, E, S, M, E, GRAD_GOT, S, M, E, E, M, M, E, S, OUT_JOIN, GRAD_JOIN, S,
    S_WIDEN, M, E, E, E_WIDEN, UNPACK, M, M_NEAR, M,
)


def solution(mesh):
    pairs = mesh.shape["blk"] == 2 and mesh.shape["dp"] == 16
    return jax.shard_map(
        pair_shards if pairs else general_shards,
        mesh=mesh,
        in_specs=(
            P("blk", "dp", None),
            P("dp"),
            P("dp"),
            P("dp"),
            P("blk", "dp", None),
            P(),
            P(),
            P(),
            P(),
            P(),
            P(),
            P(),
            P(),
            P(),
            P(),
            P(),
            P(),
            P(),
            P(),
            P(),
        ),
        out_specs=(
            P("blk", "dp", None),
            P("blk", "dp", None),
            P(),
            P(),
            P(),
            P(),
            P(),
            P(),
            P(),
            P(),
            P(),
            P(),
            P(),
            P(),
            P(),
            P(),
            P(),
        ),
        check_vma=False,
    )
```
